32 devices in a mesh: fsdp: 8 (over y, x, core), dp: 4 (over z).
Axes of the slice: x: 2, y: 2, z: 4, core: 2. Of those that a mesh axis runs over, the one named last changes fastest.
Arguments:
- enc_input: bfloat16 [32768, 1024], P(('fsdp', 'dp')), may hold values from -6 to 6
- dec_input: bfloat16 [8192, 1024], P(('fsdp', 'dp')), may hold values from -6 to 6
- enc_cot: bfloat16 [32768, 1024], P(('fsdp', 'dp')), may hold values from -6 to 6
- dec_cot: bfloat16 [8192, 1024], P(('fsdp', 'dp')), may hold values from -6 to 6
- enc_qkv: bfloat16 [1024, 3072], P('fsdp'), may hold values from -0.1875 to 0.1875
- enc_attn_out: bfloat16 [1024, 1024], P('fsdp'), may hold values from -0.75 to 0.75
- enc_ffn_in: bfloat16 [1024, 4096], P('fsdp'), may hold values from -0.1875 to 0.1875
- enc_ffn_out: bfloat16 [4096, 1024], P('fsdp'), may hold values from -0.09375 to 0.09375
- dec_self_qkv: bfloat16 [1024, 3072], P('fsdp'), may hold values from -0.1875 to 0.1875
- dec_self_out: bfloat16 [1024, 1024], P('fsdp'), may hold values from -0.75 to 0.75
- dec_cross_q: bfloat16 [1024, 1024], P('fsdp'), may hold values from -0.1875 to 0.1875
- dec_cross_kv: bfloat16 [1024, 2048], P('fsdp'), may hold values from -0.1875 to 0.1875
- dec_cross_out: bfloat16 [1024, 1024], P('fsdp'), may hold values from -0.75 to 0.75
- dec_ffn_in: bfloat16 [1024, 4096], P('fsdp'), may hold values from -0.1875 to 0.1875
- dec_ffn_out: bfloat16 [4096, 1024], P('fsdp'), may hold values from -0.09375 to 0.09375
- norm_gains: float32 [5, 1024], replicated, may hold values from 0.25 to 1.75
- enc_down: float32 [1024, 512], replicated, may hold values from -0.1875 to 0.1875
- enc_up: float32 [512, 1024], replicated, may hold values from -0.0625 to 0.0625
- dec_down: float32 [1024, 512], replicated, may hold values from -0.1875 to 0.1875
- dec_up: float32 [512, 1024], replicated, may hold values from -0.0625 to 0.0625
- enc_lengths: int32 [32], P(('fsdp', 'dp')), may hold values from 256 to 1024, as said below
- dec_lengths: int32 [32], P(('fsdp', 'dp')), may hold values from 64 to 256, as said below
Outputs:
- enc_out: bfloat16 [32768, 1024], P(('fsdp', 'dp'))
- dec_out: bfloat16 [8192, 1024], P(('fsdp', 'dp'))
- enc_input_grad: float32 [32768, 1024], P(('fsdp', 'dp'))
- dec_input_grad: float32 [8192, 1024], P(('fsdp', 'dp'))
- enc_down_grad: float32 [1024, 512], replicated
- enc_up_grad: float32 [512, 1024], replicated
- dec_down_grad: float32 [1024, 512], replicated
- dec_up_grad: float32 [512, 1024], replicated
- rms: float32 [7], replicated
The draws below stay inside these ranges and needn't reach their ends.
Inputs may be any that keep to these rules, and one draw needn't show every extreme that they name: `enc_lengths`: one sequence of every draw has all 1024 encoder positions valid. `dec_lengths`: one sequence of every draw has all 256 decoder positions valid.
All inputs are finite; a program needn't handle non-finite values.
Results may differ from the reference program's by a relative error of at most 0.015.
Values may be sent and summed in bfloat16 or wider, within the bound.
A program may use at most 320 MiB of HBM per device.

```python
import math
import jax
import jax.numpy as jnp
from jax import lax

D = 1024
FF = 4096
HEADS = 16
HEAD = 64
A = 512
ENC_LEN = 1024
DEC_LEN = 256
SEQS = 32


def ragged_lengths(key, longest):
    first_key, second_key = jax.random.split(key)
    drawn = jax.random.randint(first_key, (SEQS,), longest // 4, longest + 1)
    chosen = jax.random.randint(second_key, (), 0, SEQS)
    return jnp.where(jnp.arange(SEQS) == chosen, longest, drawn).astype(jnp.int32)


def draw_enc_lengths(key, part):
    key = jax.random.fold_in(key, 11)
    return ragged_lengths(key, ENC_LEN)


def draw_dec_lengths(key, part):
    key = jax.random.fold_in(key, 12)
    return ragged_lengths(key, DEC_LEN)


def block_scale(rng, shape, cuts, least, top_value):
    def one(axis_at, blocks):
        heights = jax.random.uniform(jax.random.fold_in(jax.random.fold_in(rng, 6), axis_at), (blocks,), jnp.float32, least / len(cuts), top_value / len(cuts))
        return jnp.repeat(jnp.exp(heights), shape[axis_at] // blocks).reshape((-1,) + (1,) * (len(shape) - axis_at - 1))

    factor_of = one(*cuts[0])
    for cut in cuts[1:]:
        factor_of = factor_of * one(*cut)
    return factor_of


def scatter_about(rng, shape, scale, bound, shards=(), kind=jnp.bfloat16):
    level = block_scale(rng, shape, shards, -0.22, 0.18) if shards else 1.0
    array = jax.random.normal(rng, shape, jnp.float32) * scale * level
    return jnp.minimum(jnp.maximum(array, -bound), bound).astype(kind)


def setup_inputs(seed: int = 0) -> dict:
    key_of = jax.random.split(jax.random.key(seed), 23)
    return {
        "enc_input": scatter_about(key_of[0], (SEQS * ENC_LEN, D), 1.0, 6.0, ((0, 32),)),
        "dec_input": scatter_about(key_of[1], (SEQS * DEC_LEN, D), 1.0, 6.0, ((0, 32),)),
        "enc_cot": scatter_about(key_of[2], (SEQS * ENC_LEN, D), 1.0, 6.0, ((0, 32),)),
        "dec_cot": scatter_about(key_of[3], (SEQS * DEC_LEN, D), 1.0, 6.0, ((0, 32),)),
        "enc_qkv": scatter_about(key_of[4], (D, 3 * D), D ** -0.5, 0.1875, ((0, 8),)),
        "enc_attn_out": scatter_about(key_of[5], (D, D), (D // 16) ** -0.5, 0.75, ((0, 8),)),
        "enc_ffn_in": scatter_about(key_of[6], (D, FF), D ** -0.5, 0.1875, ((0, 8),)),
        "enc_ffn_out": scatter_about(key_of[7], (FF, D), FF ** -0.5, 0.09375, ((0, 8),)),
        "dec_self_qkv": scatter_about(key_of[8], (D, 3 * D), D ** -0.5, 0.1875, ((0, 8),)),
        "dec_self_out": scatter_about(key_of[9], (D, D), (D // 16) ** -0.5, 0.75, ((0, 8),)),
        "dec_cross_q": scatter_about(key_of[10], (D, D), D ** -0.5, 0.1875, ((0, 8),)),
        "dec_cross_kv": scatter_about(key_of[11], (D, 2 * D), D ** -0.5, 0.1875, ((0, 8),)),
        "dec_cross_out": scatter_about(key_of[12], (D, D), (D // 16) ** -0.5, 0.75, ((0, 8),)),
        "dec_ffn_in": scatter_about(key_of[13], (D, FF), D ** -0.5, 0.1875, ((0, 8),)),
        "dec_ffn_out": scatter_about(key_of[14], (FF, D), FF ** -0.5, 0.09375, ((0, 8),)),
        "norm_gains": jnp.clip(1.0 + 0.15 * jax.random.normal(key_of[15], (5, D), jnp.float32), 0.25, 1.75),
        "enc_down": scatter_about(key_of[16], (D, A), D ** -0.5, 0.1875, (), jnp.float32),
        "enc_up": scatter_about(key_of[17], (A, D), (16 * A) ** -0.5, 0.0625, (), jnp.float32),
        "dec_down": scatter_about(key_of[18], (D, A), D ** -0.5, 0.1875, (), jnp.float32),
        "dec_up": scatter_about(key_of[19], (A, D), (16 * A) ** -0.5, 0.0625, (), jnp.float32),
        "enc_lengths": draw_enc_lengths(jax.random.fold_in(key_of[22], 71), 0),
        "dec_lengths": draw_dec_lengths(jax.random.fold_in(key_of[22], 71), 0),
    }


@jax.custom_vjp
def low(v):
    return lax.optimization_barrier(v.astype(jnp.bfloat16)).astype(jnp.float32)

@jax.custom_vjp
def low_back(v):
    return v

def low_keep(v):
    return (low(v), None)

def low_pass(kept, grad):
    return (grad,)

def back_keep(v):
    return (v, None)

def back_low(kept, grad):
    return (low(grad),)
low.defvjp(low_keep, low_pass)
low_back.defvjp(back_keep, back_low)

def both_round(entries):
    return low(low_back(entries))

def matmul(former, latter):
    return jnp.dot(former, latter, precision=lax.Precision.HIGHEST, preferred_element_type=jnp.float32)

def gelu_exact(entries):
    return 0.5 * entries * (1.0 + lax.erf(entries * (1.0 / math.sqrt(2.0))))

def silu_smooth(entries):
    return entries * jax.nn.sigmoid(entries)

def layer_norm(entries, gain_row):
    centered = entries - lax.optimization_barrier(jnp.mean(entries, axis=-1, keepdims=True))
    spread = lax.optimization_barrier(jnp.mean(centered * centered, axis=-1, keepdims=True))
    return centered * lax.rsqrt(spread + 1e-05) * gain_row

def attention(queries, key_rows, value_rows, allowed):
    query_heads = queries.reshape(queries.shape[0], HEADS, HEAD)
    key_heads = key_rows.reshape(key_rows.shape[0], HEADS, HEAD)
    value_heads = value_rows.reshape(value_rows.shape[0], HEADS, HEAD)
    scores = jnp.einsum('qhd,khd->hqk', query_heads, key_heads, precision=lax.Precision.HIGHEST) / math.sqrt(HEAD)
    scores = low_back(scores)
    scores = jnp.where(allowed[None], scores, -1000000000.0)
    highest = lax.optimization_barrier(jnp.max(scores, axis=-1, keepdims=True))
    weights = jnp.exp(scores - highest)
    probs = low(weights / lax.optimization_barrier(jnp.sum(weights, axis=-1, keepdims=True)))
    mixture = jnp.einsum('hqk,khd->qhd', probs, value_heads, precision=lax.Precision.HIGHEST)
    return mixture.reshape(queries.shape[0], D)

def ffn_adapter(hidden, w_in, w_back, down_low, up_low):
    hidden_low = low(hidden)
    pre_ffn = low_back(matmul(hidden_low, w_in))
    act_ffn = low(gelu_exact(pre_ffn))
    ffn_result = low_back(matmul(act_ffn, w_back))
    pre_adapter = low_back(matmul(hidden_low, down_low))
    act_adapter = low(silu_smooth(pre_adapter))
    adapted = low_back(matmul(act_adapter, up_low))
    return ffn_result + 4.0 * adapted

def masked_square(entries, row_mask):
    return jnp.sum(lax.optimization_barrier(jnp.sum(entries * entries, axis=1)) * row_mask)

def encoder_layer(enc_rows, weights, gains, down_low, up_low, key_limit):
    w_qkv, w_out, w_in, w_back = weights
    positions = jnp.arange(ENC_LEN, dtype=jnp.int32)
    qkv = both_round(matmul(enc_rows, w_qkv))
    queries, key_rows, value_rows = jnp.split(qkv, 3, axis=1)
    allowed = jnp.broadcast_to(positions[None, :] < key_limit, (ENC_LEN, ENC_LEN))
    mixture = both_round(attention(queries, key_rows, value_rows, allowed))
    attended = low_back(matmul(mixture, w_out))
    hidden = layer_norm(enc_rows + attended, gains[0])
    branch = ffn_adapter(hidden, w_in, w_back, down_low, up_low)
    output = layer_norm(hidden + branch, gains[1])
    row_mask = (positions < key_limit).astype(jnp.float32)
    squares = jnp.stack([masked_square(attended, row_mask), masked_square(branch, row_mask), masked_square(output, row_mask)])
    return (output, squares)

def decoder_layer(dec_rows, enc_low, weights, gains, down_low, up_low, enc_limit, dec_limit):
    w_sqkv, w_so, w_cq, w_ckv, w_co, w_in, w_back = weights
    dec_positions = jnp.arange(DEC_LEN, dtype=jnp.int32)
    enc_positions = jnp.arange(ENC_LEN, dtype=jnp.int32)
    qkv = both_round(matmul(dec_rows, w_sqkv))
    queries, key_rows, value_rows = jnp.split(qkv, 3, axis=1)
    self_allowed = (dec_positions[None, :] <= dec_positions[:, None]) & (dec_positions[None, :] < dec_limit)
    mixture = both_round(attention(queries, key_rows, value_rows, self_allowed))
    attended = low_back(matmul(mixture, w_so))
    hidden = layer_norm(dec_rows + attended, gains[2])
    hidden_low = low(hidden)
    cross_q = both_round(matmul(hidden_low, w_cq))
    cross_kv = both_round(matmul(enc_low, w_ckv))
    cross_k, cross_v = jnp.split(cross_kv, 2, axis=1)
    cross_allowed = jnp.broadcast_to(enc_positions[None, :] < enc_limit, (DEC_LEN, ENC_LEN))
    cross_mix = both_round(attention(cross_q, cross_k, cross_v, cross_allowed))
    crossed = low_back(matmul(cross_mix, w_co))
    hidden_c = layer_norm(hidden + crossed, gains[3])
    branch = ffn_adapter(hidden_c, w_in, w_back, down_low, up_low)
    output = layer_norm(hidden_c + branch, gains[4])
    row_mask = (dec_positions < dec_limit).astype(jnp.float32)
    squares = jnp.stack([masked_square(attended, row_mask), masked_square(crossed, row_mask), masked_square(branch, row_mask), masked_square(output, row_mask)])
    return (output, squares)

def reference(enc_input, dec_input, enc_cot, dec_cot, enc_qkv, enc_attn_out, enc_ffn_in, enc_ffn_out, dec_self_qkv, dec_self_out, dec_cross_q, dec_cross_kv, dec_cross_out, dec_ffn_in, dec_ffn_out, norm_gains, enc_down, enc_up, dec_down, dec_up, enc_lengths, dec_lengths):
    enc_weights = tuple((matrix.astype(jnp.float32) for matrix in (enc_qkv, enc_attn_out, enc_ffn_in, enc_ffn_out)))
    dec_weights = tuple((matrix.astype(jnp.float32) for matrix in (dec_self_qkv, dec_self_out, dec_cross_q, dec_cross_kv, dec_cross_out, dec_ffn_in, dec_ffn_out)))
    enc_seqs = enc_input.astype(jnp.float32).reshape(SEQS, ENC_LEN, D)
    dec_seqs = dec_input.astype(jnp.float32).reshape(SEQS, DEC_LEN, D)

    def forward(enc_all, dec_all, e_down, e_up, d_down, d_up):
        e_down_low = low(e_down)
        e_up_low = low(e_up)
        d_down_low = low(d_down)
        d_up_low = low(d_up)

        def one_sequence(totals, packed):
            enc_rows, dec_rows, enc_limit, dec_limit = packed
            enc_result, enc_squares = encoder_layer(enc_rows, enc_weights, norm_gains, e_down_low, e_up_low, enc_limit)
            enc_low = low(enc_result)
            dec_result, dec_squares = decoder_layer(dec_rows, enc_low, dec_weights, norm_gains, d_down_low, d_up_low, enc_limit, dec_limit)
            return (totals + jnp.concatenate([enc_squares, dec_squares]), (enc_low, dec_result))
        totals, results = lax.scan(jax.checkpoint(one_sequence), jnp.zeros((7,), jnp.float32), (enc_all, dec_all, enc_lengths, dec_lengths))
        return (results, totals)
    results, backward, totals = jax.vjp(forward, enc_seqs, dec_seqs, enc_down, enc_up, dec_down, dec_up, has_aux=True)
    enc_result, dec_result = results
    cotangents = (enc_cot.astype(jnp.float32).reshape(SEQS, ENC_LEN, D), dec_cot.astype(jnp.float32).reshape(SEQS, DEC_LEN, D))
    grad_enc, grad_dec, grad_e_down, grad_e_up, grad_d_down, grad_d_up = backward(cotangents)
    enc_count = jnp.sum(enc_lengths).astype(jnp.float32)
    dec_count = jnp.sum(dec_lengths).astype(jnp.float32)
    counts = jnp.concatenate([jnp.broadcast_to(enc_count, (3,)), jnp.broadcast_to(dec_count, (4,))])
    rms = jnp.sqrt(totals / (counts * D))
    return (enc_result.reshape(SEQS * ENC_LEN, D).astype(jnp.bfloat16), dec_result.reshape(SEQS * DEC_LEN, D).astype(jnp.bfloat16), grad_enc.reshape(SEQS * ENC_LEN, D), grad_dec.reshape(SEQS * DEC_LEN, D), grad_e_down, grad_e_up, grad_d_down, grad_d_up, rms)
```

```python
import functools
import math

import jax
import jax.numpy as jnp
from jax import lax
from jax.experimental import pallas as pl
from jax.experimental.pallas import tpu as pltpu
from jax.sharding import PartitionSpec as P

HEAD = 64
PAIR = 2 * HEAD
EPSILON = 1e-05
F32 = jnp.float32
BF16 = jnp.bfloat16
VMEM_BYTES = 58 * 2**20


def nn(former, latter):
    return jnp.dot(former, latter, preferred_element_type=F32)


def nt(former, latter):
    return lax.dot_general(
        former, latter, (((1,), (1,)), ((), ())), preferred_element_type=F32
    )


def tn(former, latter):
    return lax.dot_general(
        former, latter, (((0,), (0,)), ((), ())), preferred_element_type=F32
    )


def standardize(entries):
    centered = entries - jnp.mean(entries, axis=-1, keepdims=True)
    spread = jnp.mean(centered * centered, axis=-1, keepdims=True)
    inverse = lax.rsqrt(spread + EPSILON)
    return centered * inverse, inverse


def standardize_grad(unit, inverse, scaled):
    return inverse * (
        scaled
        - jnp.mean(scaled, axis=-1, keepdims=True)
        - unit * jnp.mean(scaled * unit, axis=-1, keepdims=True)
    )


class Fetch:
    def __init__(self, source, whole, sems, chunks):
        self.source, self.whole, self.sems, self.chunks = source, whole, sems, chunks

    def copy(self, chunk):
        width = self.whole.shape[1] // self.chunks
        columns = pl.ds(chunk * width, width)
        return pltpu.make_async_copy(
            self.source.at[:, columns], self.whole.at[:, columns], self.sems.at[chunk]
        )

    def start(self):
        for chunk in range(self.chunks):
            self.copy(chunk).start()

    def wait(self, chunk):
        @pl.when(pl.program_id(0) == 0)
        def _():
            self.copy(chunk).wait()

    def wait_all(self):
        for chunk in range(self.chunks):
            self.wait(chunk)


UNIT_US = 5.8
LEAD_US = 4.0


class Gather:
    def __init__(self, owns, wholes, splits, sends, recvs, locals_):
        self.owns, self.wholes, self.splits = owns, wholes, splits
        self.sends, self.recvs, self.locals = sends, recvs, locals_
        self.units = [(m, part) for m, split in enumerate(splits) for part in range(split)]
        f, z = lax.axis_index("fsdp"), lax.axis_index("dp")
        odd = z % 2
        y, x, core = f // 4, (f // 2) % 2, f % 2
        beside, above = f + 2 - 4 * x, f + 4 - 8 * y
        self.own = f
        self.direct = beside + odd * (above - beside)
        self.onward = above + odd * (beside - above)
        self.far = beside + 4 - 8 * y
        self.twin = f + 1 - 2 * core
        self.partner = z + 1 - 2 * odd

    def meet(self):
        barrier = pltpu.get_barrier_semaphore()
        mesh = pl.DeviceIdType.MESH
        for to in ({"fsdp": self.direct}, {"fsdp": self.onward}, {"fsdp": self.twin}, {"dp": self.partner}):
            pl.semaphore_signal(barrier, inc=1, device_id=to, device_id_type=mesh)
        pl.semaphore_wait(barrier, 4)

    def transfer(self, unit, kind):
        m, part = self.units[unit]
        whole, own = self.wholes[m], self.owns[m]
        block = own.shape[0]
        rows = block // self.splits[m]
        owner = (self.own, self.direct, self.direct, self.own, self.direct, self.far, self.onward)[kind]
        there = whole.at[pl.ds(pl.multiple_of(owner * block + part * rows, 16), rows), :]
        here = own.at[pl.ds(part * rows, rows), :] if kind in (0, 3) else there
        to = {"fsdp": (self.direct, self.onward, None, self.twin, self.twin, self.twin, self.twin)[kind]}
        if kind == 2:
            to = {"dp": self.partner}
        return pltpu.make_async_remote_copy(
            src_ref=here,
            dst_ref=there,
            send_sem=self.sends.at[unit, kind],
            recv_sem=self.recvs.at[unit, kind],
            device_id=to,
            device_id_type=pl.DeviceIdType.MESH,
        )

    def keep(self, m):
        block = self.owns[m].shape[0]
        rows = pl.ds(pl.multiple_of(self.own * block, 16), block)
        return pltpu.make_async_copy(self.owns[m], self.wholes[m].at[rows, :], self.locals.at[m])

    def begin(self):
        self.meet()
        for unit in range(len(self.units)):
            self.transfer(unit, 0).start()
        for unit in range(len(self.units)):
            self.transfer(unit, 3).start()
        for m in range(len(self.owns)):
            self.keep(m).start()

    def pass_on(self, unit):
        self.transfer(unit, 0).wait_recv()
        for kind in (1, 2, 4):
            self.transfer(unit, kind).start()

    def share(self, unit):
        self.transfer(unit, 1).wait_recv()
        self.transfer(unit, 5).start()
        self.transfer(unit, 2).wait_recv()
        self.transfer(unit, 6).start()

    def arrived(self, unit):
        for kind in (3, 4, 5, 6):
            self.transfer(unit, kind).wait_recv()

    def first(self, count):
        for unit in range(count):
            self.pass_on(unit)
            if unit:
                self.share(unit - 1)
        self.share(count - 1)
        for unit in range(count):
            self.arrived(unit)
        self.keep(0).wait()

    def plan(self, skip, slots, steps, pace, lead):
        acts = {}
        for unit in range(skip, len(self.units)):
            due = lead + LEAD_US + UNIT_US * (unit - skip + 1)
            for act, at in ((self.pass_on, due), (self.share, due + UNIT_US + 2.0)):
                tick = min(math.ceil(at / pace), steps * slots - 1)
                acts.setdefault((tick // slots, tick % slots), []).append((act, unit))
        return acts

    def poll(self, acts, slot):
        for (step, at), todo in acts.items():
            if at == slot:

                @pl.when(pl.program_id(0) == step)
                def _(todo=todo):
                    for act, unit in todo:
                        act(unit)

    def finish(self, skip):
        for unit in range(len(self.units)):
            if unit >= skip:
                self.arrived(unit)
            for kind in range(7):
                self.transfer(unit, kind).wait_send()
        for m in range(len(self.owns)):
            if not (m == 0 and skip):
                self.keep(m).wait()


class Hosted:
    def __init__(self, owns, skip_first=False, fsdp=8):
        self.owns = list(owns)
        self.fsdp = fsdp
        self.splits = [max(1, a.size // 131072) for a in self.owns]
        self.splits = [4 if a.shape == (128, 3072) else n for a, n in zip(self.owns, self.splits)]
        self.skip = self.splits[0] if skip_first else 0

    def out_shapes(self):
        return [
            jax.ShapeDtypeStruct((a.shape[0] * self.fsdp, a.shape[1]), a.dtype) for a in self.owns
        ]

    def scratch(self):
        units = sum(self.splits)
        return [
            pltpu.SemaphoreType.DMA((units, 7)),
            pltpu.SemaphoreType.DMA((units, 7)),
            pltpu.SemaphoreType.DMA((len(self.owns),)),
        ]

    def run(self, own_refs, whole_refs, scratch):
        return Gather(own_refs, whole_refs, self.splits, *scratch)


ANY = pl.BlockSpec(memory_space=pl.ANY)
SCALAR = pl.BlockSpec(memory_space=pltpu.SMEM)


def rows_spec(rows, width):
    return pl.BlockSpec((rows, width), lambda i: (i, 0))


def whole_spec(shape):
    return pl.BlockSpec(shape, lambda i: (0,) * len(shape))


def hosted_call(body, name, grid, ins, outs, scratch, flops, moved, hosted=None, collective=None):
    count = len(hosted.owns) if hosted else 0

    def kernel(*refs):
        refs = list(refs)

        def take(n):
            taken = refs[:n]
            del refs[:n]
            return taken

        own_refs, in_refs, whole_refs, out_refs = take(count), take(len(ins)), take(count), take(len(outs))
        gather = None
        if hosted:
            gather = hosted.run(own_refs, whole_refs, refs[-3:])
            refs = refs[:-3]

            @pl.when(pl.program_id(0) == 0)
            def _():
                gather.begin()

        body(in_refs, out_refs, refs, gather)
        if hosted:

            @pl.when(pl.program_id(0) == grid[0] - 1)
            def _():
                gather.finish(hosted.skip)

    out = pl.pallas_call(
        kernel,
        grid=grid,
        in_specs=[ANY] * count + [s for _, s in ins],
        out_specs=[ANY] * count + [s for _, _, s in outs],
        scratch_shapes=[*scratch, *(hosted.scratch() if hosted else [])],
        out_shape=(hosted.out_shapes() if hosted else [])
        + [jax.ShapeDtypeStruct(s, d) for s, d, _ in outs],
        compiler_params=pltpu.CompilerParams(
            vmem_limit_bytes=VMEM_BYTES,
            **({"collective_id": collective, "has_side_effects": True} if hosted else {}),
        ),
        cost_estimate=pl.CostEstimate(flops=flops, bytes_accessed=moved, transcendentals=0),
        name=name,
    )(*(hosted.owns if hosted else []), *[a for a, _ in ins])
    return list(out[count:]), list(out[:count])


def staged_call(
    body, name, grid, limit, mats, ins, outs, scratch=(), flops=0, hosted=None, collective=None
):
    holders = []
    for mat, chunks in mats:
        like = hosted.out_shapes()[0] if mat is None else mat
        holders.append(pltpu.VMEM(like.shape, like.dtype))
        holders.append(pltpu.SemaphoreType.DMA((chunks,)))
    given = [mat for mat, _ in mats if mat is not None]

    def staged(in_refs, out_refs, rest, gather):
        sources = list(in_refs[1 : 1 + len(given)])
        fetches = []
        for at, (mat, chunks) in enumerate(mats):
            source = gather.wholes[0] if mat is None else sources.pop(0)
            fetches.append(Fetch(source, rest[2 * at], rest[2 * at + 1], chunks))

        @pl.when(pl.program_id(0) == 0)
        def _():
            for fetch, (mat, _) in zip(fetches, mats):
                if mat is not None:
                    fetch.start()

        args = (in_refs[0], fetches, in_refs[1 + len(given) :], out_refs, rest[2 * len(mats) :])
        body(*args, gather)

    moved = sum(a.size * a.dtype.itemsize for a in given)
    moved += sum(a.size * a.dtype.itemsize for a, _ in ins)
    moved += sum(math.prod(s) * jnp.dtype(d).itemsize for s, d, _ in outs)
    return hosted_call(
        staged,
        name,
        grid,
        [(limit, SCALAR)] + [(mat, ANY) for mat in given] + list(ins),
        outs,
        [*holders, *scratch],
        flops,
        moved,
        hosted,
        collective,
    )


def project(name, limit, rows_in, mat, width, chunks, hosted=None, collective=None):
    total, depth = rows_in.shape
    block = min(256, total)
    step = width // chunks

    def body(limit, fetches, ins, outs, extra, gather):
        (fetch,) = fetches
        acts = gather.plan(hosted.skip, chunks, total // block, 1.1, 0.0) if gather else {}
        if gather and mat is None:

            @pl.when(pl.program_id(0) == 0)
            def _():
                gather.first(hosted.skip)
                fetch.start()

        left = ins[0][...]
        for chunk in range(chunks):
            if gather:
                gather.poll(acts, chunk)
            fetch.wait(chunk)
            columns = slice(chunk * step, (chunk + 1) * step)
            outs[0][:, columns] = nn(left, fetch.whole[:, columns]).astype(BF16)

    outs, wholes = staged_call(
        body,
        name,
        (total // block,),
        limit,
        [(mat, chunks)],
        [(rows_in, rows_spec(block, depth))],
        [((total, width), BF16, rows_spec(block, width))],
        flops=2 * total * depth * width,
        hosted=hosted,
        collective=collective,
    )
    return outs[0], wholes


def attend(name, limit, queries, keys, values, causal, hosted=None, collective=None, pace=3.3):
    q_len, k_len = queries[0].shape[0], keys[0].shape[0]
    pairs = 1024 // PAIR
    step = min(256, q_len)

    def body(ins, outs, extra, gather):
        limit_ref, q_ref, k_ref, v_ref = ins
        e_ref, o_ref, inv_ref = outs
        acts = gather.plan(0, 2, pairs, pace, 0.0) if gather else {}
        lanes = lax.broadcasted_iota(jnp.int32, (1, PAIR), 1)
        places = lax.broadcasted_iota(jnp.int32, (k_len, 1), 0)
        bias = jnp.where(places < limit_ref[0], 0.0, -1000000000.0)
        q_two = q_ref[...].astype(F32) * (1.0 / math.sqrt(HEAD))
        k_two = k_ref[...].astype(F32)
        v_two = v_ref[...].astype(F32)
        mixed = []
        for half in range(2):
            if gather:
                gather.poll(acts, half)
            own = (lanes >= HEAD * half) & (lanes < HEAD * (half + 1))
            spare = lanes == HEAD * (1 - half)
            q_own = jnp.where(own, q_two, jnp.where(spare, 1.0, 0.0)).astype(BF16)
            k_own = jnp.where(own, k_two, jnp.where(spare, bias, 0.0)).astype(BF16)
            v_own = jnp.where(own, v_two, jnp.where(spare, 1.0, 0.0)).T.astype(BF16)
            parts = []
            for start in range(0, q_len, step):
                scores = nt(k_own, q_own[start : start + step])
                if causal:
                    shape = (k_len, step)
                    key_at = lax.broadcasted_iota(jnp.int32, shape, 0)
                    query_at = lax.broadcasted_iota(jnp.int32, shape, 1) + start
                    scores = jnp.where(key_at <= query_at, scores, -1000000000.0)
                highest = jnp.max(scores, axis=0, keepdims=True)
                weights = jnp.exp(scores - highest).astype(BF16)
                e_ref[0, :, half * q_len + start : half * q_len + start + step] = weights
                parts.append(nn(v_own, weights))
            out = jnp.concatenate(parts, axis=1) if len(parts) > 1 else parts[0]
            at = HEAD * (1 - half)
            inverse = 1.0 / out[at : at + 1]
            own_rows = out[HEAD * half : HEAD * (half + 1)]
            mixed.append((own_rows * inverse, jnp.broadcast_to(inverse, own_rows.shape)))
        o_ref[...] = jnp.concatenate([mixed[0][0], mixed[1][0]], axis=0).T.astype(BF16)
        inv_ref[...] = jnp.concatenate([mixed[0][1], mixed[1][1]], axis=0).T

    def columns(rows, first):
        return pl.BlockSpec((rows, PAIR), lambda i: (0, first + i))

    outs, wholes = hosted_call(
        body,
        name,
        (pairs,),
        [
            (limit, SCALAR),
            (queries[0], columns(q_len, queries[1])),
            (keys[0], columns(k_len, keys[1])),
            (values[0], columns(k_len, values[1])),
        ],
        [
            (
                (pairs, k_len, 2 * q_len),
                BF16,
                pl.BlockSpec((1, k_len, 2 * q_len), lambda i: (i, 0, 0)),
            ),
            ((q_len, 1024), BF16, columns(q_len, 0)),
            ((q_len, 1024), F32, columns(q_len, 0)),
        ],
        [],
        16 * pairs * q_len * k_len * PAIR,
        4 * pairs * q_len * k_len,
        hosted,
        collective,
    )
    return *outs, wholes


def attend_grad(name, queries, keys, values, weights, mixture, inverse, upstream):
    q_len, k_len = queries[0].shape[0], keys[0].shape[0]
    pairs = 1024 // PAIR
    step = min(256, q_len)
    factor = 1.0 / math.sqrt(HEAD)

    def kernel(q_ref, k_ref, v_ref, e_ref, o_ref, inv_ref, do_ref, dq_ref, dk_ref, dv_ref, ds_ref):
        lanes = lax.broadcasted_iota(jnp.int32, (1, PAIR), 1)
        first = lanes < HEAD
        scaled = do_ref[...].astype(F32) * inv_ref[...]
        inner = scaled.astype(BF16).astype(F32) * o_ref[...].astype(F32)
        coarse = inner.astype(BF16)
        fine = (inner - coarse.astype(F32)).astype(BF16)
        picks = lax.broadcasted_iota(jnp.int32, (8, PAIR), 1)
        ones = [
            jnp.where(picks < HEAD, 1.0, 0.0).astype(BF16),
            jnp.where(picks < HEAD, 0.0, 1.0).astype(BF16),
        ]
        delta = [(nt(one, coarse) + nt(one, fine))[0:1] for one in ones]
        do_two = jnp.concatenate(
            [jnp.where(first, scaled, 0.0).astype(BF16), jnp.where(first, 0.0, scaled).astype(BF16)],
            axis=0,
        )
        q_all = q_ref[...].astype(F32) * factor
        q_two = jnp.concatenate(
            [jnp.where(first, q_all, 0.0).astype(BF16), jnp.where(first, 0.0, q_all).astype(BF16)],
            axis=0,
        )
        k_flip = k_ref[...].astype(F32).T.astype(BF16)
        v_all = v_ref[...]
        for half in range(2):
            for start in range(0, q_len, step):
                at = half * q_len + start
                probs_grad = nt(v_all, do_two[at : at + step])
                held = e_ref[0, :, at : at + step].astype(F32)
                ds_ref[:, at : at + step] = (
                    held * (probs_grad - delta[half][:, start : start + step])
                ).astype(BF16)
        dv_ref[...] = nn(e_ref[0], do_two).astype(BF16)
        dk_ref[...] = nn(ds_ref[...], q_two).astype(BF16)
        turned = nn(k_flip, ds_ref[...]) * factor
        rows = lax.broadcasted_iota(jnp.int32, (PAIR, 1), 0)
        dq_ref[...] = jnp.where(rows < HEAD, turned[:, :q_len], turned[:, q_len:]).T.astype(BF16)

    def columns(rows, at):
        return pl.BlockSpec((rows, PAIR), lambda i: (0, at + i))

    return pl.pallas_call(
        kernel,
        grid=(pairs,),
        in_specs=[
            columns(q_len, queries[1]),
            columns(k_len, keys[1]),
            columns(k_len, values[1]),
            pl.BlockSpec((1, k_len, 2 * q_len), lambda i: (i, 0, 0)),
            columns(q_len, 0),
            columns(q_len, 0),
            columns(q_len, 0),
        ],
        out_specs=[columns(q_len, 0), columns(k_len, 0), columns(k_len, 0)],
        out_shape=[
            jax.ShapeDtypeStruct((q_len, 1024), BF16),
            jax.ShapeDtypeStruct((k_len, 1024), BF16),
            jax.ShapeDtypeStruct((k_len, 1024), BF16),
        ],
        scratch_shapes=[pltpu.VMEM((k_len, 2 * q_len), BF16)],
        compiler_params=pltpu.CompilerParams(vmem_limit_bytes=VMEM_BYTES),
        cost_estimate=pl.CostEstimate(
            flops=32 * pairs * q_len * k_len * PAIR,
            bytes_accessed=4 * pairs * q_len * k_len,
            transcendentals=0,
        ),
        name=name,
    )(queries[0], keys[0], values[0], weights, mixture, inverse, upstream)


def row_mask(limit, block):
    at = lax.broadcasted_iota(jnp.int32, (block, 1), 0) + pl.program_id(0) * block
    return (at < limit).astype(F32)


def add_squares(ref, row, entries, mask):
    sums = jnp.sum(entries * entries * mask, axis=0, keepdims=True)
    first = pl.program_id(0) == 0

    @pl.when(first)
    def _():
        ref[row : row + 1, :] = sums

    @pl.when(jnp.logical_not(first))
    def _():
        ref[row : row + 1, :] += sums


def spread_lanes(column):
    return jnp.broadcast_to(column, (column.shape[0], 128))


def out_norm(name, limit, mixture, residual, gain, mat, next_mat=None, residual_gain=None):
    total, width = mixture.shape
    block = min(256, total)
    mats = [(mat, 1)] + ([] if next_mat is None else [(next_mat, 1)])

    def body(limit, fetches, ins, outs, extra, gather):
        o_ref, r_ref, g_ref, rg_ref = ins
        fetches[0].wait_all()
        added = nn(o_ref[...], fetches[0].whole[...])
        base = r_ref[...].astype(F32)
        if residual_gain is not None:
            base = base * rg_ref[...]
        unit, inverse = standardize(base + added)
        outs[0][...] = unit.astype(BF16)
        outs[1][...] = spread_lanes(inverse)
        add_squares(outs[2], 0, added, row_mask(limit[0], block))
        if next_mat is not None:
            fetches[1].wait_all()
            hidden = (unit * g_ref[...]).astype(BF16)
            outs[3][...] = nn(hidden, fetches[1].whole[...]).astype(BF16)

    outs = [
        ((total, width), BF16, rows_spec(block, width)),
        ((total, 128), F32, rows_spec(block, 128)),
        ((8, width), F32, whole_spec((8, width))),
    ]
    if next_mat is not None:
        outs.append(((total, width), BF16, rows_spec(block, width)))
    return staged_call(
        body,
        name,
        (total // block,),
        limit,
        mats,
        [
            (mixture, rows_spec(block, width)),
            (residual, rows_spec(block, width)),
            (gain, whole_spec((1, width))),
            (gain if residual_gain is None else residual_gain, whole_spec((1, width))),
        ],
        outs,
        flops=2 * total * width * width * len(mats),
    )[0]


def branch(
    name, limit, unit, gain, gain_out, w_in, w_back, down_low, up_low,
    hosted=None, collective=None, pace=2.4,
):
    total, width = unit.shape
    hidden_units = w_in.shape[1]
    adapter = down_low.shape[1]
    block = min(256, total)
    chunks = 4
    step = hidden_units // chunks

    def body(limit, fetches, ins, outs, extra, gather):
        u_ref, g_ref, go_ref, ad_ref, au_ref = ins
        y_ref, unit_ref, inv_ref, slope_ref, wa_ref, ad_slope_ref, sq_ref = outs
        (act,) = extra
        first, second = fetches
        hidden = u_ref[...].astype(F32) * g_ref[...]
        low = hidden.astype(BF16)
        pre = nn(low, ad_ref[...])
        gate = jax.nn.sigmoid(pre)
        wa = (pre * gate).astype(BF16)
        wa_ref[...] = wa
        ad_slope_ref[...] = (gate * (1.0 + pre * (1.0 - gate))).astype(BF16)
        adapted = 4.0 * nn(wa, au_ref[...])
        acts = gather.plan(0, chunks, total // block, pace, 0.0) if gather else {}
        for chunk in range(chunks):
            if gather:
                gather.poll(acts, chunk)
            first.wait(chunk)
            columns = slice(chunk * step, (chunk + 1) * step)
            fp = nn(low, first.whole[:, columns])
            cdf = 0.5 * (1.0 + lax.erf(fp * (1.0 / math.sqrt(2.0))))
            act[:, columns] = (fp * cdf).astype(BF16)
            bell = jnp.exp(-0.5 * fp * fp) * (1.0 / math.sqrt(2.0 * math.pi))
            slope_ref[:, columns] = (cdf + fp * bell).astype(BF16)
        second.wait_all()
        added = nn(act[...], second.whole[...]) + adapted
        out_unit, inverse = standardize(hidden + added)
        result = out_unit * go_ref[...]
        y_ref[...] = result.astype(BF16)
        unit_ref[...] = out_unit.astype(BF16)
        inv_ref[...] = spread_lanes(inverse)
        mask = row_mask(limit[0], block)
        add_squares(sq_ref, 0, added, mask)
        add_squares(sq_ref, 1, result, mask)

    outs, wholes = staged_call(
        body,
        name,
        (total // block,),
        limit,
        [(w_in, chunks), (w_back, 1)],
        [
            (unit, rows_spec(block, width)),
            (gain, whole_spec((1, width))),
            (gain_out, whole_spec((1, width))),
            (down_low, whole_spec(down_low.shape)),
            (up_low, whole_spec(up_low.shape)),
        ],
        [
            ((total, width), BF16, rows_spec(block, width)),
            ((total, width), BF16, rows_spec(block, width)),
            ((total, 128), F32, rows_spec(block, 128)),
            ((total, hidden_units), BF16, rows_spec(block, hidden_units)),
            ((total, adapter), BF16, rows_spec(block, adapter)),
            ((total, adapter), BF16, rows_spec(block, adapter)),
            ((8, width), F32, whole_spec((8, width))),
        ],
        scratch=[pltpu.VMEM((block, hidden_units), BF16)],
        flops=4 * total * width * (hidden_units + adapter),
        hosted=hosted,
        collective=collective,
    )
    return *outs, wholes


def adapter_grad(upstream, refs):
    (uo_ref, io_ref, go_ref, ui_ref, gi_ref, wa_ref, as_ref, ad_ref, au_ref) = refs
    grad_two = standardize_grad(uo_ref[...].astype(F32), io_ref[:, 0:1], upstream * go_ref[...])
    dvd = (4.0 * grad_two).astype(BF16)
    low = (ui_ref[...].astype(F32) * gi_ref[...]).astype(BF16)
    du = (nt(dvd, au_ref[...]) * as_ref[...].astype(F32)).astype(BF16)
    total = grad_two + nt(du, ad_ref[...])
    return grad_two.astype(BF16), total, tn(low, du), tn(wa_ref[...], dvd)


def hidden_grad(dz, total, fetches, refs, dfp, chunks):
    slope_ref, ui_ref, ii_ref, gi_ref = refs
    back, within, last = fetches
    step = dfp.shape[1] // chunks
    back.wait_all()
    for chunk in range(chunks):
        columns = slice(chunk * step, (chunk + 1) * step)
        act_grad = nt(dz, back.whole[columns, :])
        dfp[:, columns] = (act_grad * slope_ref[:, columns].astype(F32)).astype(BF16)
    within.wait_all()
    total = total + nt(dfp[...], within.whole[...])
    grad_one = standardize_grad(ui_ref[...].astype(F32), ii_ref[:, 0:1], total * gi_ref[...])
    last.wait_all()
    return grad_one, nt(grad_one.astype(BF16), last.whole[...]).astype(BF16)


def dec_branch_grad(
    name, limits, cot, saved_out, gain_out, saved_in, gain_in, slope, wa, ad_slope,
    w_back, w_in, w_out, down_low, up_low, squares,
):
    total, width = cot.shape
    hidden_units = w_in.shape[1]
    adapter = down_low.shape[1]
    whole = [
        cot, saved_out[0], saved_out[1], gain_out, saved_in[0], gain_in, wa, ad_slope, down_low,
        up_low, slope, saved_in[1], *squares,
    ]

    def body(limit, fetches, ins, outs, extra, gather):
        grad_ref, mix_ref, down_ref, up_ref = outs
        (other,), cot_ref, slope_ref, ii_ref = ins[:1], ins[1], ins[11], ins[12]
        dz, part, down_ref[...], up_ref[:adapter] = adapter_grad(cot_ref[...].astype(F32), ins[2:11])
        sums = [ref[row : row + 1, :] for ref, rows in zip(ins[13:], (1, 2, 1, 1, 2)) for row in range(rows)]
        lanes = lax.broadcasted_iota(jnp.int32, (1, width), 1)
        counts = jnp.where(lanes == 0, limit[0], jnp.where(lanes == 1, other[0], 0)).astype(F32)
        up_ref[adapter:] = jnp.concatenate([*sums, counts], axis=0)
        grad_ref[...], mix_ref[...] = hidden_grad(
            dz, part, fetches, (slope_ref, ins[5], ii_ref, ins[6]), extra[0], 4
        )

    return staged_call(
        body,
        name,
        (1,),
        limits[0],
        [(w_back, 1), (w_in, 1), (w_out, 1)],
        [(limits[1], SCALAR)] + [(a, whole_spec(a.shape)) for a in whole],
        [
            (cot.shape, F32, whole_spec(cot.shape)),
            (cot.shape, BF16, whole_spec(cot.shape)),
            (down_low.shape, F32, whole_spec(down_low.shape)),
            ((adapter + 8, width), F32, whole_spec((adapter + 8, width))),
        ],
        scratch=[pltpu.VMEM((total, hidden_units), BF16)],
        flops=4 * total * width * (hidden_units + 2 * adapter),
    )[0]


def enc_adapter_grad(
    name, limit, cot, cross, cross_mat, saved_out, gain_out, saved_in, gain_in, wa, ad_slope,
    down_low, up_low,
):
    total, width = cot.shape
    adapter = down_low.shape[1]
    block = min(256, total)
    rows = rows_spec(block, width)

    def body(limit, fetches, ins, outs, extra, gather):
        dz_ref, part_ref, down_ref, up_ref = outs
        down_sum, up_sum = extra
        fetches[0].wait_all()
        upstream = ins[0][...].astype(F32)
        for at in range(2):
            upstream = upstream + nt(ins[1 + at][...], fetches[0].whole[:, at * width : (at + 1) * width])
        dz_ref[...], part_ref[...], down_part, up_part = adapter_grad(upstream, ins[3:])
        at = pl.program_id(0)

        @pl.when(at == 0)
        def _():
            up_sum[...] = up_part
            down_sum[...] = down_part

        @pl.when(at > 0)
        def _():
            up_sum[...] += up_part
            down_sum[...] += down_part

        @pl.when(at == total // block - 1)
        def _():
            up_ref[...] = up_sum[...].astype(BF16)
            down_ref[...] = down_sum[...].astype(BF16)

    return staged_call(
        body,
        name,
        (total // block,),
        limit,
        [(cross_mat, 1)],
        [
            (cot, rows),
            (cross[0], rows),
            (cross[1], rows),
            (saved_out[0], rows),
            (saved_out[1], rows_spec(block, 128)),
            (gain_out, whole_spec((1, width))),
            (saved_in[0], rows),
            (gain_in, whole_spec((1, width))),
            (wa, rows_spec(block, adapter)),
            (ad_slope, rows_spec(block, adapter)),
            (down_low, whole_spec(down_low.shape)),
            (up_low, whole_spec(up_low.shape)),
        ],
        [
            ((total, width), BF16, rows),
            ((total, width), F32, rows),
            (down_low.shape, BF16, whole_spec(down_low.shape)),
            (up_low.shape, BF16, whole_spec(up_low.shape)),
        ],
        scratch=[pltpu.VMEM(down_low.shape, F32), pltpu.VMEM(up_low.shape, F32)],
        flops=4 * total * width * (width + 2 * adapter),
    )[0]


def enc_hidden_grad(name, limit, dz, part, slope, saved_in, gain_in, w_back, w_in, w_out):
    total, width = dz.shape
    hidden_units = w_in.shape[1]
    block = min(256, total)
    rows = rows_spec(block, width)

    def body(limit, fetches, ins, outs, extra, gather):
        outs[0][...], outs[1][...] = hidden_grad(
            ins[0][...], ins[1][...], fetches, ins[2:], extra[0], 4
        )

    return staged_call(
        body,
        name,
        (total // block,),
        limit,
        [(w_back, 1), (w_in, 1), (w_out, 1)],
        [
            (dz, rows),
            (part, rows),
            (slope, rows_spec(block, hidden_units)),
            (saved_in[0], rows),
            (saved_in[1], rows_spec(block, 128)),
            (gain_in, whole_spec((1, width))),
        ],
        [((total, width), F32, rows), ((total, width), BF16, rows)],
        scratch=[pltpu.VMEM((block, hidden_units), BF16)],
        flops=4 * total * width * hidden_units,
    )[0]


def middle_grad(name, limit, grad_cross, dq, saved, gain, w_cq, w_so):
    total, width = dq.shape
    block = min(256, total)
    unit, inv = saved

    def body(limit, fetches, ins, outs, extra, gather):
        gc_ref, dq_ref, u_ref, i_ref, g_ref = ins
        fetches[0].wait_all()
        hidden_grad = gc_ref[...] + nt(dq_ref[...], fetches[0].whole[...])
        grad_self = standardize_grad(
            u_ref[...].astype(F32), i_ref[:, 0:1], hidden_grad * g_ref[...]
        )
        outs[0][...] = grad_self
        fetches[1].wait_all()
        outs[1][...] = nt(grad_self.astype(BF16), fetches[1].whole[...]).astype(BF16)

    return staged_call(
        body,
        name,
        (total // block,),
        limit,
        [(w_cq, 1), (w_so, 1)],
        [
            (grad_cross, rows_spec(block, width)),
            (dq, rows_spec(block, width)),
            (unit, rows_spec(block, width)),
            (inv, rows_spec(block, 128)),
            (gain, whole_spec((1, width))),
        ],
        [
            ((total, width), F32, rows_spec(block, width)),
            ((total, width), BF16, rows_spec(block, width)),
        ],
        flops=4 * total * width * width,
    )[0]


def input_grad(name, limit, base, parts, mat):
    total, width = base.shape
    block = min(256, total)
    count = len(parts)

    def body(limit, fetches, ins, outs, extra, gather):
        (fetch,) = fetches
        result = ins[0][...]
        for at in range(count):
            fetch.wait(at)
            result = result + nt(ins[1 + at][...], fetch.whole[:, at * width : (at + 1) * width])
        outs[0][...] = result

    return staged_call(
        body,
        name,
        (total // block,),
        limit,
        [(mat, count)],
        [(base, rows_spec(block, width))] + [(p, rows_spec(block, width)) for p in parts],
        [((total, width), F32, rows_spec(block, width))],
        flops=2 * total * width * width * count,
    )[0][0]


NAMES = (
    "enc_qkv",
    "enc_attn_out",
    "enc_ffn_in",
    "enc_ffn_out",
    "dec_self_qkv",
    "dec_self_out",
    "dec_cross_q",
    "dec_cross_kv",
    "dec_cross_out",
    "dec_ffn_in",
    "dec_ffn_out",
)


class Weights(dict):
    def __init__(self, blocks, hosting, fsdp):
        super().__init__()
        self.blocks, self.hosting, self.fsdp = blocks, hosting, fsdp
        if not hosting:
            for name, block in blocks.items():
                self[name] = lax.all_gather(block, "fsdp", axis=0, tiled=True)

    def host(self, collective, *names, skip_first=False):
        self.names = names
        if not self.hosting:
            return {}
        owns = [self.blocks[name] for name in names]
        return {"hosted": Hosted(owns, skip_first, self.fsdp), "collective": collective}

    def take(self, wholes):
        self.update(zip(self.names, wholes))


def layers(enc_limit, dec_limit, enc_input, dec_input, enc_cot, dec_cot, w, gains, adapters):
    gain = [gains[k : k + 1] for k in range(5)]
    enc_down, enc_up, dec_down, dec_up = (a.astype(BF16) for a in adapters)
    host = w.host(1, "enc_qkv", "enc_attn_out", "dec_self_out", skip_first=True)
    qkv, wholes = project("enc_project", enc_limit, enc_input, w.get("enc_qkv"), 3072, 3, **host)
    w.take(wholes)
    host = w.host(2, "enc_ffn_in", "enc_ffn_out")
    e_enc, o_enc, inv_enc, wholes = attend(
        "enc_attend", enc_limit, (qkv, 0), (qkv, 8), (qkv, 16), False, **host
    )
    w.take(wholes)
    unit1, dev1, sq_a = out_norm("enc_out_norm", enc_limit, o_enc, enc_input, gain[0], w["enc_attn_out"])
    host = w.host(3, "dec_self_qkv", "dec_cross_kv", "dec_cross_q")
    enc_out, unit2, dev2, slope_e, wa_e, ads_e, sq_b, wholes = branch(
        "enc_branch", enc_limit, unit1, gain[0], gain[1], w["enc_ffn_in"], w["enc_ffn_out"],
        enc_down, enc_up, **host,
    )
    w.take(wholes)
    sqkv, _ = project("dec_project", dec_limit, dec_input, w["dec_self_qkv"], 3072, 3)
    e_self, o_self, inv_self, _ = attend(
        "dec_attend", dec_limit, (sqkv, 0), (sqkv, 8), (sqkv, 16), True
    )
    unit3, dev3, sq_c, cross_q = out_norm(
        "dec_out_norm", dec_limit, o_self, dec_input, gain[2], w["dec_self_out"], w["dec_cross_q"]
    )
    kv, _ = project("cross_project", enc_limit, enc_out, w["dec_cross_kv"], 2048, 2)
    host = w.host(4, "dec_cross_out", "dec_ffn_in", "dec_ffn_out")
    e_cross, o_cross, inv_cross, wholes = attend(
        "cross_attend", enc_limit, (cross_q, 0), (kv, 0), (kv, 8), False, pace=1.0, **host
    )
    w.take(wholes)
    unit4, dev4, sq_d = out_norm(
        "cross_out_norm", dec_limit, o_cross, unit3, gain[3], w["dec_cross_out"], residual_gain=gain[2]
    )
    dec_out, unit5, dev5, slope_d, wa_d, ads_d, sq_e, _ = branch(
        "dec_branch", dec_limit, unit4, gain[3], gain[4], w["dec_ffn_in"], w["dec_ffn_out"],
        dec_down, dec_up,
    )
    grad_cross, do_cross, dec_down_grad, dec_up_grad = dec_branch_grad(
        "dec_branch_grad", (enc_limit, dec_limit), dec_cot, (unit5, dev5), gain[4], (unit4, dev4), gain[3],
        slope_d, wa_d, ads_d, w["dec_ffn_out"], w["dec_ffn_in"], w["dec_cross_out"], dec_down, dec_up,
        (sq_a, sq_b, sq_c, sq_d, sq_e),
    )
    dcq, dck, dcv = attend_grad(
        "cross_attend_grad", (cross_q, 0), (kv, 0), (kv, 8), e_cross, o_cross, inv_cross, do_cross
    )
    dz, part, enc_down_grad, enc_up_grad = enc_adapter_grad(
        "enc_adapter_grad", enc_limit, enc_cot, (dck, dcv), w["dec_cross_kv"], (unit2, dev2), gain[1],
        (unit1, dev1), gain[0], wa_e, ads_e, enc_down, enc_up,
    )
    grad_self, do_self = middle_grad(
        "dec_middle_grad", dec_limit, grad_cross, dcq, (unit3, dev3), gain[2], w["dec_cross_q"], w["dec_self_out"]
    )
    dsq, dsk, dsv = attend_grad(
        "dec_attend_grad", (sqkv, 0), (sqkv, 8), (sqkv, 16), e_self, o_self, inv_self, do_self
    )
    dec_grad = input_grad("dec_input_grad", dec_limit, grad_self, [dsq, dsk, dsv], w["dec_self_qkv"])
    grad_one, do_enc = enc_hidden_grad(
        "enc_hidden_grad", enc_limit, dz, part, slope_e, (unit1, dev1), gain[0],
        w["enc_ffn_out"], w["enc_ffn_in"], w["enc_attn_out"],
    )
    deq, dek, dev = attend_grad(
        "enc_attend_grad", (qkv, 0), (qkv, 8), (qkv, 16), e_enc, o_enc, inv_enc, do_enc
    )
    enc_grad = input_grad("enc_input_grad", enc_limit, grad_one, [deq, dek, dev], w["enc_qkv"])
    return (
        (enc_out, dec_out, enc_grad, dec_grad),
        (enc_down_grad, enc_up_grad),
        (dec_down_grad, dec_up_grad),
    )


def shards(fsdp, dp, enc_input, dec_input, enc_cot, dec_cot, *rest):
    mats, (gains, enc_down, enc_up, dec_down, dec_up, enc_lengths, dec_lengths) = rest[:11], rest[11:]
    weights = Weights(dict(zip(NAMES, mats)), fsdp == 8 and dp % 2 == 0, fsdp)
    results, enc_grads, dec_grads = layers(
        enc_lengths, dec_lengths, enc_input, dec_input, enc_cot, dec_cot, weights, gains,
        (enc_down, enc_up, dec_down, dec_up),
    )
    everyone = ("fsdp", "dp")
    dec_down_grad, dec_up_grad = lax.psum(dec_grads, everyone)
    enc_down_grad, enc_up_grad = lax.psum(enc_grads, everyone)
    width = enc_input.shape[1]
    adapter = dec_up.shape[0]
    statistics = dec_up_grad[adapter:]
    rows = jnp.stack([statistics[7, 0]] * 3 + [statistics[7, 1]] * 4)
    rms = jnp.sqrt(jnp.sum(statistics[:7], axis=1) / (rows * width))
    return (
        *results,
        enc_down_grad.astype(F32),
        enc_up_grad.astype(F32),
        dec_down_grad,
        dec_up_grad[:adapter],
        rms,
    )


def solution(mesh):
    by_rows = P(("fsdp", "dp"), None)
    placed = (by_rows,) * 4 + (P("fsdp", None),) * 11 + (P(),) * 5 + (P(("fsdp", "dp")),) * 2
    return jax.shard_map(
        functools.partial(shards, mesh.shape["fsdp"], mesh.shape["dp"]),
        mesh=mesh,
        in_specs=placed,
        out_specs=(by_rows,) * 4 + (P(),) * 5,
        check_vma=False,
    )
```

```python
import functools
import math

import jax
import jax.numpy as jnp
from jax import lax
from jax.experimental import pallas as pl
from jax.experimental.pallas import tpu as pltpu
from jax.sharding import PartitionSpec as P

HEAD = 64
PAIR = 2 * HEAD
EPSILON = 1e-05
F32 = jnp.float32
BF16 = jnp.bfloat16
VMEM_BYTES = 58 * 2**20


def nn(former, latter):
    return jnp.dot(former, latter, preferred_element_type=F32)


def nt(former, latter):
    return lax.dot_general(
        former, latter, (((1,), (1,)), ((), ())), preferred_element_type=F32
    )


def tn(former, latter):
    return lax.dot_general(
        former, latter, (((0,), (0,)), ((), ())), preferred_element_type=F32
    )


def standardize(entries):
    centered = entries - jnp.mean(entries, axis=-1, keepdims=True)
    spread = jnp.mean(centered * centered, axis=-1, keepdims=True)
    inverse = lax.rsqrt(spread + EPSILON)
    return centered * inverse, inverse


def standardize_grad(unit, inverse, scaled):
    return inverse * (
        scaled
        - jnp.mean(scaled, axis=-1, keepdims=True)
        - unit * jnp.mean(scaled * unit, axis=-1, keepdims=True)
    )


class Fetch:
    def __init__(self, source, whole, sems, chunks):
        self.source, self.whole, self.sems, self.chunks = source, whole, sems, chunks

    def copy(self, chunk):
        width = self.whole.shape[1] // self.chunks
        columns = pl.ds(chunk * width, width)
        return pltpu.make_async_copy(
            self.source.at[:, columns], self.whole.at[:, columns], self.sems.at[chunk]
        )

    def start(self):
        for chunk in range(self.chunks):
            self.copy(chunk).start()

    def wait(self, chunk):
        @pl.when(pl.program_id(0) == 0)
        def _():
            self.copy(chunk).wait()

    def wait_all(self):
        for chunk in range(self.chunks):
            self.wait(chunk)


UNIT_US = 5.8
LEAD_US = 5.0


class Gather:
    def __init__(self, owns, wholes, splits, sends, recvs, locals_):
        self.owns, self.wholes, self.splits = owns, wholes, splits
        self.sends, self.recvs, self.locals = sends, recvs, locals_
        self.units = [(m, part) for m, split in enumerate(splits) for part in range(split)]
        f, z = lax.axis_index("fsdp"), lax.axis_index("dp")
        odd = z % 2
        y, x, core = f // 4, (f // 2) % 2, f % 2
        beside, above = f + 2 - 4 * x, f + 4 - 8 * y
        self.own = f
        self.direct = beside + odd * (above - beside)
        self.onward = above + odd * (beside - above)
        self.far = beside + 4 - 8 * y
        self.twin = f + 1 - 2 * core
        self.partner = z + 1 - 2 * odd

    def meet(self):
        barrier = pltpu.get_barrier_semaphore()
        mesh = pl.DeviceIdType.MESH
        for to in ({"fsdp": self.direct}, {"fsdp": self.onward}, {"fsdp": self.twin}, {"dp": self.partner}):
            pl.semaphore_signal(barrier, inc=1, device_id=to, device_id_type=mesh)
        pl.semaphore_wait(barrier, 4)

    def transfer(self, unit, kind):
        m, part = self.units[unit]
        whole, own = self.wholes[m], self.owns[m]
        block = own.shape[0]
        rows = block // self.splits[m]
        owner = (self.own, self.direct, self.direct, self.own, self.direct, self.far, self.onward)[kind]
        there = whole.at[pl.ds(pl.multiple_of(owner * block + part * rows, 16), rows), :]
        here = own.at[pl.ds(part * rows, rows), :] if kind in (0, 3) else there
        to = {"fsdp": (self.direct, self.onward, None, self.twin, self.twin, self.twin, self.twin)[kind]}
        if kind == 2:
            to = {"dp": self.partner}
        return pltpu.make_async_remote_copy(
            src_ref=here,
            dst_ref=there,
            send_sem=self.sends.at[unit, kind],
            recv_sem=self.recvs.at[unit, kind],
            device_id=to,
            device_id_type=pl.DeviceIdType.MESH,
        )

    def keep(self, m):
        block = self.owns[m].shape[0]
        rows = pl.ds(pl.multiple_of(self.own * block, 16), block)
        return pltpu.make_async_copy(self.owns[m], self.wholes[m].at[rows, :], self.locals.at[m])

    def begin(self):
        self.meet()
        for unit in range(len(self.units)):
            self.transfer(unit, 0).start()
        for unit in range(len(self.units)):
            self.transfer(unit, 3).start()
        for m in range(len(self.owns)):
            self.keep(m).start()

    def pass_on(self, unit):
        self.transfer(unit, 0).wait_recv()
        for kind in (1, 2, 4):
            self.transfer(unit, kind).start()

    def share(self, unit):
        self.transfer(unit, 1).wait_recv()
        self.transfer(unit, 5).start()
        self.transfer(unit, 2).wait_recv()
        self.transfer(unit, 6).start()

    def complete(self, m):
        for unit, (of, _) in enumerate(self.units):
            if of == m:
                for kind in (3, 4, 5, 6):
                    self.transfer(unit, kind).wait_recv()
        self.keep(m).wait()

    def finish(self):
        for unit in range(len(self.units)):
            for kind in range(7):
                self.transfer(unit, kind).wait_send()


ANY = pl.BlockSpec(memory_space=pl.ANY)
SCALAR = pl.BlockSpec(memory_space=pltpu.SMEM)


def rows_spec(rows, width):
    return pl.BlockSpec((rows, width), lambda i: (i, 0))


def whole_spec(shape):
    return pl.BlockSpec(shape, lambda i: (0,) * len(shape))


class Later:
    def __init__(self, shape, dtype):
        self.shape, self.dtype = tuple(shape), jnp.dtype(dtype)
        self.size = math.prod(self.shape)


class Recorder:
    def __init__(self, blocks, fsdp):
        self.names = list(blocks)
        self.owns = list(blocks.values())
        self.wholes = [Later((a.shape[0] * fsdp, a.shape[1]), a.dtype) for a in self.owns]
        self.splits = [4 if a.shape[1] == 3072 else max(1, a.size // 131072) for a in self.owns]
        self.stages = []

    def add(self, **stage):
        stage["results"] = [Later(shape, dtype) for shape, dtype, _ in stage["outs"]]
        self.stages.append(stage)
        return stage["results"]

    def schedule(self):
        acts, unit, due = [], 0, LEAD_US
        last_of = {}
        for m, split in enumerate(self.splits):
            for _ in range(split):
                time = UNIT_US * self.owns[m].size / split / 131072
                due += time
                acts.append((due, "pass_on", unit))
                acts.append((due + time + 2.0, "share", unit))
                last_of[m] = unit
                unit += 1
        acts.sort(key=lambda act: act[0])
        clock, plans = 0.0, []
        for stage in self.stages:
            before, ticks = [], {}
            needed = [last_of[self.wholes.index(mat)] for mat in stage["needs"]]
            if needed:
                while any(act[2] <= max(needed) for act in acts):
                    clock = max(clock, acts[0][0])
                    before.append(acts.pop(0)[1:])
            pace = stage["time"] / stage["grid"][0] / stage["slots"]
            for tick in range(stage["grid"][0] * stage["slots"]):
                while acts and acts[0][0] <= clock:
                    ticks.setdefault(divmod(tick, stage["slots"]), []).append(acts.pop(0)[1:])
                clock += pace
            plans.append((before, ticks))
        return plans, [act[1:] for act in acts]

    def run(self):
        given = []
        for stage in self.stages:
            for array, spec in stage["ins"]:
                if not isinstance(array, Later) and not any(array is g for g, _ in given):
                    given.append((array, SCALAR if spec is SCALAR else ANY))
        results = self.wholes + [r for stage in self.stages for r in stage["results"]]
        plans, left = self.schedule()
        units = sum(self.splits)

        def kernel(*refs):
            refs = list(refs)
            owns = refs[: len(self.owns)]
            of = {}
            for (array, _), ref in zip(given, refs[len(self.owns) :]):
                of[id(array)] = ref
            rest = refs[len(self.owns) + len(given) :]
            for result, ref in zip(results, rest):
                of[id(result)] = ref
            gather = Gather(owns, [of[id(w)] for w in self.wholes], self.splits, *rest[len(results) :])
            gather.begin()
            waited = set()

            def act(kind, unit):
                getattr(gather, kind)(unit)

            for stage, (before, ticks) in zip(self.stages, plans):
                for kind, unit in before:
                    act(kind, unit)
                for mat in stage["needs"]:
                    m = self.wholes.index(mat)
                    if m not in waited:
                        waited.add(m)
                        gather.complete(m)
                self.run_stage(stage, ticks, act, of)
            for kind, unit in left:
                act(kind, unit)
            for m in range(len(self.owns)):
                if m not in waited:
                    gather.complete(m)
            gather.finish()

        out = pl.pallas_call(
            kernel,
            in_specs=[ANY] * len(self.owns) + [spec for _, spec in given],
            out_specs=[ANY] * len(results),
            scratch_shapes=[
                pltpu.SemaphoreType.DMA((units, 7)),
                pltpu.SemaphoreType.DMA((units, 7)),
                pltpu.SemaphoreType.DMA((len(self.owns),)),
            ],
            out_shape=[jax.ShapeDtypeStruct(r.shape, r.dtype) for r in results],
            compiler_params=pltpu.CompilerParams(
                vmem_limit_bytes=VMEM_BYTES, collective_id=1, has_side_effects=True
            ),
            name="forward",
        )(*self.owns, *[array for array, _ in given])
        arrays = {id(result): array for result, array in zip(results, out)}
        return lambda later: arrays[id(later)]

    def run_stage(self, stage, ticks, act, of):
        ins, outs = stage["ins"], stage["outs"]
        piped = [at for at, (_, spec) in enumerate(ins) if spec is not ANY and spec is not SCALAR]
        fixed = {at: of[id(a)] for at, (a, _) in enumerate(ins) if at not in piped}

        def poll(slot):
            for (step, at), todo in ticks.items():
                if at == slot:

                    @pl.when(pl.program_id(0) == step)
                    def _(todo=todo):
                        for kind, unit in todo:
                            act(kind, unit)

        def scoped(*scratch):
            if stage["prepare"]:
                stage["prepare"]([fixed.get(at) for at in range(len(ins))], scratch)

            def body(*blocks):
                in_refs = [fixed.get(at) for at in range(len(ins))]
                for at, ref in zip(piped, blocks):
                    in_refs[at] = ref
                stage["body"](in_refs, list(blocks[len(piped) :]), scratch, poll)

            pltpu.emit_pipeline(
                body,
                grid=stage["grid"],
                in_specs=[ins[at][1] for at in piped],
                out_specs=[spec for _, _, spec in outs],
            )(*[of[id(ins[at][0])] for at in piped], *[of[id(r)] for r in stage["results"]])

        pl.run_scoped(scoped, *stage["scratch"])


def launch(
    body, name, grid, ins, outs, scratch, flops, moved, recorder=None, prepare=None, needs=(),
    slots=1, time=1.0,
):
    if recorder is not None:
        return recorder.add(
            body=body, grid=grid, ins=ins, outs=outs, scratch=scratch, prepare=prepare, needs=needs,
            slots=slots, time=time,
        )

    def kernel(*refs):
        in_refs, out_refs = list(refs[: len(ins)]), list(refs[len(ins) : len(ins) + len(outs)])
        rest = refs[len(ins) + len(outs) :]
        if prepare:

            @pl.when(pl.program_id(0) == 0)
            def _():
                prepare(in_refs, rest)

        body(in_refs, out_refs, rest, lambda slot: None)

    return pl.pallas_call(
        kernel,
        grid=grid,
        in_specs=[spec for _, spec in ins],
        out_specs=[spec for _, _, spec in outs],
        scratch_shapes=scratch,
        out_shape=[jax.ShapeDtypeStruct(s, d) for s, d, _ in outs],
        compiler_params=pltpu.CompilerParams(vmem_limit_bytes=VMEM_BYTES),
        cost_estimate=pl.CostEstimate(flops=flops, bytes_accessed=moved, transcendentals=0),
        name=name,
    )(*[a for a, _ in ins])


def staged_call(body, name, grid, limit, mats, ins, outs, scratch=(), flops=0, **record):
    holders = []
    for mat, chunks in mats:
        holders.append(pltpu.VMEM(mat.shape, mat.dtype))
        holders.append(pltpu.SemaphoreType.DMA((chunks,)))
    given = [mat for mat, _ in mats]

    def fetches(in_refs, rest):
        return [
            Fetch(in_refs[1 + at], rest[2 * at], rest[2 * at + 1], chunks)
            for at, (_, chunks) in enumerate(mats)
        ]

    def prepare(in_refs, rest):
        for fetch in fetches(in_refs, rest):
            fetch.start()

    def staged(in_refs, out_refs, rest, poll):
        args = (in_refs[0], fetches(in_refs, rest), in_refs[1 + len(given) :], out_refs)
        body(*args, rest[2 * len(mats) :], poll)

    moved = sum(a.size * a.dtype.itemsize for a in given)
    moved += sum(a.size * a.dtype.itemsize for a, _ in ins)
    moved += sum(math.prod(s) * jnp.dtype(d).itemsize for s, d, _ in outs)
    return launch(
        staged,
        name,
        grid,
        [(limit, SCALAR)] + [(mat, ANY) for mat in given] + list(ins),
        outs,
        [*holders, *scratch],
        flops,
        moved,
        prepare=prepare,
        needs=given if record else (),
        **record,
    )


def project(name, limit, rows_in, mat, chunks, **record):
    total, depth = rows_in.shape
    width = mat.shape[1]
    block = min(256, total)
    step = width // chunks

    def body(limit, fetches, ins, outs, extra, poll):
        (fetch,) = fetches
        left = ins[0][...]
        for chunk in range(chunks):
            poll(chunk)
            fetch.wait(chunk)
            columns = slice(chunk * step, (chunk + 1) * step)
            outs[0][:, columns] = nn(left, fetch.whole[:, columns]).astype(BF16)

    return staged_call(
        body,
        name,
        (total // block,),
        limit,
        [(mat, chunks)],
        [(rows_in, rows_spec(block, depth))],
        [((total, width), BF16, rows_spec(block, width))],
        flops=2 * total * depth * width,
        **record,
    )[0]


def attend(name, limit, queries, keys, values, causal, **record):
    q_len, k_len = queries[0].shape[0], keys[0].shape[0]
    pairs = 1024 // PAIR
    step = min(256, q_len)

    def body(ins, outs, extra, poll):
        limit_ref, q_ref, k_ref, v_ref = ins
        e_ref, o_ref, inv_ref = outs
        lanes = lax.broadcasted_iota(jnp.int32, (1, PAIR), 1)
        places = lax.broadcasted_iota(jnp.int32, (k_len, 1), 0)
        bias = jnp.where(places < limit_ref[0], 0.0, -1000000000.0)
        q_two = q_ref[...].astype(F32) * (1.0 / math.sqrt(HEAD))
        k_two = k_ref[...].astype(F32)
        v_two = v_ref[...].astype(F32)
        mixed = []
        for half in range(2):
            poll(half)
            own = (lanes >= HEAD * half) & (lanes < HEAD * (half + 1))
            spare = lanes == HEAD * (1 - half)
            q_own = jnp.where(own, q_two, jnp.where(spare, 1.0, 0.0)).astype(BF16)
            k_own = jnp.where(own, k_two, jnp.where(spare, bias, 0.0)).astype(BF16)
            v_own = jnp.where(own, v_two, jnp.where(spare, 1.0, 0.0)).T.astype(BF16)
            parts = []
            for start in range(0, q_len, step):
                scores = nt(k_own, q_own[start : start + step])
                if causal:
                    shape = (k_len, step)
                    key_at = lax.broadcasted_iota(jnp.int32, shape, 0)
                    query_at = lax.broadcasted_iota(jnp.int32, shape, 1) + start
                    scores = jnp.where(key_at <= query_at, scores, -1000000000.0)
                highest = jnp.max(scores, axis=0, keepdims=True)
                weights = jnp.exp(scores - highest).astype(BF16)
                e_ref[0, :, half * q_len + start : half * q_len + start + step] = weights
                parts.append(nn(v_own, weights))
            out = jnp.concatenate(parts, axis=1) if len(parts) > 1 else parts[0]
            at = HEAD * (1 - half)
            inverse = 1.0 / out[at : at + 1]
            own_rows = out[HEAD * half : HEAD * (half + 1)]
            mixed.append((own_rows * inverse, jnp.broadcast_to(inverse, own_rows.shape)))
        o_ref[...] = jnp.concatenate([mixed[0][0], mixed[1][0]], axis=0).T.astype(BF16)
        inv_ref[...] = jnp.concatenate([mixed[0][1], mixed[1][1]], axis=0).T

    def columns(rows, first):
        return pl.BlockSpec((rows, PAIR), lambda i: (0, first + i))

    return launch(
        body,
        name,
        (pairs,),
        [
            (limit, SCALAR),
            (queries[0], columns(q_len, queries[1])),
            (keys[0], columns(k_len, keys[1])),
            (values[0], columns(k_len, values[1])),
        ],
        [
            (
                (pairs, k_len, 2 * q_len),
                BF16,
                pl.BlockSpec((1, k_len, 2 * q_len), lambda i: (i, 0, 0)),
            ),
            ((q_len, 1024), BF16, columns(q_len, 0)),
            ((q_len, 1024), F32, columns(q_len, 0)),
        ],
        [],
        16 * pairs * q_len * k_len * PAIR,
        4 * pairs * q_len * k_len,
        **record,
    )


def attend_grad(name, queries, keys, values, weights, mixture, inverse, upstream):
    q_len, k_len = queries[0].shape[0], keys[0].shape[0]
    pairs = 1024 // PAIR
    step = min(256, q_len)
    factor = 1.0 / math.sqrt(HEAD)

    def kernel(q_ref, k_ref, v_ref, e_ref, o_ref, inv_ref, do_ref, dq_ref, dk_ref, dv_ref, ds_ref):
        lanes = lax.broadcasted_iota(jnp.int32, (1, PAIR), 1)
        first = lanes < HEAD
        scaled = do_ref[...].astype(F32) * inv_ref[...]
        inner = scaled.astype(BF16).astype(F32) * o_ref[...].astype(F32)
        coarse = inner.astype(BF16)
        fine = (inner - coarse.astype(F32)).astype(BF16)
        picks = lax.broadcasted_iota(jnp.int32, (8, PAIR), 1)
        ones = [
            jnp.where(picks < HEAD, 1.0, 0.0).astype(BF16),
            jnp.where(picks < HEAD, 0.0, 1.0).astype(BF16),
        ]
        delta = [(nt(one, coarse) + nt(one, fine))[0:1] for one in ones]
        do_two = jnp.concatenate(
            [jnp.where(first, scaled, 0.0).astype(BF16), jnp.where(first, 0.0, scaled).astype(BF16)],
            axis=0,
        )
        q_all = q_ref[...].astype(F32) * factor
        q_two = jnp.concatenate(
            [jnp.where(first, q_all, 0.0).astype(BF16), jnp.where(first, 0.0, q_all).astype(BF16)],
            axis=0,
        )
        k_flip = k_ref[...].astype(F32).T.astype(BF16)
        v_all = v_ref[...]
        for half in range(2):
            for start in range(0, q_len, step):
                at = half * q_len + start
                probs_grad = nt(v_all, do_two[at : at + step])
                held = e_ref[0, :, at : at + step].astype(F32)
                ds_ref[:, at : at + step] = (
                    held * (probs_grad - delta[half][:, start : start + step])
                ).astype(BF16)
        dv_ref[...] = nn(e_ref[0], do_two).astype(BF16)
        dk_ref[...] = nn(ds_ref[...], q_two).astype(BF16)
        turned = nn(k_flip, ds_ref[...]) * factor
        rows = lax.broadcasted_iota(jnp.int32, (PAIR, 1), 0)
        dq_ref[...] = jnp.where(rows < HEAD, turned[:, :q_len], turned[:, q_len:]).T.astype(BF16)

    def columns(rows, at):
        return pl.BlockSpec((rows, PAIR), lambda i: (0, at + i))

    return pl.pallas_call(
        kernel,
        grid=(pairs,),
        in_specs=[
            columns(q_len, queries[1]),
            columns(k_len, keys[1]),
            columns(k_len, values[1]),
            pl.BlockSpec((1, k_len, 2 * q_len), lambda i: (i, 0, 0)),
            columns(q_len, 0),
            columns(q_len, 0),
            columns(q_len, 0),
        ],
        out_specs=[columns(q_len, 0), columns(k_len, 0), columns(k_len, 0)],
        out_shape=[
            jax.ShapeDtypeStruct((q_len, 1024), BF16),
            jax.ShapeDtypeStruct((k_len, 1024), BF16),
            jax.ShapeDtypeStruct((k_len, 1024), BF16),
        ],
        scratch_shapes=[pltpu.VMEM((k_len, 2 * q_len), BF16)],
        compiler_params=pltpu.CompilerParams(vmem_limit_bytes=VMEM_BYTES),
        cost_estimate=pl.CostEstimate(
            flops=32 * pairs * q_len * k_len * PAIR,
            bytes_accessed=4 * pairs * q_len * k_len,
            transcendentals=0,
        ),
        name=name,
    )(queries[0], keys[0], values[0], weights, mixture, inverse, upstream)


def row_mask(limit, block):
    at = lax.broadcasted_iota(jnp.int32, (block, 1), 0) + pl.program_id(0) * block
    return (at < limit).astype(F32)


def add_squares(ref, row, entries, mask):
    sums = jnp.sum(entries * entries * mask, axis=0, keepdims=True)
    first = pl.program_id(0) == 0

    @pl.when(first)
    def _():
        ref[row : row + 1, :] = sums

    @pl.when(jnp.logical_not(first))
    def _():
        ref[row : row + 1, :] += sums


def spread_lanes(column):
    return jnp.broadcast_to(column, (column.shape[0], 128))


def out_norm(name, limit, mixture, residual, gain, mat, next_mat=None, residual_gain=None, **record):
    total, width = mixture.shape
    block = min(256, total)
    mats = [(mat, 1)] + ([] if next_mat is None else [(next_mat, 1)])

    def body(limit, fetches, ins, outs, extra, poll):
        poll(0)
        o_ref, r_ref, g_ref, rg_ref = ins
        fetches[0].wait_all()
        added = nn(o_ref[...], fetches[0].whole[...])
        base = r_ref[...].astype(F32)
        if residual_gain is not None:
            base = base * rg_ref[...]
        unit, inverse = standardize(base + added)
        outs[0][...] = unit.astype(BF16)
        outs[1][...] = spread_lanes(inverse)
        add_squares(outs[2], 0, added, row_mask(limit[0], block))
        if next_mat is not None:
            fetches[1].wait_all()
            hidden = (unit * g_ref[...]).astype(BF16)
            outs[3][...] = nn(hidden, fetches[1].whole[...]).astype(BF16)

    outs = [
        ((total, width), BF16, rows_spec(block, width)),
        ((total, 128), F32, rows_spec(block, 128)),
        ((8, width), F32, whole_spec((8, width))),
    ]
    if next_mat is not None:
        outs.append(((total, width), BF16, rows_spec(block, width)))
    return staged_call(
        body,
        name,
        (total // block,),
        limit,
        mats,
        [
            (mixture, rows_spec(block, width)),
            (residual, rows_spec(block, width)),
            (gain, whole_spec((1, width))),
            (gain if residual_gain is None else residual_gain, whole_spec((1, width))),
        ],
        outs,
        flops=2 * total * width * width * len(mats),
        **record,
    )


def branch(name, limit, unit, gain, gain_out, w_in, w_back, down_low, up_low, **record):
    total, width = unit.shape
    hidden_units = w_in.shape[1]
    adapter = down_low.shape[1]
    block = min(256, total)
    chunks = 4
    step = hidden_units // chunks

    def body(limit, fetches, ins, outs, extra, poll):
        u_ref, g_ref, go_ref, ad_ref, au_ref = ins
        y_ref, unit_ref, inv_ref, slope_ref, wa_ref, ad_slope_ref, sq_ref = outs
        (act,) = extra
        first, second = fetches
        hidden = u_ref[...].astype(F32) * g_ref[...]
        low = hidden.astype(BF16)
        pre = nn(low, ad_ref[...].astype(BF16))
        gate = jax.nn.sigmoid(pre)
        wa = (pre * gate).astype(BF16)
        wa_ref[...] = wa
        ad_slope_ref[...] = (gate * (1.0 + pre * (1.0 - gate))).astype(BF16)
        adapted = 4.0 * nn(wa, au_ref[...].astype(BF16))
        for chunk in range(chunks):
            poll(chunk)
            first.wait(chunk)
            columns = slice(chunk * step, (chunk + 1) * step)
            fp = nn(low, first.whole[:, columns])
            cdf = 0.5 * (1.0 + lax.erf(fp * (1.0 / math.sqrt(2.0))))
            act[:, columns] = (fp * cdf).astype(BF16)
            bell = jnp.exp(-0.5 * fp * fp) * (1.0 / math.sqrt(2.0 * math.pi))
            slope_ref[:, columns] = (cdf + fp * bell).astype(BF16)
        second.wait_all()
        added = nn(act[...], second.whole[...]) + adapted
        out_unit, inverse = standardize(hidden + added)
        result = out_unit * go_ref[...]
        y_ref[...] = result.astype(BF16)
        unit_ref[...] = out_unit.astype(BF16)
        inv_ref[...] = spread_lanes(inverse)
        mask = row_mask(limit[0], block)
        add_squares(sq_ref, 0, added, mask)
        add_squares(sq_ref, 1, result, mask)

    return staged_call(
        body,
        name,
        (total // block,),
        limit,
        [(w_in, chunks), (w_back, 1)],
        [
            (unit, rows_spec(block, width)),
            (gain, whole_spec((1, width))),
            (gain_out, whole_spec((1, width))),
            (down_low, whole_spec(down_low.shape)),
            (up_low, whole_spec(up_low.shape)),
        ],
        [
            ((total, width), BF16, rows_spec(block, width)),
            ((total, width), BF16, rows_spec(block, width)),
            ((total, 128), F32, rows_spec(block, 128)),
            ((total, hidden_units), BF16, rows_spec(block, hidden_units)),
            ((total, adapter), BF16, rows_spec(block, adapter)),
            ((total, adapter), BF16, rows_spec(block, adapter)),
            ((8, width), F32, whole_spec((8, width))),
        ],
        scratch=[pltpu.VMEM((block, hidden_units), BF16)],
        flops=4 * total * width * (hidden_units + adapter),
        **record,
    )


def adapter_grad(upstream, refs):
    (uo_ref, io_ref, go_ref, ui_ref, gi_ref, wa_ref, as_ref, ad_ref, au_ref) = refs
    grad_two = standardize_grad(uo_ref[...].astype(F32), io_ref[:, 0:1], upstream * go_ref[...])
    dvd = (4.0 * grad_two).astype(BF16)
    low = (ui_ref[...].astype(F32) * gi_ref[...]).astype(BF16)
    du = (nt(dvd, au_ref[...].astype(BF16)) * as_ref[...].astype(F32)).astype(BF16)
    total = grad_two + nt(du, ad_ref[...].astype(BF16))
    return grad_two.astype(BF16), total, tn(low, du), tn(wa_ref[...], dvd)


def hidden_grad(dz, total, fetches, refs, dfp, chunks):
    slope_ref, ui_ref, ii_ref, gi_ref = refs
    back, within, last = fetches
    step = dfp.shape[1] // chunks
    back.wait_all()
    for chunk in range(chunks):
        columns = slice(chunk * step, (chunk + 1) * step)
        act_grad = nt(dz, back.whole[columns, :])
        dfp[:, columns] = (act_grad * slope_ref[:, columns].astype(F32)).astype(BF16)
    within.wait_all()
    total = total + nt(dfp[...], within.whole[...])
    grad_one = standardize_grad(ui_ref[...].astype(F32), ii_ref[:, 0:1], total * gi_ref[...])
    last.wait_all()
    return grad_one, nt(grad_one.astype(BF16), last.whole[...]).astype(BF16)


def dec_branch_grad(
    name, limits, cot, saved_out, gain_out, saved_in, gain_in, slope, wa, ad_slope,
    w_back, w_in, w_out, down_low, up_low, squares,
):
    total, width = cot.shape
    hidden_units = w_in.shape[1]
    adapter = down_low.shape[1]
    whole = [
        cot, saved_out[0], saved_out[1], gain_out, saved_in[0], gain_in, wa, ad_slope, down_low,
        up_low, slope, saved_in[1], *squares,
    ]

    def body(limit, fetches, ins, outs, extra, poll):
        grad_ref, mix_ref, down_ref, up_ref = outs
        (other,), cot_ref, slope_ref, ii_ref = ins[:1], ins[1], ins[11], ins[12]
        dz, part, down_ref[...], up_ref[:adapter] = adapter_grad(cot_ref[...].astype(F32), ins[2:11])
        sums = [ref[row : row + 1, :] for ref, rows in zip(ins[13:], (1, 2, 1, 1, 2)) for row in range(rows)]
        lanes = lax.broadcasted_iota(jnp.int32, (1, width), 1)
        counts = jnp.where(lanes == 0, limit[0], jnp.where(lanes == 1, other[0], 0)).astype(F32)
        up_ref[adapter:] = jnp.concatenate([*sums, counts], axis=0)
        grad_ref[...], mix_ref[...] = hidden_grad(
            dz, part, fetches, (slope_ref, ins[5], ii_ref, ins[6]), extra[0], 4
        )

    return staged_call(
        body,
        name,
        (1,),
        limits[0],
        [(w_back, 1), (w_in, 1), (w_out, 1)],
        [(limits[1], SCALAR)] + [(a, whole_spec(a.shape)) for a in whole],
        [
            (cot.shape, F32, whole_spec(cot.shape)),
            (cot.shape, BF16, whole_spec(cot.shape)),
            (down_low.shape, F32, whole_spec(down_low.shape)),
            ((adapter + 8, width), F32, whole_spec((adapter + 8, width))),
        ],
        scratch=[pltpu.VMEM((total, hidden_units), BF16)],
        flops=4 * total * width * (hidden_units + 2 * adapter),
    )


def enc_adapter_grad(
    name, limit, cot, cross, cross_mat, saved_out, gain_out, saved_in, gain_in, wa, ad_slope,
    down_low, up_low,
):
    total, width = cot.shape
    adapter = down_low.shape[1]
    block = min(256, total)
    rows = rows_spec(block, width)

    def body(limit, fetches, ins, outs, extra, poll):
        dz_ref, part_ref, down_ref, up_ref = outs
        down_sum, up_sum = extra
        fetches[0].wait_all()
        upstream = ins[0][...].astype(F32)
        for at in range(2):
            upstream = upstream + nt(ins[1 + at][...], fetches[0].whole[:, at * width : (at + 1) * width])
        dz_ref[...], part_ref[...], down_part, up_part = adapter_grad(upstream, ins[3:])
        at = pl.program_id(0)

        @pl.when(at == 0)
        def _():
            up_sum[...] = up_part
            down_sum[...] = down_part

        @pl.when(at > 0)
        def _():
            up_sum[...] += up_part
            down_sum[...] += down_part

        @pl.when(at == total // block - 1)
        def _():
            up_ref[...] = up_sum[...].astype(BF16)
            down_ref[...] = down_sum[...].astype(BF16)

    return staged_call(
        body,
        name,
        (total // block,),
        limit,
        [(cross_mat, 1)],
        [
            (cot, rows),
            (cross[0], rows),
            (cross[1], rows),
            (saved_out[0], rows),
            (saved_out[1], rows_spec(block, 128)),
            (gain_out, whole_spec((1, width))),
            (saved_in[0], rows),
            (gain_in, whole_spec((1, width))),
            (wa, rows_spec(block, adapter)),
            (ad_slope, rows_spec(block, adapter)),
            (down_low, whole_spec(down_low.shape)),
            (up_low, whole_spec(up_low.shape)),
        ],
        [
            ((total, width), BF16, rows),
            ((total, width), F32, rows),
            (down_low.shape, BF16, whole_spec(down_low.shape)),
            (up_low.shape, BF16, whole_spec(up_low.shape)),
        ],
        scratch=[pltpu.VMEM(down_low.shape, F32), pltpu.VMEM(up_low.shape, F32)],
        flops=4 * total * width * (width + 2 * adapter),
    )


def enc_hidden_grad(name, limit, dz, part, slope, saved_in, gain_in, w_back, w_in, w_out):
    total, width = dz.shape
    hidden_units = w_in.shape[1]
    block = min(256, total)
    rows = rows_spec(block, width)

    def body(limit, fetches, ins, outs, extra, poll):
        outs[0][...], outs[1][...] = hidden_grad(
            ins[0][...], ins[1][...], fetches, ins[2:], extra[0], 4
        )

    return staged_call(
        body,
        name,
        (total // block,),
        limit,
        [(w_back, 1), (w_in, 1), (w_out, 1)],
        [
            (dz, rows),
            (part, rows),
            (slope, rows_spec(block, hidden_units)),
            (saved_in[0], rows),
            (saved_in[1], rows_spec(block, 128)),
            (gain_in, whole_spec((1, width))),
        ],
        [((total, width), F32, rows), ((total, width), BF16, rows)],
        scratch=[pltpu.VMEM((block, hidden_units), BF16)],
        flops=4 * total * width * hidden_units,
    )


def middle_grad(name, limit, grad_cross, dq, saved, gain, w_cq, w_so):
    total, width = dq.shape
    block = min(256, total)
    unit, inv = saved

    def body(limit, fetches, ins, outs, extra, poll):
        gc_ref, dq_ref, u_ref, i_ref, g_ref = ins
        fetches[0].wait_all()
        hidden_grad = gc_ref[...] + nt(dq_ref[...], fetches[0].whole[...])
        grad_self = standardize_grad(
            u_ref[...].astype(F32), i_ref[:, 0:1], hidden_grad * g_ref[...]
        )
        outs[0][...] = grad_self
        fetches[1].wait_all()
        outs[1][...] = nt(grad_self.astype(BF16), fetches[1].whole[...]).astype(BF16)

    return staged_call(
        body,
        name,
        (total // block,),
        limit,
        [(w_cq, 1), (w_so, 1)],
        [
            (grad_cross, rows_spec(block, width)),
            (dq, rows_spec(block, width)),
            (unit, rows_spec(block, width)),
            (inv, rows_spec(block, 128)),
            (gain, whole_spec((1, width))),
        ],
        [
            ((total, width), F32, rows_spec(block, width)),
            ((total, width), BF16, rows_spec(block, width)),
        ],
        flops=4 * total * width * width,
    )


def input_grad(name, limit, base, parts, mat):
    total, width = base.shape
    block = min(256, total)
    count = len(parts)

    def body(limit, fetches, ins, outs, extra, poll):
        (fetch,) = fetches
        result = ins[0][...]
        for at in range(count):
            fetch.wait(at)
            result = result + nt(ins[1 + at][...], fetch.whole[:, at * width : (at + 1) * width])
        outs[0][...] = result

    return staged_call(
        body,
        name,
        (total // block,),
        limit,
        [(mat, count)],
        [(base, rows_spec(block, width))] + [(p, rows_spec(block, width)) for p in parts],
        [((total, width), F32, rows_spec(block, width))],
        flops=2 * total * width * width * count,
    )[0]


NAMES = (
    "enc_qkv",
    "enc_attn_out",
    "enc_ffn_in",
    "enc_ffn_out",
    "dec_self_qkv",
    "dec_self_out",
    "dec_cross_q",
    "dec_cross_kv",
    "dec_cross_out",
    "dec_ffn_in",
    "dec_ffn_out",
)


def layers(enc_limit, dec_limit, enc_input, dec_input, enc_cot, dec_cot, blocks, hosting, fsdp, gains, adapters):
    gain = [gains[k : k + 1] for k in range(5)]
    enc_down, enc_up, dec_down, dec_up = adapters
    if hosting:
        recorder = Recorder(blocks, fsdp)
        w = dict(zip(recorder.names, recorder.wholes))
    else:
        recorder = None
        w = {name: lax.all_gather(b, "fsdp", axis=0, tiled=True) for name, b in blocks.items()}

    def at(slots, time):
        return {"recorder": recorder, "slots": slots, "time": time} if hosting else {}

    qkv = project("enc_project", enc_limit, enc_input, w["enc_qkv"], 3, **at(3, 13.0))
    e_enc, o_enc, inv_enc = attend(
        "enc_attend", enc_limit, (qkv, 0), (qkv, 8), (qkv, 16), False, **at(2, 53.0)
    )
    unit1, dev1, sq_a = out_norm(
        "enc_out_norm", enc_limit, o_enc, enc_input, gain[0], w["enc_attn_out"], **at(1, 9.0)
    )
    enc_out, unit2, dev2, slope_e, wa_e, ads_e, sq_b = branch(
        "enc_branch", enc_limit, unit1, gain[0], gain[1], w["enc_ffn_in"], w["enc_ffn_out"],
        enc_down, enc_up, **at(4, 38.0),
    )
    sqkv = project("dec_project", dec_limit, dec_input, w["dec_self_qkv"], 3, **at(3, 6.0))
    e_self, o_self, inv_self = attend(
        "dec_attend", dec_limit, (sqkv, 0), (sqkv, 8), (sqkv, 16), True, **at(2, 8.5)
    )
    unit3, dev3, sq_c, cross_q = out_norm(
        "dec_out_norm", dec_limit, o_self, dec_input, gain[2], w["dec_self_out"], w["dec_cross_q"],
        **at(1, 5.3),
    )
    kv = project("cross_project", enc_limit, enc_out, w["dec_cross_kv"], 2, **at(2, 9.5))
    e_cross, o_cross, inv_cross = attend(
        "cross_attend", enc_limit, (cross_q, 0), (kv, 0), (kv, 8), False, **at(2, 16.0)
    )
    unit4, dev4, sq_d = out_norm(
        "cross_out_norm", dec_limit, o_cross, unit3, gain[3], w["dec_cross_out"],
        residual_gain=gain[2], **at(1, 4.6),
    )
    dec_out, unit5, dev5, slope_d, wa_d, ads_d, sq_e = branch(
        "dec_branch", dec_limit, unit4, gain[3], gain[4], w["dec_ffn_in"], w["dec_ffn_out"],
        dec_down, dec_up, **at(4, 11.4),
    )
    if hosting:
        value = recorder.run()
        w = {name: value(mat) for name, mat in w.items()}
        qkv, e_enc, o_enc, inv_enc, unit1, dev1, sq_a = map(
            value, (qkv, e_enc, o_enc, inv_enc, unit1, dev1, sq_a)
        )
        enc_out, unit2, dev2, slope_e, wa_e, ads_e, sq_b = map(
            value, (enc_out, unit2, dev2, slope_e, wa_e, ads_e, sq_b)
        )
        sqkv, e_self, o_self, inv_self, unit3, dev3, sq_c, cross_q = map(
            value, (sqkv, e_self, o_self, inv_self, unit3, dev3, sq_c, cross_q)
        )
        kv, e_cross, o_cross, inv_cross, unit4, dev4, sq_d = map(
            value, (kv, e_cross, o_cross, inv_cross, unit4, dev4, sq_d)
        )
        dec_out, unit5, dev5, slope_d, wa_d, ads_d, sq_e = map(
            value, (dec_out, unit5, dev5, slope_d, wa_d, ads_d, sq_e)
        )
    grad_cross, do_cross, dec_down_grad, dec_up_grad = dec_branch_grad(
        "dec_branch_grad", (enc_limit, dec_limit), dec_cot, (unit5, dev5), gain[4], (unit4, dev4), gain[3],
        slope_d, wa_d, ads_d, w["dec_ffn_out"], w["dec_ffn_in"], w["dec_cross_out"], dec_down, dec_up,
        (sq_a, sq_b, sq_c, sq_d, sq_e),
    )
    dcq, dck, dcv = attend_grad(
        "cross_attend_grad", (cross_q, 0), (kv, 0), (kv, 8), e_cross, o_cross, inv_cross, do_cross
    )
    dz, part, enc_down_grad, enc_up_grad = enc_adapter_grad(
        "enc_adapter_grad", enc_limit, enc_cot, (dck, dcv), w["dec_cross_kv"], (unit2, dev2), gain[1],
        (unit1, dev1), gain[0], wa_e, ads_e, enc_down, enc_up,
    )
    grad_self, do_self = middle_grad(
        "dec_middle_grad", dec_limit, grad_cross, dcq, (unit3, dev3), gain[2], w["dec_cross_q"], w["dec_self_out"]
    )
    dsq, dsk, dsv = attend_grad(
        "dec_attend_grad", (sqkv, 0), (sqkv, 8), (sqkv, 16), e_self, o_self, inv_self, do_self
    )
    dec_grad = input_grad("dec_input_grad", dec_limit, grad_self, [dsq, dsk, dsv], w["dec_self_qkv"])
    grad_one, do_enc = enc_hidden_grad(
        "enc_hidden_grad", enc_limit, dz, part, slope_e, (unit1, dev1), gain[0],
        w["enc_ffn_out"], w["enc_ffn_in"], w["enc_attn_out"],
    )
    deq, dek, dev = attend_grad(
        "enc_attend_grad", (qkv, 0), (qkv, 8), (qkv, 16), e_enc, o_enc, inv_enc, do_enc
    )
    enc_grad = input_grad("enc_input_grad", enc_limit, grad_one, [deq, dek, dev], w["enc_qkv"])
    return (
        (enc_out, dec_out, enc_grad, dec_grad),
        (enc_down_grad, enc_up_grad),
        (dec_down_grad, dec_up_grad),
    )


def shards(fsdp, dp, enc_input, dec_input, enc_cot, dec_cot, *rest):
    mats, (gains, enc_down, enc_up, dec_down, dec_up, enc_lengths, dec_lengths) = rest[:11], rest[11:]
    results, enc_grads, dec_grads = layers(
        enc_lengths, dec_lengths, enc_input, dec_input, enc_cot, dec_cot, dict(zip(NAMES, mats)),
        fsdp == 8 and dp % 2 == 0, fsdp, gains, (enc_down, enc_up, dec_down, dec_up),
    )
    everyone = ("fsdp", "dp")
    dec_down_grad, dec_up_grad = lax.psum(dec_grads, everyone)
    enc_down_grad, enc_up_grad = lax.psum(enc_grads, everyone)
    width = enc_input.shape[1]
    adapter = dec_up.shape[0]
    statistics = dec_up_grad[adapter:]
    rows = jnp.stack([statistics[7, 0]] * 3 + [statistics[7, 1]] * 4)
    rms = jnp.sqrt(jnp.sum(statistics[:7], axis=1) / (rows * width))
    return (
        *results,
        enc_down_grad.astype(F32),
        enc_up_grad.astype(F32),
        dec_down_grad,
        dec_up_grad[:adapter],
        rms,
    )


def solution(mesh):
    by_rows = P(("fsdp", "dp"), None)
    placed = (by_rows,) * 4 + (P("fsdp", None),) * 11 + (P(),) * 5 + (P(("fsdp", "dp")),) * 2
    return jax.shard_map(
        functools.partial(shards, mesh.shape["fsdp"], mesh.shape["dp"]),
        mesh=mesh,
        in_specs=placed,
        out_specs=(by_rows,) * 4 + (P(),) * 5,
        check_vma=False,
    )
```

```python
import functools
import math

import jax
import jax.numpy as jnp
from jax import lax
from jax.experimental import pallas as pl
from jax.experimental.pallas import tpu as pltpu
from jax.sharding import PartitionSpec as P

HEAD = 64
PAIR = 2 * HEAD
EPSILON = 1e-05
F32 = jnp.float32
BF16 = jnp.bfloat16
VMEM_BYTES = 58 * 2**20


def nn(former, latter):
    return jnp.dot(former, latter, preferred_element_type=F32)


def nt(former, latter):
    return lax.dot_general(
        former, latter, (((1,), (1,)), ((), ())), preferred_element_type=F32
    )


def tn(former, latter):
    return lax.dot_general(
        former, latter, (((0,), (0,)), ((), ())), preferred_element_type=F32
    )


def standardize(entries):
    centered = entries - jnp.mean(entries, axis=-1, keepdims=True)
    spread = jnp.mean(centered * centered, axis=-1, keepdims=True)
    inverse = lax.rsqrt(spread + EPSILON)
    return centered * inverse, inverse


def standardize_grad(unit, inverse, scaled):
    return inverse * (
        scaled
        - jnp.mean(scaled, axis=-1, keepdims=True)
        - unit * jnp.mean(scaled * unit, axis=-1, keepdims=True)
    )


class Fetch:
    def __init__(self, source, whole, sems, chunks):
        self.source, self.whole, self.sems, self.chunks = source, whole, sems, chunks

    def copy(self, chunk):
        width = self.whole.shape[1] // self.chunks
        columns = pl.ds(chunk * width, width)
        return pltpu.make_async_copy(
            self.source.at[:, columns], self.whole.at[:, columns], self.sems.at[chunk]
        )

    def start(self):
        for chunk in range(self.chunks):
            self.copy(chunk).start()

    def wait(self, chunk):
        @pl.when(pl.program_id(0) == 0)
        def _():
            self.copy(chunk).wait()

    def wait_all(self):
        for chunk in range(self.chunks):
            self.wait(chunk)


UNIT_US = 5.8
LEAD_US = 5.0


class Place:
    def __init__(self):
        f, z = lax.axis_index("fsdp"), lax.axis_index("dp")
        self.core, self.x, self.y = f % 2, (f // 2) % 2, f // 4
        self.odd, self.high = z % 2, z // 2
        self.own = f
        self.twin = {"fsdp": f + 1 - 2 * self.core}
        self.beside = {"fsdp": f + 2 - 4 * self.x}
        self.above = {"fsdp": f + 4 - 8 * self.y}
        self.partner = {"dp": z + 1 - 2 * self.odd}
        self.distant = {"dp": z + 2 - 4 * self.high}

    def meet(self):
        barrier = pltpu.get_barrier_semaphore()
        all_of_them = (self.twin, self.beside, self.above, self.partner, self.distant)
        for to in all_of_them:
            pl.semaphore_signal(barrier, inc=1, device_id=to, device_id_type=pl.DeviceIdType.MESH)
        pl.semaphore_wait(barrier, len(all_of_them))


class Gather:
    def __init__(self, place, owns, wholes, splits, sends, recvs, locals_):
        self.place, self.owns, self.wholes, self.splits = place, owns, wholes, splits
        self.sends, self.recvs, self.locals = sends, recvs, locals_
        self.units = [(m, part) for m, split in enumerate(splits) for part in range(split)]
        beside, above = place.beside["fsdp"], place.above["fsdp"]
        self.own = place.own
        self.direct = beside + place.odd * (above - beside)
        self.onward = above + place.odd * (beside - above)
        self.far = beside + 4 - 8 * place.y

    def transfer(self, unit, kind):
        m, part = self.units[unit]
        whole, own = self.wholes[m], self.owns[m]
        block = own.shape[0]
        rows = block // self.splits[m]
        owner = (self.own, self.direct, self.direct, self.own, self.direct, self.far, self.onward)[kind]
        there = whole.at[pl.ds(pl.multiple_of(owner * block + part * rows, 16), rows), :]
        here = own.at[pl.ds(part * rows, rows), :] if kind in (0, 3) else there
        to = self.place.twin if kind >= 3 else self.place.partner
        if kind < 2:
            to = {"fsdp": (self.direct, self.onward)[kind]}
        return pltpu.make_async_remote_copy(
            src_ref=here,
            dst_ref=there,
            send_sem=self.sends.at[unit, kind],
            recv_sem=self.recvs.at[unit, kind],
            device_id=to,
            device_id_type=pl.DeviceIdType.MESH,
        )

    def keep(self, m):
        block = self.owns[m].shape[0]
        rows = pl.ds(pl.multiple_of(self.own * block, 16), block)
        return pltpu.make_async_copy(self.owns[m], self.wholes[m].at[rows, :], self.locals.at[m])

    def begin(self):
        for unit in range(len(self.units)):
            self.transfer(unit, 0).start()
        for unit in range(len(self.units)):
            self.transfer(unit, 3).start()
        for m in range(len(self.owns)):
            self.keep(m).start()

    def pass_on(self, unit):
        self.transfer(unit, 0).wait_recv()
        for kind in (1, 2, 4):
            self.transfer(unit, kind).start()

    def share(self, unit):
        self.transfer(unit, 1).wait_recv()
        self.transfer(unit, 5).start()
        self.transfer(unit, 2).wait_recv()
        self.transfer(unit, 6).start()

    def complete(self, m):
        for unit, (of, _) in enumerate(self.units):
            if of == m:
                for kind in (3, 4, 5, 6):
                    self.transfer(unit, kind).wait_recv()
        self.keep(m).wait()

    def finish(self):
        for unit in range(len(self.units)):
            for kind in range(7):
                self.transfer(unit, kind).wait_send()


LEVELS = 5
SHAPES = ((1024, 512), (512, 1024))


class Reduce:
    def __init__(self, place, totals, gives, takes, pieces, wholes, sems, tallies=None):
        self.place, self.totals, self.gives, self.takes = place, totals, gives, takes
        self.pieces, self.wholes, self.tallies = pieces, wholes, tallies
        self.sends, self.recvs, self.locals = sems
        p = place
        along = [(p.core, p.twin), (p.x, p.beside), (p.y, p.above), (p.odd, p.partner), (p.high, p.distant)]
        self.ways = [along, [along[0], along[2], along[1], along[3], along[4]]]

    def range(self, part, level):
        rows = SHAPES[part][0]
        first = 0
        for bit, _ in self.ways[part][:level]:
            rows = rows // 2
            first = first + bit * rows
        return first, rows

    def halves(self, part, level):
        first, rows = self.range(part, level)
        bit = self.ways[part][level][0]
        half = rows // 2
        return pl.multiple_of(first + bit * half, half), pl.multiple_of(first + (1 - bit) * half, half), half

    def slot(self, part, level):
        rows = SHAPES[part][0]
        return pl.ds(rows - (rows >> level), rows >> (level + 1))

    def remote(self, src, dst, part, level, back):
        return pltpu.make_async_remote_copy(
            src_ref=src,
            dst_ref=dst,
            send_sem=self.sends.at[part, level, back],
            recv_sem=self.recvs.at[part, level, back],
            device_id=self.ways[part if part < 2 else 0][level][1],
            device_id_type=pl.DeviceIdType.MESH,
        )

    def down(self, part, level):
        rows = self.slot(part, level)
        return self.remote(self.gives[part].at[rows, :], self.takes[part].at[rows, :], part, level, 0)

    def up(self, part, level):
        first, rows = self.range(part, level + 1)
        rows = pl.ds(pl.multiple_of(first, rows), rows)
        return self.remote(self.wholes[part].at[rows, :], self.wholes[part].at[rows, :], part, level, 1)

    def tally(self, level):
        return self.remote(self.tallies[0].at[level], self.tallies[1].at[level], 2, level, 0)

    def piece(self, part):
        first, rows = self.range(part, LEVELS)
        rows = pl.ds(pl.multiple_of(first, rows), rows)
        return pltpu.make_async_copy(self.pieces[part], self.wholes[part].at[rows, :], self.locals.at[part])

    def tally_out(self):
        return pltpu.make_async_copy(self.tallies[0].at[LEVELS], self.tallies[2], self.locals.at[2])

    def step(self, at):
        for part in range(2):
            if 0 < at <= LEVELS:
                keep, _, half = self.halves(part, at - 1)
                self.down(part, at - 1).wait_recv()
                rows = pl.ds(keep, half)
                taken = self.takes[part][self.slot(part, at - 1), :].astype(F32)
                self.totals[part][rows, :] = self.totals[part][rows, :] + taken
            if at < LEVELS:
                _, give, half = self.halves(part, at)
                self.gives[part][self.slot(part, at), :] = self.totals[part][pl.ds(give, half), :].astype(BF16)
                self.down(part, at).start()
            elif at == LEVELS:
                first, rows = self.range(part, LEVELS)
                last = pl.ds(pl.multiple_of(first, rows), rows)
                self.pieces[part][...] = self.totals[part][last, :].astype(BF16)
                self.piece(part).start()
                self.piece(part).wait()
                self.up(part, LEVELS - 1).start()
            else:
                level = 2 * LEVELS - at
                self.up(part, level).wait_recv()
                if level:
                    self.up(part, level - 1).start()
        if self.tallies and at <= LEVELS:
            if at:
                self.tally(at - 1).wait_recv()
                self.tallies[0][at] = self.tallies[0][at - 1] + self.tallies[1][at - 1]
            if at < LEVELS:
                self.tally(at).start()
            else:
                self.tally_out().start()

    def finish(self):
        for level in range(LEVELS):
            for part in range(2):
                self.down(part, level).wait_send()
                self.up(part, level).wait_send()
            if self.tallies:
                self.tally(level).wait_send()
        if self.tallies:
            self.tally_out().wait()


REDUCE_US = (0.0, 5.0, 9.0, 6.5, 6.0, 6.0, 6.0, 6.0, 6.5, 9.0, 5.0)


ANY = pl.BlockSpec(memory_space=pl.ANY)
SCALAR = pl.BlockSpec(memory_space=pltpu.SMEM)


def rows_spec(rows, width):
    return pl.BlockSpec((rows, width), lambda i: (i, 0))


def whole_spec(shape):
    return pl.BlockSpec(shape, lambda i: (0,) * len(shape))


class Later:
    def __init__(self, shape, dtype):
        self.shape, self.dtype = tuple(shape), jnp.dtype(dtype)
        self.size = math.prod(self.shape)


class Recorder:
    def __init__(self, blocks, fsdp):
        self.names = list(blocks)
        self.owns = list(blocks.values())
        self.wholes = [Later((a.shape[0] * fsdp, a.shape[1]), a.dtype) for a in self.owns]
        self.splits = [4 if a.shape[1] == 3072 else max(1, a.size // 131072) for a in self.owns]
        self.stages = []
        self.sums = {}

    def reduce(self, name, tallied):
        self.sums[name] = [Later(shape, BF16) for shape in SHAPES]
        if tallied:
            self.sums[name].append(Later((8, 1024), F32))
        return self.sums[name]

    def add(self, **stage):
        stage["results"] = [Later(shape, dtype) for shape, dtype, _ in stage["outs"]]
        self.stages.append(stage)
        return stage["results"]

    def schedule(self):
        acts, unit, due = [], 0, LEAD_US
        last_of = {}
        for m, split in enumerate(self.splits):
            for _ in range(split):
                time = UNIT_US * self.owns[m].size / split / 131072
                due += time
                acts.append((due, "pass_on", unit))
                acts.append((due + time + 2.0, "share", unit))
                last_of[m] = unit
                unit += 1
        acts.sort(key=lambda act: act[0])
        clock, plans, started = 0.0, [], []
        for stage in self.stages:
            before, ticks = started, {}
            started = []
            needed = [last_of[self.wholes.index(mat)] for mat in stage["needs"]]
            if needed:
                while any(act[1] in ("pass_on", "share") and act[2] <= max(needed) for act in acts):
                    clock = max(clock, acts[0][0])
                    before.append(acts.pop(0)[1:])
            pace = stage["time"] / stage["grid"][0] / stage["slots"]
            for tick in range(stage["grid"][0] * stage["slots"]):
                while acts and acts[0][0] <= clock:
                    ticks.setdefault(divmod(tick, stage["slots"]), []).append(acts.pop(0)[1:])
                clock += pace
            plans.append((before, ticks))
            if stage["sums"]:
                started = [("step", (stage["sums"], 0))]
                due = clock
                for at, time in enumerate(REDUCE_US):
                    due += time
                    if at:
                        acts.append((due, "step", (stage["sums"], at)))
                acts.sort(key=lambda act: act[0])
        return plans, [act[1:] for act in acts]

    def run(self):
        given = []
        for stage in self.stages:
            for array, spec in stage["ins"]:
                if not isinstance(array, Later) and not any(array is g for g, _ in given):
                    given.append((array, SCALAR if spec is SCALAR else ANY))
        results = self.wholes + [r for stage in self.stages for r in stage["results"]]
        results += [r for sums in self.sums.values() for r in sums]
        plans, left = self.schedule()
        units = sum(self.splits)

        def kernel(*refs):
            refs = list(refs)
            owns = refs[: len(self.owns)]
            of = {}
            for (array, _), ref in zip(given, refs[len(self.owns) :]):
                of[id(array)] = ref
            rest = refs[len(self.owns) + len(given) :]
            for result, ref in zip(results, rest):
                of[id(result)] = ref
            rest = rest[len(results) :]
            place = Place()
            gather = Gather(place, owns, [of[id(w)] for w in self.wholes], self.splits, *rest[:3])
            rest = rest[3:]
            sums = {}
            for name, whole in self.sums.items():
                tallies = [*rest[11:13], of[id(whole[2])]] if len(whole) > 2 else None
                sums[name] = Reduce(
                    place, rest[:2], rest[2:4], rest[4:6], rest[6:8], [of[id(w)] for w in whole[:2]],
                    rest[8:11], tallies,
                )
                rest = rest[13:] if tallies else rest[11:]
            place.meet()
            gather.begin()
            waited = set()

            def act(kind, unit):
                if kind == "step":
                    sums[unit[0]].step(unit[1])
                else:
                    getattr(gather, kind)(unit)

            for stage, (before, ticks) in zip(self.stages, plans):
                for kind, unit in before:
                    act(kind, unit)
                for mat in stage["needs"]:
                    m = self.wholes.index(mat)
                    if m not in waited:
                        waited.add(m)
                        gather.complete(m)
                self.run_stage(stage, ticks, act, of, sums)
            for kind, unit in left:
                act(kind, unit)
            for m in range(len(self.owns)):
                if m not in waited:
                    gather.complete(m)
            gather.finish()
            for each in sums.values():
                each.finish()

        buffers = []
        for whole in self.sums.values():
            for kind, share in ((F32, 1), (BF16, 1), (BF16, 1), (BF16, 32)):
                buffers += [pltpu.VMEM((rows // share, width), kind) for rows, width in SHAPES]
            buffers += [pltpu.SemaphoreType.DMA((3, LEVELS, 2)), pltpu.SemaphoreType.DMA((3, LEVELS, 2))]
            buffers.append(pltpu.SemaphoreType.DMA((3,)))
            if len(whole) > 2:
                buffers.append(pltpu.VMEM((LEVELS + 1, 8, 1024), F32))
                buffers.append(pltpu.VMEM((LEVELS, 8, 1024), F32))

        out = pl.pallas_call(
            kernel,
            in_specs=[ANY] * len(self.owns) + [spec for _, spec in given],
            out_specs=[ANY] * len(results),
            scratch_shapes=[
                pltpu.SemaphoreType.DMA((units, 7)),
                pltpu.SemaphoreType.DMA((units, 7)),
                pltpu.SemaphoreType.DMA((len(self.owns),)),
                *buffers,
            ],
            out_shape=[jax.ShapeDtypeStruct(r.shape, r.dtype) for r in results],
            compiler_params=pltpu.CompilerParams(
                vmem_limit_bytes=VMEM_BYTES, collective_id=1, has_side_effects=True
            ),
            name="everything",
        )(*self.owns, *[array for array, _ in given])
        arrays = {id(result): array for result, array in zip(results, out)}
        return lambda later: arrays[id(later)]

    def run_stage(self, stage, ticks, act, of, sums):
        ins, outs = stage["ins"], stage["outs"]
        piped = [at for at, (_, spec) in enumerate(ins) if spec is not ANY and spec is not SCALAR]
        fixed = {at: of[id(a)] for at, (a, _) in enumerate(ins) if at not in piped}

        def poll(slot):
            for (step, at), todo in ticks.items():
                if at == slot:

                    @pl.when(pl.program_id(0) == step)
                    def _(todo=todo):
                        for kind, unit in todo:
                            act(kind, unit)

        poll.sums = sums.get(stage["sums"])

        def scoped(*scratch):
            if stage["prepare"]:
                stage["prepare"]([fixed.get(at) for at in range(len(ins))], scratch)

            def body(*blocks):
                in_refs = [fixed.get(at) for at in range(len(ins))]
                for at, ref in zip(piped, blocks):
                    in_refs[at] = ref
                stage["body"](in_refs, list(blocks[len(piped) :]), scratch, poll)

            pltpu.emit_pipeline(
                body,
                grid=stage["grid"],
                in_specs=[ins[at][1] for at in piped],
                out_specs=[spec for _, _, spec in outs],
            )(*[of[id(ins[at][0])] for at in piped], *[of[id(r)] for r in stage["results"]])

        pl.run_scoped(scoped, *stage["scratch"])


def launch(
    body, name, grid, ins, outs, scratch, flops, moved, recorder=None, prepare=None, needs=(),
    slots=1, time=1.0, sums=None,
):
    if recorder is not None:
        return recorder.add(
            body=body, grid=grid, ins=ins, outs=outs, scratch=scratch, prepare=prepare, needs=needs,
            slots=slots, time=time, sums=sums,
        )

    def kernel(*refs):
        in_refs, out_refs = list(refs[: len(ins)]), list(refs[len(ins) : len(ins) + len(outs)])
        rest = refs[len(ins) + len(outs) :]
        if prepare:

            @pl.when(pl.program_id(0) == 0)
            def _():
                prepare(in_refs, rest)

        body(in_refs, out_refs, rest, lambda slot: None)

    return pl.pallas_call(
        kernel,
        grid=grid,
        in_specs=[spec for _, spec in ins],
        out_specs=[spec for _, _, spec in outs],
        scratch_shapes=scratch,
        out_shape=[jax.ShapeDtypeStruct(s, d) for s, d, _ in outs],
        compiler_params=pltpu.CompilerParams(vmem_limit_bytes=VMEM_BYTES),
        cost_estimate=pl.CostEstimate(flops=flops, bytes_accessed=moved, transcendentals=0),
        name=name,
    )(*[a for a, _ in ins])


def staged_call(body, name, grid, limit, mats, ins, outs, scratch=(), flops=0, **record):
    holders = []
    for mat, chunks in mats:
        holders.append(pltpu.VMEM(mat.shape, mat.dtype))
        holders.append(pltpu.SemaphoreType.DMA((chunks,)))
    given = [mat for mat, _ in mats]

    def fetches(in_refs, rest):
        return [
            Fetch(in_refs[1 + at], rest[2 * at], rest[2 * at + 1], chunks)
            for at, (_, chunks) in enumerate(mats)
        ]

    def prepare(in_refs, rest):
        for fetch in fetches(in_refs, rest):
            fetch.start()

    def staged(in_refs, out_refs, rest, poll):
        args = (in_refs[0], fetches(in_refs, rest), in_refs[1 + len(given) :], out_refs)
        body(*args, rest[2 * len(mats) :], poll)

    moved = sum(a.size * a.dtype.itemsize for a in given)
    moved += sum(a.size * a.dtype.itemsize for a, _ in ins)
    moved += sum(math.prod(s) * jnp.dtype(d).itemsize for s, d, _ in outs)
    return launch(
        staged,
        name,
        grid,
        [(limit, SCALAR)] + [(mat, ANY) for mat in given] + list(ins),
        outs,
        [*holders, *scratch],
        flops,
        moved,
        prepare=prepare,
        needs=given if record else (),
        **record,
    )


def project(name, limit, rows_in, mat, chunks, **record):
    total, depth = rows_in.shape
    width = mat.shape[1]
    block = min(256, total)
    step = width // chunks

    def body(limit, fetches, ins, outs, extra, poll):
        (fetch,) = fetches
        left = ins[0][...]
        for chunk in range(chunks):
            poll(chunk)
            fetch.wait(chunk)
            columns = slice(chunk * step, (chunk + 1) * step)
            outs[0][:, columns] = nn(left, fetch.whole[:, columns]).astype(BF16)

    return staged_call(
        body,
        name,
        (total // block,),
        limit,
        [(mat, chunks)],
        [(rows_in, rows_spec(block, depth))],
        [((total, width), BF16, rows_spec(block, width))],
        flops=2 * total * depth * width,
        **record,
    )[0]


def attend(name, limit, queries, keys, values, causal, **record):
    q_len, k_len = queries[0].shape[0], keys[0].shape[0]
    pairs = 1024 // PAIR
    step = min(256, q_len)

    def body(ins, outs, extra, poll):
        limit_ref, q_ref, k_ref, v_ref = ins
        e_ref, o_ref, inv_ref = outs
        lanes = lax.broadcasted_iota(jnp.int32, (1, PAIR), 1)
        places = lax.broadcasted_iota(jnp.int32, (k_len, 1), 0)
        bias = jnp.where(places < limit_ref[0], 0.0, -1000000000.0)
        q_two = q_ref[...].astype(F32) * (1.0 / math.sqrt(HEAD))
        k_two = k_ref[...].astype(F32)
        v_two = v_ref[...].astype(F32)
        mixed = []
        for half in range(2):
            poll(half)
            own = (lanes >= HEAD * half) & (lanes < HEAD * (half + 1))
            spare = lanes == HEAD * (1 - half)
            q_own = jnp.where(own, q_two, jnp.where(spare, 1.0, 0.0)).astype(BF16)
            k_own = jnp.where(own, k_two, jnp.where(spare, bias, 0.0)).astype(BF16)
            v_own = jnp.where(own, v_two, jnp.where(spare, 1.0, 0.0)).T.astype(BF16)
            parts = []
            for start in range(0, q_len, step):
                scores = nt(k_own, q_own[start : start + step])
                if causal:
                    shape = (k_len, step)
                    key_at = lax.broadcasted_iota(jnp.int32, shape, 0)
                    query_at = lax.broadcasted_iota(jnp.int32, shape, 1) + start
                    scores = jnp.where(key_at <= query_at, scores, -1000000000.0)
                highest = jnp.max(scores, axis=0, keepdims=True)
                weights = jnp.exp(scores - highest).astype(BF16)
                e_ref[0, :, half * q_len + start : half * q_len + start + step] = weights
                parts.append(nn(v_own, weights))
            out = jnp.concatenate(parts, axis=1) if len(parts) > 1 else parts[0]
            at = HEAD * (1 - half)
            inverse = 1.0 / out[at : at + 1]
            own_rows = out[HEAD * half : HEAD * (half + 1)]
            mixed.append((own_rows * inverse, jnp.broadcast_to(inverse, own_rows.shape)))
        o_ref[...] = jnp.concatenate([mixed[0][0], mixed[1][0]], axis=0).T.astype(BF16)
        inv_ref[...] = jnp.concatenate([mixed[0][1], mixed[1][1]], axis=0).T

    def columns(rows, first):
        return pl.BlockSpec((rows, PAIR), lambda i: (0, first + i))

    return launch(
        body,
        name,
        (pairs,),
        [
            (limit, SCALAR),
            (queries[0], columns(q_len, queries[1])),
            (keys[0], columns(k_len, keys[1])),
            (values[0], columns(k_len, values[1])),
        ],
        [
            (
                (pairs, k_len, 2 * q_len),
                BF16,
                pl.BlockSpec((1, k_len, 2 * q_len), lambda i: (i, 0, 0)),
            ),
            ((q_len, 1024), BF16, columns(q_len, 0)),
            ((q_len, 1024), F32, columns(q_len, 0)),
        ],
        [],
        16 * pairs * q_len * k_len * PAIR,
        4 * pairs * q_len * k_len,
        **record,
    )


def attend_grad(name, queries, keys, values, weights, mixture, inverse, upstream, **record):
    q_len, k_len = queries[0].shape[0], keys[0].shape[0]
    pairs = 1024 // PAIR
    step = min(256, q_len)
    factor = 1.0 / math.sqrt(HEAD)

    def body(ins, outs, extra, poll):
        q_ref, k_ref, v_ref, e_ref, o_ref, inv_ref, do_ref = ins
        dq_ref, dk_ref, dv_ref = outs
        (ds_ref,) = extra
        poll(0)
        lanes = lax.broadcasted_iota(jnp.int32, (1, PAIR), 1)
        first = lanes < HEAD
        scaled = do_ref[...].astype(F32) * inv_ref[...]
        inner = scaled.astype(BF16).astype(F32) * o_ref[...].astype(F32)
        coarse = inner.astype(BF16)
        fine = (inner - coarse.astype(F32)).astype(BF16)
        picks = lax.broadcasted_iota(jnp.int32, (8, PAIR), 1)
        ones = [
            jnp.where(picks < HEAD, 1.0, 0.0).astype(BF16),
            jnp.where(picks < HEAD, 0.0, 1.0).astype(BF16),
        ]
        delta = [(nt(one, coarse) + nt(one, fine))[0:1] for one in ones]
        do_two = jnp.concatenate(
            [jnp.where(first, scaled, 0.0).astype(BF16), jnp.where(first, 0.0, scaled).astype(BF16)],
            axis=0,
        )
        q_all = q_ref[...].astype(F32) * factor
        q_two = jnp.concatenate(
            [jnp.where(first, q_all, 0.0).astype(BF16), jnp.where(first, 0.0, q_all).astype(BF16)],
            axis=0,
        )
        k_flip = k_ref[...].astype(F32).T.astype(BF16)
        v_all = v_ref[...]
        for half in range(2):
            for start in range(0, q_len, step):
                at = half * q_len + start
                probs_grad = nt(v_all, do_two[at : at + step])
                held = e_ref[0, :, at : at + step].astype(F32)
                ds_ref[:, at : at + step] = (
                    held * (probs_grad - delta[half][:, start : start + step])
                ).astype(BF16)
        dv_ref[...] = nn(e_ref[0], do_two).astype(BF16)
        dk_ref[...] = nn(ds_ref[...], q_two).astype(BF16)
        turned = nn(k_flip, ds_ref[...]) * factor
        rows = lax.broadcasted_iota(jnp.int32, (PAIR, 1), 0)
        dq_ref[...] = jnp.where(rows < HEAD, turned[:, :q_len], turned[:, q_len:]).T.astype(BF16)

    def columns(rows, at):
        return pl.BlockSpec((rows, PAIR), lambda i: (0, at + i))

    return launch(
        body,
        name,
        (pairs,),
        [
            (queries[0], columns(q_len, queries[1])),
            (keys[0], columns(k_len, keys[1])),
            (values[0], columns(k_len, values[1])),
            (weights, pl.BlockSpec((1, k_len, 2 * q_len), lambda i: (i, 0, 0))),
            (mixture, columns(q_len, 0)),
            (inverse, columns(q_len, 0)),
            (upstream, columns(q_len, 0)),
        ],
        [
            ((q_len, 1024), BF16, columns(q_len, 0)),
            ((k_len, 1024), BF16, columns(k_len, 0)),
            ((k_len, 1024), BF16, columns(k_len, 0)),
        ],
        [pltpu.VMEM((k_len, 2 * q_len), BF16)],
        32 * pairs * q_len * k_len * PAIR,
        4 * pairs * q_len * k_len,
        **record,
    )


def row_mask(limit, block):
    at = lax.broadcasted_iota(jnp.int32, (block, 1), 0) + pl.program_id(0) * block
    return (at < limit).astype(F32)


def add_squares(ref, row, entries, mask):
    sums = jnp.sum(entries * entries * mask, axis=0, keepdims=True)
    first = pl.program_id(0) == 0

    @pl.when(first)
    def _():
        ref[row : row + 1, :] = sums

    @pl.when(jnp.logical_not(first))
    def _():
        ref[row : row + 1, :] += sums


def spread_lanes(column):
    return jnp.broadcast_to(column, (column.shape[0], 128))


def out_norm(name, limit, mixture, residual, gain, mat, next_mat=None, residual_gain=None, **record):
    total, width = mixture.shape
    block = min(256, total)
    mats = [(mat, 1)] + ([] if next_mat is None else [(next_mat, 1)])

    def body(limit, fetches, ins, outs, extra, poll):
        poll(0)
        o_ref, r_ref, g_ref, rg_ref = ins
        fetches[0].wait_all()
        added = nn(o_ref[...], fetches[0].whole[...])
        base = r_ref[...].astype(F32)
        if residual_gain is not None:
            base = base * rg_ref[...]
        unit, inverse = standardize(base + added)
        outs[0][...] = unit.astype(BF16)
        outs[1][...] = spread_lanes(inverse)
        add_squares(outs[2], 0, added, row_mask(limit[0], block))
        if next_mat is not None:
            fetches[1].wait_all()
            hidden = (unit * g_ref[...]).astype(BF16)
            outs[3][...] = nn(hidden, fetches[1].whole[...]).astype(BF16)

    outs = [
        ((total, width), BF16, rows_spec(block, width)),
        ((total, 128), F32, rows_spec(block, 128)),
        ((8, width), F32, whole_spec((8, width))),
    ]
    if next_mat is not None:
        outs.append(((total, width), BF16, rows_spec(block, width)))
    return staged_call(
        body,
        name,
        (total // block,),
        limit,
        mats,
        [
            (mixture, rows_spec(block, width)),
            (residual, rows_spec(block, width)),
            (gain, whole_spec((1, width))),
            (gain if residual_gain is None else residual_gain, whole_spec((1, width))),
        ],
        outs,
        flops=2 * total * width * width * len(mats),
        **record,
    )


def branch(name, limit, unit, gain, gain_out, w_in, w_back, down_low, up_low, **record):
    total, width = unit.shape
    hidden_units = w_in.shape[1]
    adapter = down_low.shape[1]
    block = min(256, total)
    chunks = 4
    step = hidden_units // chunks

    def body(limit, fetches, ins, outs, extra, poll):
        u_ref, g_ref, go_ref, ad_ref, au_ref = ins
        y_ref, unit_ref, inv_ref, slope_ref, wa_ref, ad_slope_ref, sq_ref = outs
        (act,) = extra
        first, second = fetches
        hidden = u_ref[...].astype(F32) * g_ref[...]
        low = hidden.astype(BF16)
        pre = nn(low, ad_ref[...].astype(BF16))
        gate = jax.nn.sigmoid(pre)
        wa = (pre * gate).astype(BF16)
        wa_ref[...] = wa
        ad_slope_ref[...] = (gate * (1.0 + pre * (1.0 - gate))).astype(BF16)
        adapted = 4.0 * nn(wa, au_ref[...].astype(BF16))
        for chunk in range(chunks):
            poll(chunk)
            first.wait(chunk)
            columns = slice(chunk * step, (chunk + 1) * step)
            fp = nn(low, first.whole[:, columns])
            cdf = 0.5 * (1.0 + lax.erf(fp * (1.0 / math.sqrt(2.0))))
            act[:, columns] = (fp * cdf).astype(BF16)
            bell = jnp.exp(-0.5 * fp * fp) * (1.0 / math.sqrt(2.0 * math.pi))
            slope_ref[:, columns] = (cdf + fp * bell).astype(BF16)
        second.wait_all()
        added = nn(act[...], second.whole[...]) + adapted
        out_unit, inverse = standardize(hidden + added)
        result = out_unit * go_ref[...]
        y_ref[...] = result.astype(BF16)
        unit_ref[...] = out_unit.astype(BF16)
        inv_ref[...] = spread_lanes(inverse)
        mask = row_mask(limit[0], block)
        add_squares(sq_ref, 0, added, mask)
        add_squares(sq_ref, 1, result, mask)

    return staged_call(
        body,
        name,
        (total // block,),
        limit,
        [(w_in, chunks), (w_back, 1)],
        [
            (unit, rows_spec(block, width)),
            (gain, whole_spec((1, width))),
            (gain_out, whole_spec((1, width))),
            (down_low, whole_spec(down_low.shape)),
            (up_low, whole_spec(up_low.shape)),
        ],
        [
            ((total, width), BF16, rows_spec(block, width)),
            ((total, width), BF16, rows_spec(block, width)),
            ((total, 128), F32, rows_spec(block, 128)),
            ((total, hidden_units), BF16, rows_spec(block, hidden_units)),
            ((total, adapter), BF16, rows_spec(block, adapter)),
            ((total, adapter), BF16, rows_spec(block, adapter)),
            ((8, width), F32, whole_spec((8, width))),
        ],
        scratch=[pltpu.VMEM((block, hidden_units), BF16)],
        flops=4 * total * width * (hidden_units + adapter),
        **record,
    )


def adapter_grad(upstream, refs):
    (uo_ref, io_ref, go_ref, ui_ref, gi_ref, wa_ref, as_ref, ad_ref, au_ref) = refs
    grad_two = standardize_grad(uo_ref[...].astype(F32), io_ref[:, 0:1], upstream * go_ref[...])
    dvd = (4.0 * grad_two).astype(BF16)
    low = (ui_ref[...].astype(F32) * gi_ref[...]).astype(BF16)
    du = (nt(dvd, au_ref[...].astype(BF16)) * as_ref[...].astype(F32)).astype(BF16)
    total = grad_two + nt(du, ad_ref[...].astype(BF16))
    return grad_two.astype(BF16), total, tn(low, du), tn(wa_ref[...], dvd)


def hidden_grad(dz, total, fetches, refs, dfp, chunks, poll=lambda slot: None):
    slope_ref, ui_ref, ii_ref, gi_ref = refs
    back, within, last = fetches
    step = dfp.shape[1] // chunks
    back.wait_all()
    poll(0)
    for chunk in range(chunks):
        columns = slice(chunk * step, (chunk + 1) * step)
        act_grad = nt(dz, back.whole[columns, :])
        dfp[:, columns] = (act_grad * slope_ref[:, columns].astype(F32)).astype(BF16)
    within.wait_all()
    poll(1)
    total = total + nt(dfp[...], within.whole[...])
    grad_one = standardize_grad(ui_ref[...].astype(F32), ii_ref[:, 0:1], total * gi_ref[...])
    last.wait_all()
    return grad_one, nt(grad_one.astype(BF16), last.whole[...]).astype(BF16)


def dec_branch_grad(
    name, limits, cot, saved_out, gain_out, saved_in, gain_in, slope, wa, ad_slope,
    w_back, w_in, w_out, down_low, up_low, squares, **record,
):
    total, width = cot.shape
    hidden_units = w_in.shape[1]
    adapter = down_low.shape[1]
    whole = [
        cot, saved_out[0], saved_out[1], gain_out, saved_in[0], gain_in, wa, ad_slope, down_low,
        up_low, slope, saved_in[1], *squares,
    ]

    def body(limit, fetches, ins, outs, extra, poll):
        grad_ref, mix_ref = outs[:2]
        if record:
            (down_ref, up_ref), tally_ref = poll.sums.totals, poll.sums.tallies[0].at[0]
        else:
            down_ref, up_ref, tally_ref = outs[2], outs[3].at[:adapter], outs[3].at[adapter:]
        (other,), cot_ref, slope_ref, ii_ref = ins[:1], ins[1], ins[11], ins[12]
        dz, part, down_ref[...], up_ref[...] = adapter_grad(cot_ref[...].astype(F32), ins[2:11])
        sums = [ref[row : row + 1, :] for ref, rows in zip(ins[13:], (1, 2, 1, 1, 2)) for row in range(rows)]
        lanes = lax.broadcasted_iota(jnp.int32, (1, width), 1)
        counts = jnp.where(lanes == 0, limit[0], jnp.where(lanes == 1, other[0], 0)).astype(F32)
        tally_ref[...] = jnp.concatenate([*sums, counts], axis=0)
        grad_ref[...], mix_ref[...] = hidden_grad(
            dz, part, fetches, (slope_ref, ins[5], ii_ref, ins[6]), extra[0], 4
        )

    return staged_call(
        body,
        name,
        (1,),
        limits[0],
        [(w_back, 1), (w_in, 1), (w_out, 1)],
        [(limits[1], SCALAR)] + [(a, whole_spec(a.shape)) for a in whole],
        [
            (cot.shape, F32, whole_spec(cot.shape)),
            (cot.shape, BF16, whole_spec(cot.shape)),
        ]
        + [
            (shape, F32, whole_spec(shape))
            for shape in (() if record else (down_low.shape, (adapter + 8, width)))
        ],
        scratch=[pltpu.VMEM((total, hidden_units), BF16)],
        flops=4 * total * width * (hidden_units + 2 * adapter),
        **record,
    )


def enc_adapter_grad(
    name, limit, cot, cross, cross_mat, saved_out, gain_out, saved_in, gain_in, wa, ad_slope,
    down_low, up_low, **record,
):
    total, width = cot.shape
    adapter = down_low.shape[1]
    block = min(256, total)
    rows = rows_spec(block, width)

    def body(limit, fetches, ins, outs, extra, poll):
        poll(0)
        dz_ref, part_ref = outs[:2]
        down_sum, up_sum = poll.sums.totals if record else extra
        fetches[0].wait_all()
        upstream = ins[0][...].astype(F32)
        for at in range(2):
            upstream = upstream + nt(ins[1 + at][...], fetches[0].whole[:, at * width : (at + 1) * width])
        dz_ref[...], part_ref[...], down_part, up_part = adapter_grad(upstream, ins[3:])
        at = pl.program_id(0)

        @pl.when(at == 0)
        def _():
            up_sum[...] = up_part
            down_sum[...] = down_part

        @pl.when(at > 0)
        def _():
            up_sum[...] += up_part
            down_sum[...] += down_part

        if not record:

            @pl.when(at == total // block - 1)
            def _():
                outs[2][...] = down_sum[...].astype(BF16)
                outs[3][...] = up_sum[...].astype(BF16)

    return staged_call(
        body,
        name,
        (total // block,),
        limit,
        [(cross_mat, 1)],
        [
            (cot, rows),
            (cross[0], rows),
            (cross[1], rows),
            (saved_out[0], rows),
            (saved_out[1], rows_spec(block, 128)),
            (gain_out, whole_spec((1, width))),
            (saved_in[0], rows),
            (gain_in, whole_spec((1, width))),
            (wa, rows_spec(block, adapter)),
            (ad_slope, rows_spec(block, adapter)),
            (down_low, whole_spec(down_low.shape)),
            (up_low, whole_spec(up_low.shape)),
        ],
        [
            ((total, width), BF16, rows),
            ((total, width), F32, rows),
        ]
        + [(a.shape, BF16, whole_spec(a.shape)) for a in (() if record else (down_low, up_low))],
        scratch=[pltpu.VMEM(a.shape, F32) for a in (() if record else (down_low, up_low))],
        flops=4 * total * width * (width + 2 * adapter),
        **record,
    )


def enc_hidden_grad(name, limit, dz, part, slope, saved_in, gain_in, w_back, w_in, w_out, **record):
    total, width = dz.shape
    hidden_units = w_in.shape[1]
    block = min(256, total)
    rows = rows_spec(block, width)

    def body(limit, fetches, ins, outs, extra, poll):
        outs[0][...], outs[1][...] = hidden_grad(
            ins[0][...], ins[1][...], fetches, ins[2:], extra[0], 4, poll
        )

    return staged_call(
        body,
        name,
        (total // block,),
        limit,
        [(w_back, 1), (w_in, 1), (w_out, 1)],
        [
            (dz, rows),
            (part, rows),
            (slope, rows_spec(block, hidden_units)),
            (saved_in[0], rows),
            (saved_in[1], rows_spec(block, 128)),
            (gain_in, whole_spec((1, width))),
        ],
        [((total, width), F32, rows), ((total, width), BF16, rows)],
        scratch=[pltpu.VMEM((block, hidden_units), BF16)],
        flops=4 * total * width * hidden_units,
        **record,
    )


def middle_grad(name, limit, grad_cross, dq, saved, gain, w_cq, w_so, **record):
    total, width = dq.shape
    block = min(256, total)
    unit, inv = saved

    def body(limit, fetches, ins, outs, extra, poll):
        poll(0)
        gc_ref, dq_ref, u_ref, i_ref, g_ref = ins
        fetches[0].wait_all()
        hidden_grad = gc_ref[...] + nt(dq_ref[...], fetches[0].whole[...])
        grad_self = standardize_grad(
            u_ref[...].astype(F32), i_ref[:, 0:1], hidden_grad * g_ref[...]
        )
        outs[0][...] = grad_self
        fetches[1].wait_all()
        outs[1][...] = nt(grad_self.astype(BF16), fetches[1].whole[...]).astype(BF16)

    return staged_call(
        body,
        name,
        (total // block,),
        limit,
        [(w_cq, 1), (w_so, 1)],
        [
            (grad_cross, rows_spec(block, width)),
            (dq, rows_spec(block, width)),
            (unit, rows_spec(block, width)),
            (inv, rows_spec(block, 128)),
            (gain, whole_spec((1, width))),
        ],
        [
            ((total, width), F32, rows_spec(block, width)),
            ((total, width), BF16, rows_spec(block, width)),
        ],
        flops=4 * total * width * width,
        **record,
    )


def input_grad(name, limit, base, parts, mat, narrow=(), tally=None):
    total, width = base.shape
    block = min(256, total)
    steps = total // block
    count = len(parts)

    def body(limit, fetches, ins, outs, extra, poll):
        (fetch,) = fetches
        result = ins[0][...]
        for at in range(count):
            fetch.wait(at)
            result = result + nt(ins[1 + at][...], fetch.whole[:, at * width : (at + 1) * width])
        outs[0][...] = result
        for at in range(len(narrow)):
            outs[1 + at][...] = ins[1 + count + at][...].astype(F32)
        if tally is not None:
            rows = ins[-1][...]
            at = lax.broadcasted_iota(jnp.int32, (8, 1), 0)
            numbers = jnp.where(at < 3, rows[7:8, 0:1], rows[7:8, 1:2])
            outs[-1][...] = spread_lanes(
                jnp.sqrt(jnp.sum(rows, axis=1, keepdims=True) / (numbers * width))
            )

    slices = [(a, rows_spec(a.shape[0] // steps, a.shape[1])) for a in narrow]
    tallies = [] if tally is None else [(tally, whole_spec(tally.shape))]
    return staged_call(
        body,
        name,
        (steps,),
        limit,
        [(mat, count)],
        [(base, rows_spec(block, width))] + [(p, rows_spec(block, width)) for p in parts] + slices + tallies,
        [((total, width), F32, rows_spec(block, width))]
        + [(a.shape, F32, spec) for a, spec in slices]
        + [((8, 128), F32, whole_spec((8, 128))) for _ in tallies],
        flops=2 * total * width * width * count,
    )


NAMES = (
    "enc_qkv",
    "enc_attn_out",
    "enc_ffn_in",
    "enc_ffn_out",
    "dec_self_qkv",
    "dec_self_out",
    "dec_cross_q",
    "dec_cross_kv",
    "dec_cross_out",
    "dec_ffn_in",
    "dec_ffn_out",
)


def layers(enc_limit, dec_limit, enc_input, dec_input, enc_cot, dec_cot, blocks, hosting, fsdp, gains, adapters):
    gain = [gains[k : k + 1] for k in range(5)]
    enc_down, enc_up, dec_down, dec_up = adapters
    if hosting:
        recorder = Recorder(blocks, fsdp)
        w = dict(zip(recorder.names, recorder.wholes))
    else:
        recorder = None
        w = {name: lax.all_gather(b, "fsdp", axis=0, tiled=True) for name, b in blocks.items()}

    def at(slots, time, sums=None):
        if not hosting:
            return {}
        return {"recorder": recorder, "slots": slots, "time": time, "sums": sums}

    qkv = project("enc_project", enc_limit, enc_input, w["enc_qkv"], 3, **at(3, 13.0))
    e_enc, o_enc, inv_enc = attend(
        "enc_attend", enc_limit, (qkv, 0), (qkv, 8), (qkv, 16), False, **at(2, 53.0)
    )
    unit1, dev1, sq_a = out_norm(
        "enc_out_norm", enc_limit, o_enc, enc_input, gain[0], w["enc_attn_out"], **at(1, 9.0)
    )
    enc_out, unit2, dev2, slope_e, wa_e, ads_e, sq_b = branch(
        "enc_branch", enc_limit, unit1, gain[0], gain[1], w["enc_ffn_in"], w["enc_ffn_out"],
        enc_down, enc_up, **at(4, 38.0),
    )
    sqkv = project("dec_project", dec_limit, dec_input, w["dec_self_qkv"], 3, **at(3, 6.0))
    e_self, o_self, inv_self = attend(
        "dec_attend", dec_limit, (sqkv, 0), (sqkv, 8), (sqkv, 16), True, **at(2, 8.5)
    )
    unit3, dev3, sq_c, cross_q = out_norm(
        "dec_out_norm", dec_limit, o_self, dec_input, gain[2], w["dec_self_out"], w["dec_cross_q"],
        **at(1, 5.3),
    )
    kv = project("cross_project", enc_limit, enc_out, w["dec_cross_kv"], 2, **at(2, 9.5))
    e_cross, o_cross, inv_cross = attend(
        "cross_attend", enc_limit, (cross_q, 0), (kv, 0), (kv, 8), False, **at(2, 16.0)
    )
    unit4, dev4, sq_d = out_norm(
        "cross_out_norm", dec_limit, o_cross, unit3, gain[3], w["dec_cross_out"],
        residual_gain=gain[2], **at(1, 4.6),
    )
    dec_out, unit5, dev5, slope_d, wa_d, ads_d, sq_e = branch(
        "dec_branch", dec_limit, unit4, gain[3], gain[4], w["dec_ffn_in"], w["dec_ffn_out"],
        dec_down, dec_up, **at(4, 11.4),
    )
    dec_sums = recorder.reduce("dec", True) if hosting else []
    grad_cross, do_cross, *dec_grads = dec_branch_grad(
        "dec_branch_grad", (enc_limit, dec_limit), dec_cot, (unit5, dev5), gain[4], (unit4, dev4), gain[3],
        slope_d, wa_d, ads_d, w["dec_ffn_out"], w["dec_ffn_in"], w["dec_cross_out"], dec_down, dec_up,
        (sq_a, sq_b, sq_c, sq_d, sq_e), **at(1, 15.0, "dec"),
    )
    dcq, dck, dcv = attend_grad(
        "cross_attend_grad", (cross_q, 0), (kv, 0), (kv, 8), e_cross, o_cross, inv_cross, do_cross,
        **at(1, 13.0),
    )
    enc_sums = recorder.reduce("enc", False) if hosting else []
    dz, part, *enc_grads = enc_adapter_grad(
        "enc_adapter_grad", enc_limit, enc_cot, (dck, dcv), w["dec_cross_kv"], (unit2, dev2), gain[1],
        (unit1, dev1), gain[0], wa_e, ads_e, enc_down, enc_up, **at(1, 20.0, "enc"),
    )
    grad_one, do_enc = enc_hidden_grad(
        "enc_hidden_grad", enc_limit, dz, part, slope_e, (unit1, dev1), gain[0],
        w["enc_ffn_out"], w["enc_ffn_in"], w["enc_attn_out"], **at(2, 31.0),
    )
    deq, dek, dev = attend_grad(
        "enc_attend_grad", (qkv, 0), (qkv, 8), (qkv, 16), e_enc, o_enc, inv_enc, do_enc, **at(1, 39.0)
    )
    grad_self, do_self = middle_grad(
        "dec_middle_grad", dec_limit, grad_cross, dcq, (unit3, dev3), gain[2], w["dec_cross_q"],
        w["dec_self_out"], **at(1, 6.0),
    )
    dsq, dsk, dsv = attend_grad(
        "dec_attend_grad", (sqkv, 0), (sqkv, 8), (sqkv, 16), e_self, o_self, inv_self, do_self,
        **at(1, 8.0),
    )
    if hosting:
        value = recorder.run()
        w = {name: value(mat) for name, mat in w.items()}
        enc_out, dec_out, grad_one, grad_self = map(value, (enc_out, dec_out, grad_one, grad_self))
        deq, dek, dev, dsq, dsk, dsv = map(value, (deq, dek, dev, dsq, dsk, dsv))
        *dec_grads, tally = map(value, dec_sums)
        enc_grads = [value(a) for a in enc_sums]
    else:
        everyone = ("fsdp", "dp")
        down, up = lax.psum(dec_grads, everyone)
        dec_grads, tally = [down, up[: dec_up.shape[0]]], up[dec_up.shape[0] :]
        enc_grads = lax.psum(enc_grads, everyone)
    dec_grad, *dec_grads = input_grad(
        "dec_input_grad", dec_limit, grad_self, [dsq, dsk, dsv], w["dec_self_qkv"], dec_grads
    )
    enc_grad, *enc_grads, rms = input_grad(
        "enc_input_grad", enc_limit, grad_one, [deq, dek, dev], w["enc_qkv"], enc_grads, tally
    )
    return enc_out, dec_out, enc_grad, dec_grad, *enc_grads, *dec_grads, rms[:7, 0]


def shards(fsdp, dp, enc_input, dec_input, enc_cot, dec_cot, *rest):
    mats, (gains, enc_down, enc_up, dec_down, dec_up, enc_lengths, dec_lengths) = rest[:11], rest[11:]
    return layers(
        enc_lengths, dec_lengths, enc_input, dec_input, enc_cot, dec_cot, dict(zip(NAMES, mats)),
        fsdp == 8 and dp == 4, fsdp, gains, (enc_down, enc_up, dec_down, dec_up),
    )


def solution(mesh):
    by_rows = P(("fsdp", "dp"), None)
    placed = (by_rows,) * 4 + (P("fsdp", None),) * 11 + (P(),) * 5 + (P(("fsdp", "dp")),) * 2
    return jax.shard_map(
        functools.partial(shards, mesh.shape["fsdp"], mesh.shape["dp"]),
        mesh=mesh,
        in_specs=placed,
        out_specs=(by_rows,) * 4 + (P(),) * 5,
        check_vma=False,
    )
```

```python
import functools
import math

import jax
import jax.numpy as jnp
from jax import lax
from jax.experimental import pallas as pl
from jax.experimental.pallas import tpu as pltpu
from jax.sharding import PartitionSpec as P

HEAD = 64
PAIR = 2 * HEAD
EPSILON = 1e-05
F32 = jnp.float32
BF16 = jnp.bfloat16
VMEM_BYTES = 58 * 2**20


def nn(former, latter):
    return jnp.dot(former, latter, preferred_element_type=F32)


def nt(former, latter):
    return lax.dot_general(
        former, latter, (((1,), (1,)), ((), ())), preferred_element_type=F32
    )


def tn(former, latter):
    return lax.dot_general(
        former, latter, (((0,), (0,)), ((), ())), preferred_element_type=F32
    )


def standardize(entries):
    centered = entries - jnp.mean(entries, axis=-1, keepdims=True)
    spread = jnp.mean(centered * centered, axis=-1, keepdims=True)
    inverse = lax.rsqrt(spread + EPSILON)
    return centered * inverse, inverse


def standardize_grad(unit, inverse, scaled):
    return inverse * (
        scaled
        - jnp.mean(scaled, axis=-1, keepdims=True)
        - unit * jnp.mean(scaled * unit, axis=-1, keepdims=True)
    )


class Fetch:
    def __init__(self, source, whole, sems, chunks, first=0):
        self.source, self.whole, self.sems, self.chunks = source, whole, sems, chunks
        self.first = first

    def copy(self, chunk):
        width = self.whole.shape[1] // self.chunks
        return pltpu.make_async_copy(
            self.source.at[:, pl.ds(self.first + chunk * width, width)],
            self.whole.at[:, pl.ds(chunk * width, width)],
            self.sems.at[chunk],
        )

    def start(self):
        for chunk in range(self.chunks):
            self.copy(chunk).start()

    def wait(self, chunk):
        @pl.when(pl.program_id(0) == 0)
        def _():
            self.copy(chunk).wait()

    def wait_all(self):
        for chunk in range(self.chunks):
            self.wait(chunk)


UNIT_US = 5.8
LEAD_US = 5.0


class Place:
    def __init__(self):
        f, z = lax.axis_index("fsdp"), lax.axis_index("dp")
        self.core, self.x, self.y = f % 2, (f // 2) % 2, f // 4
        self.odd, self.high = z % 2, z // 2
        self.own = f
        self.twin = {"fsdp": f + 1 - 2 * self.core}
        self.beside = {"fsdp": f + 2 - 4 * self.x}
        self.above = {"fsdp": f + 4 - 8 * self.y}
        self.partner = {"dp": z + 1 - 2 * self.odd}
        self.distant = {"dp": z + 2 - 4 * self.high}

    def meet(self):
        barrier = pltpu.get_barrier_semaphore()
        all_of_them = (self.twin, self.beside, self.above, self.partner, self.distant)
        for to in all_of_them:
            pl.semaphore_signal(barrier, inc=1, device_id=to, device_id_type=pl.DeviceIdType.MESH)
        pl.semaphore_wait(barrier, len(all_of_them))


class Gather:
    def __init__(self, place, owns, wholes, splits, sends, recvs, locals_):
        self.place, self.owns, self.wholes, self.splits = place, owns, wholes, splits
        self.sends, self.recvs, self.locals = sends, recvs, locals_
        self.units = [(m, part) for m, split in enumerate(splits) for part in range(split)]
        beside, above = place.beside["fsdp"], place.above["fsdp"]
        self.own = place.own
        self.direct = beside + place.odd * (above - beside)
        self.onward = above + place.odd * (beside - above)
        self.far = beside + 4 - 8 * place.y

    def transfer(self, unit, kind):
        m, part = self.units[unit]
        whole, own = self.wholes[m], self.owns[m]
        block, width = own.shape
        by_columns = width == 3072
        rows = block if by_columns else block // self.splits[m]
        wide = width // self.splits[m] if by_columns else width
        first_row, columns = (0, pl.ds(part * wide, wide)) if by_columns else (part * rows, pl.ds(0, wide))
        owner = (self.own, self.direct, self.direct, self.own, self.direct, self.far, self.onward)[kind]
        there = whole.at[pl.ds(pl.multiple_of(owner * block + first_row, 16), rows), columns]
        here = own.at[pl.ds(first_row, rows), columns] if kind in (0, 3) else there
        to = self.place.twin if kind >= 3 else self.place.partner
        if kind < 2:
            to = {"fsdp": (self.direct, self.onward)[kind]}
        return pltpu.make_async_remote_copy(
            src_ref=here,
            dst_ref=there,
            send_sem=self.sends.at[unit, kind],
            recv_sem=self.recvs.at[unit, kind],
            device_id=to,
            device_id_type=pl.DeviceIdType.MESH,
        )

    def keep(self, m):
        block = self.owns[m].shape[0]
        rows = pl.ds(pl.multiple_of(self.own * block, 16), block)
        return pltpu.make_async_copy(self.owns[m], self.wholes[m].at[rows, :], self.locals.at[m])

    def begin(self):
        for unit in range(len(self.units)):
            self.transfer(unit, 0).start()
        for unit in range(len(self.units)):
            self.transfer(unit, 3).start()
        for m in range(len(self.owns)):
            self.keep(m).start()

    def pass_on(self, unit):
        self.transfer(unit, 0).wait_recv()
        for kind in (1, 2, 4):
            self.transfer(unit, kind).start()

    def share(self, unit):
        self.transfer(unit, 1).wait_recv()
        self.transfer(unit, 5).start()
        self.transfer(unit, 2).wait_recv()
        self.transfer(unit, 6).start()

    def complete(self, m, part, first):
        for kind in (3, 4, 5, 6):
            self.transfer(self.units.index((m, part)), kind).wait_recv()
        if first:
            self.keep(m).wait()

    def finish(self):
        for unit in range(len(self.units)):
            for kind in range(7):
                self.transfer(unit, kind).wait_send()


LEVELS = 5
SHAPES = ((1024, 512), (512, 1024))


class Reduce:
    def __init__(self, place, totals, gives, takes, pieces, wholes, sems, tallies=None):
        self.place, self.totals, self.gives, self.takes = place, totals, gives, takes
        self.pieces, self.wholes, self.tallies = pieces, wholes, tallies
        self.sends, self.recvs, self.locals = sems
        p = place
        along = [(p.core, p.twin), (p.x, p.beside), (p.y, p.above), (p.odd, p.partner), (p.high, p.distant)]
        self.ways = [along, [along[0], along[2], along[1], along[3], along[4]]]

    def range(self, part, level):
        rows = SHAPES[part][0]
        first = 0
        for bit, _ in self.ways[part][:level]:
            rows = rows // 2
            first = first + bit * rows
        return first, rows

    def halves(self, part, level):
        first, rows = self.range(part, level)
        bit = self.ways[part][level][0]
        half = rows // 2
        return pl.multiple_of(first + bit * half, half), pl.multiple_of(first + (1 - bit) * half, half), half

    def slot(self, part, level):
        rows = SHAPES[part][0]
        return pl.ds(rows - (rows >> level), rows >> (level + 1))

    def remote(self, src, dst, part, level, back):
        return pltpu.make_async_remote_copy(
            src_ref=src,
            dst_ref=dst,
            send_sem=self.sends.at[part, level, back],
            recv_sem=self.recvs.at[part, level, back],
            device_id=self.ways[part if part < 2 else 0][level][1],
            device_id_type=pl.DeviceIdType.MESH,
        )

    def down(self, part, level):
        rows = self.slot(part, level)
        return self.remote(self.gives[part].at[rows, :], self.takes[part].at[rows, :], part, level, 0)

    def up(self, part, level):
        first, rows = self.range(part, level + 1)
        rows = pl.ds(pl.multiple_of(first, rows), rows)
        return self.remote(self.wholes[part].at[rows, :], self.wholes[part].at[rows, :], part, level, 1)

    def tally(self, level):
        return self.remote(self.tallies[0].at[level], self.tallies[1].at[level], 2, level, 0)

    def piece(self, part):
        first, rows = self.range(part, LEVELS)
        rows = pl.ds(pl.multiple_of(first, rows), rows)
        return pltpu.make_async_copy(self.pieces[part], self.wholes[part].at[rows, :], self.locals.at[part])

    def tally_out(self):
        return pltpu.make_async_copy(self.tallies[0].at[LEVELS], self.tallies[2], self.locals.at[2])

    def step(self, at):
        for part in range(2):
            if 0 < at <= LEVELS:
                keep, _, half = self.halves(part, at - 1)
                self.down(part, at - 1).wait_recv()
                rows = pl.ds(keep, half)
                taken = self.takes[part][self.slot(part, at - 1), :].astype(F32)
                self.totals[part][rows, :] = self.totals[part][rows, :] + taken
            if at < LEVELS:
                _, give, half = self.halves(part, at)
                self.gives[part][self.slot(part, at), :] = self.totals[part][pl.ds(give, half), :].astype(BF16)
                self.down(part, at).start()
            elif at == LEVELS:
                first, rows = self.range(part, LEVELS)
                last = pl.ds(pl.multiple_of(first, rows), rows)
                self.pieces[part][...] = self.totals[part][last, :].astype(BF16)
                self.piece(part).start()
                self.piece(part).wait()
                self.up(part, LEVELS - 1).start()
            else:
                level = 2 * LEVELS - at
                self.up(part, level).wait_recv()
                if level:
                    self.up(part, level - 1).start()
        if self.tallies and at <= LEVELS:
            if at:
                self.tally(at - 1).wait_recv()
                self.tallies[0][at] = self.tallies[0][at - 1] + self.tallies[1][at - 1]
            if at < LEVELS:
                self.tally(at).start()
            else:
                self.tally_out().start()

    def finish(self):
        for level in range(LEVELS):
            for part in range(2):
                self.down(part, level).wait_send()
                self.up(part, level).wait_send()
            if self.tallies:
                self.tally(level).wait_send()
        if self.tallies:
            self.tally_out().wait()


REDUCE_US = (0.0, 5.0, 9.0, 6.5, 6.0, 6.0, 6.0, 6.0, 6.5, 9.0, 5.0)


ANY = pl.BlockSpec(memory_space=pl.ANY)
SCALAR = pl.BlockSpec(memory_space=pltpu.SMEM)


def rows_spec(rows, width):
    return pl.BlockSpec((rows, width), lambda i: (i, 0))


def whole_spec(shape):
    return pl.BlockSpec(shape, lambda i: (0,) * len(shape))


class Later:
    def __init__(self, shape, dtype):
        self.shape, self.dtype = tuple(shape), jnp.dtype(dtype)
        self.size = math.prod(self.shape)


HELD = {"within": (1024, 4096), "back": (4096, 1024)}


class Recorder:
    def __init__(self, blocks, fsdp):
        self.names = list(blocks)
        self.owns = list(blocks.values())
        self.wholes = [Later((a.shape[0] * fsdp, a.shape[1]), a.dtype) for a in self.owns]
        self.splits = [max(1, a.size // 131072) for a in self.owns]
        self.stages = []
        self.sums = {}

    def reduce(self, name, tallied):
        self.sums[name] = [Later(shape, BF16) for shape in SHAPES]
        if tallied:
            self.sums[name].append(Later((8, 1024), F32))
        return self.sums[name]

    def add(self, **stage):
        stage["results"] = [Later(shape, dtype) for shape, dtype, _ in stage["outs"]]
        self.stages.append(stage)
        return stage["results"]

    def schedule(self):
        acts, unit, due = [], 0, LEAD_US
        last_of, come = {}, {}
        for m, split in enumerate(self.splits):
            for part in range(split):
                time = UNIT_US * self.owns[m].size / split / 131072
                due += time
                acts.append((due, "pass_on", unit))
                acts.append((due + time + 2.0, "share", unit))
                last_of[m, part] = unit
                come[m] = due + time + 6.0
                unit += 1
        acts.sort(key=lambda act: act[0])
        clock, plans, started = 0.0, [], []
        for slot in HELD:
            users = [stage for stage in self.stages if slot in stage["held"]]
            if users:
                mat = users[0]["held"][slot]
                acts.append((come[self.wholes.index(mat)], "fetch", (slot, mat)))
        acts.sort(key=lambda act: act[0])
        for index, stage in enumerate(self.stages):
            before, ticks = started, {}
            started = []
            needed = [last_of[m, part] for m, part in self.parts_of(stage)]
            if needed:
                while any(act[1] in ("pass_on", "share") and act[2] <= max(needed) for act in acts):
                    clock = max(clock, acts[0][0])
                    before.append(acts.pop(0)[1:])
            while any(act[1] == "fetch" and act[2][1] is stage["held"].get(act[2][0]) for act in acts):
                clock = max(clock, acts[0][0])
                before.append(acts.pop(0)[1:])
            pace = stage["time"] / stage["grid"][0] / stage["slots"]
            for tick in range(stage["grid"][0] * stage["slots"]):
                while acts and acts[0][0] <= clock:
                    ticks.setdefault(divmod(tick, stage["slots"]), []).append(acts.pop(0)[1:])
                clock += pace
            plans.append((before, ticks))
            for slot in stage["held"]:
                after = [at for at in range(index + 1, len(self.stages)) if slot in self.stages[at]["held"]]
                if after and self.stages[after[0]]["held"][slot] is not stage["held"][slot]:
                    mat = self.stages[after[0]]["held"][slot]
                    acts.append((max(clock, come[self.wholes.index(mat)]), "fetch", (slot, mat)))
                    acts.sort(key=lambda act: act[0])
            if stage["sums"]:
                started = [("step", (stage["sums"], 0))]
                due = clock
                for at, time in enumerate(REDUCE_US):
                    due += time
                    if at:
                        acts.append((due, "step", (stage["sums"], at)))
                acts.sort(key=lambda act: act[0])
        return self.completed(plans, [act[1:] for act in acts])

    def completed(self, plans, left):
        waited = []

        def waits(parts):
            found = []
            for m, part in parts:
                if (m, part) not in waited:
                    found.append(("complete", (m, part, not any(of == m for of, _ in waited))))
                    waited.append((m, part))
            return found

        def spread(acts):
            found = []
            for kind, unit in acts:
                if kind == "fetch":
                    m = self.wholes.index(unit[1])
                    found += waits((m, part) for part in range(self.splits[m]))
                found.append((kind, unit))
            return found

        full = []
        for stage, (before, ticks) in zip(self.stages, plans):
            before = spread(before) + waits(self.parts_of(stage))
            full.append((before, {tick: spread(ticks[tick]) for tick in sorted(ticks)}))
        every = [(m, part) for m, split in enumerate(self.splits) for part in range(split)]
        return full, spread(left) + waits(every)

    def parts_of(self, stage):
        found = []
        for mat, part in stage["needs"]:
            m = self.wholes.index(mat)
            found += [(m, part)] if part is not None else [(m, each) for each in range(self.splits[m])]
        return found

    def run(self):
        given = []
        for stage in self.stages:
            for array, spec in stage["ins"]:
                if not isinstance(array, Later) and not any(array is g for g, _ in given):
                    given.append((array, SCALAR if spec is SCALAR else ANY))
        results = self.wholes + [r for stage in self.stages for r in stage["results"]]
        results += [r for sums in self.sums.values() for r in sums]
        plans, left = self.schedule()
        units = sum(self.splits)

        def kernel(*refs):
            refs = list(refs)
            owns = refs[: len(self.owns)]
            of = {}
            for (array, _), ref in zip(given, refs[len(self.owns) :]):
                of[id(array)] = ref
            rest = refs[len(self.owns) + len(given) :]
            for result, ref in zip(results, rest):
                of[id(result)] = ref
            rest = rest[len(results) :]
            place = Place()
            gather = Gather(place, owns, [of[id(w)] for w in self.wholes], self.splits, *rest[:3])
            rest = rest[3:]
            sums = {}
            for name, whole in self.sums.items():
                tallies = [*rest[11:13], of[id(whole[2])]] if len(whole) > 2 else None
                sums[name] = Reduce(
                    place, rest[:2], rest[2:4], rest[4:6], rest[6:8], [of[id(w)] for w in whole[:2]],
                    rest[8:11], tallies,
                )
                rest = rest[13:] if tallies else rest[11:]
            held = {slot: (rest[2 * at], rest[2 * at + 1]) for at, slot in enumerate(HELD)}
            place.meet()
            gather.begin()

            def act(kind, unit):
                if kind == "step":
                    sums[unit[0]].step(unit[1])
                elif kind == "fetch":
                    slot, mat = unit
                    Fetch(of[id(mat)], *held[slot], 1).start()
                elif kind == "complete":
                    gather.complete(*unit)
                else:
                    getattr(gather, kind)(unit)

            present = {}
            for stage, (before, ticks) in zip(self.stages, plans):
                for kind, unit in before:
                    act(kind, unit)
                for slot, mat in stage["held"].items():
                    if present.get(slot) is not mat:
                        Fetch(of[id(mat)], *held[slot], 1).copy(0).wait()
                        present[slot] = mat
                self.run_stage(stage, ticks, act, of, sums, held)
            for kind, unit in left:
                act(kind, unit)
            gather.finish()
            for each in sums.values():
                each.finish()

        buffers = []
        for whole in self.sums.values():
            for kind, share in ((F32, 1), (BF16, 1), (BF16, 1), (BF16, 32)):
                buffers += [pltpu.VMEM((rows // share, width), kind) for rows, width in SHAPES]
            buffers += [pltpu.SemaphoreType.DMA((3, LEVELS, 2)), pltpu.SemaphoreType.DMA((3, LEVELS, 2))]
            buffers.append(pltpu.SemaphoreType.DMA((3,)))
            if len(whole) > 2:
                buffers.append(pltpu.VMEM((LEVELS + 1, 8, 1024), F32))
                buffers.append(pltpu.VMEM((LEVELS, 8, 1024), F32))

        for shape in HELD.values():
            buffers += [pltpu.VMEM(shape, BF16), pltpu.SemaphoreType.DMA((1,))]

        out = pl.pallas_call(
            kernel,
            in_specs=[ANY] * len(self.owns) + [spec for _, spec in given],
            out_specs=[ANY] * len(results),
            scratch_shapes=[
                pltpu.SemaphoreType.DMA((units, 7)),
                pltpu.SemaphoreType.DMA((units, 7)),
                pltpu.SemaphoreType.DMA((len(self.owns),)),
                *buffers,
            ],
            out_shape=[jax.ShapeDtypeStruct(r.shape, r.dtype) for r in results],
            compiler_params=pltpu.CompilerParams(
                vmem_limit_bytes=VMEM_BYTES, collective_id=1, has_side_effects=True
            ),
            name="everything",
        )(*self.owns, *[array for array, _ in given])
        arrays = {id(result): array for result, array in zip(results, out)}
        return lambda later: arrays[id(later)]

    def run_stage(self, stage, ticks, act, of, sums, held):
        ins, outs = stage["ins"], stage["outs"]
        piped = [at for at, (_, spec) in enumerate(ins) if spec is not ANY and spec is not SCALAR]
        fixed = {at: of[id(a)] for at, (a, _) in enumerate(ins) if at not in piped}

        def poll(slot):
            for (step, at), todo in ticks.items():
                if at == slot:

                    @pl.when(pl.program_id(0) == step)
                    def _(todo=todo):
                        for kind, unit in todo:
                            act(kind, unit)

        poll.sums = sums.get(stage["sums"])
        poll.held = held

        def scoped(*scratch):
            if stage["prepare"]:
                stage["prepare"]([fixed.get(at) for at in range(len(ins))], scratch)

            def body(*blocks):
                in_refs = [fixed.get(at) for at in range(len(ins))]
                for at, ref in zip(piped, blocks):
                    in_refs[at] = ref
                stage["body"](in_refs, list(blocks[len(piped) :]), scratch, poll)

            pltpu.emit_pipeline(
                body,
                grid=stage["grid"],
                in_specs=[ins[at][1] for at in piped],
                out_specs=[spec for _, _, spec in outs],
            )(*[of[id(ins[at][0])] for at in piped], *[of[id(r)] for r in stage["results"]])

        pl.run_scoped(scoped, *stage["scratch"])


def launch(
    body, name, grid, ins, outs, scratch, flops, moved, recorder=None, prepare=None, needs=(),
    slots=1, time=1.0, sums=None, held=(),
):
    if recorder is not None:
        return recorder.add(
            body=body, grid=grid, ins=ins, outs=outs, scratch=scratch, prepare=prepare, needs=needs,
            slots=slots, time=time, sums=sums, held=dict(held),
        )

    def kernel(*refs):
        in_refs, out_refs = list(refs[: len(ins)]), list(refs[len(ins) : len(ins) + len(outs)])
        rest = refs[len(ins) + len(outs) :]
        if prepare:

            @pl.when(pl.program_id(0) == 0)
            def _():
                prepare(in_refs, rest)

        body(in_refs, out_refs, rest, lambda slot: None)

    return pl.pallas_call(
        kernel,
        grid=grid,
        in_specs=[spec for _, spec in ins],
        out_specs=[spec for _, _, spec in outs],
        scratch_shapes=scratch,
        out_shape=[jax.ShapeDtypeStruct(s, d) for s, d, _ in outs],
        compiler_params=pltpu.CompilerParams(vmem_limit_bytes=VMEM_BYTES),
        cost_estimate=pl.CostEstimate(flops=flops, bytes_accessed=moved, transcendentals=0),
        name=name,
    )(*[a for a, _ in ins])


class Ready:
    def __init__(self, whole):
        self.whole = whole

    def wait(self, chunk):
        pass

    def wait_all(self):
        pass


def staged_call(body, name, grid, limit, mats, ins, outs, scratch=(), flops=0, part=None, slots_of=(), **record):
    held = dict(zip(slots_of, (mat for mat, _ in mats))) if record else {}
    own = mats[len(held) :]
    holders = []
    for mat, chunks in own:
        rows, width = mat.shape
        holders.append(pltpu.VMEM((rows, width if part is None else width // 3), mat.dtype))
        holders.append(pltpu.SemaphoreType.DMA((chunks,)))
    given = [mat for mat, _ in own]

    def fetches(in_refs, rest):
        return [
            Fetch(
                in_refs[1 + at], rest[2 * at], rest[2 * at + 1], chunks,
                0 if part is None else part * mat.shape[1] // 3,
            )
            for at, (mat, chunks) in enumerate(own)
        ]

    def prepare(in_refs, rest):
        for fetch in fetches(in_refs, rest):
            fetch.start()

    def staged(in_refs, out_refs, rest, poll):
        ready = [Ready(poll.held[slot][0]) for slot in held]
        args = (in_refs[0], ready + fetches(in_refs, rest), in_refs[1 + len(given) :], out_refs)
        body(*args, rest[2 * len(own) :], poll)

    moved = sum(a.size * a.dtype.itemsize for a in given)
    moved += sum(a.size * a.dtype.itemsize for a, _ in ins)
    moved += sum(math.prod(s) * jnp.dtype(d).itemsize for s, d, _ in outs)
    if record:
        record = dict(record, needs=[(mat, part) for mat in given], held=held)
    return launch(
        staged,
        name,
        grid,
        [(limit, SCALAR)] + [(mat, ANY) for mat in given] + list(ins),
        outs,
        [*holders, *scratch],
        flops,
        moved,
        prepare=prepare,
        **record,
    )


def project(name, limit, rows_in, mat, chunks, part=None, **record):
    total, depth = rows_in.shape
    width = mat.shape[1] if part is None else mat.shape[1] // 3
    block = min(256, total)
    step = width // chunks

    def body(limit, fetches, ins, outs, extra, poll):
        (fetch,) = fetches
        left = ins[0][...]
        for chunk in range(chunks):
            poll(chunk)
            fetch.wait(chunk)
            columns = slice(chunk * step, (chunk + 1) * step)
            outs[0][:, columns] = nn(left, fetch.whole[:, columns]).astype(BF16)

    return staged_call(
        body,
        name,
        (total // block,),
        limit,
        [(mat, chunks)],
        [(rows_in, rows_spec(block, depth))],
        [((total, width), BF16, rows_spec(block, width))],
        flops=2 * total * depth * width,
        part=part,
        **record,
    )[0]


def attend(name, limit, queries, keys, values, causal, **record):
    q_len, k_len = queries[0].shape[0], keys[0].shape[0]
    pairs = 1024 // PAIR
    step = min(512, q_len)

    def body(ins, outs, extra, poll):
        poll(0)
        limit_ref, q_ref, k_ref, v_ref = ins
        e_ref, o_ref, inv_ref = outs
        lanes = lax.broadcasted_iota(jnp.int32, (1, PAIR), 1)
        places = lax.broadcasted_iota(jnp.int32, (k_len, 1), 0)
        bias = jnp.where(places < limit_ref[0], 0.0, -1000000000.0)
        q_two = q_ref[...].astype(F32) * (1.0 / math.sqrt(HEAD))
        k_two = k_ref[...].astype(F32)
        v_two = v_ref[...].astype(F32)
        q_own, k_own, v_own = [], [], []
        for half in range(2):
            own = (lanes >= HEAD * half) & (lanes < HEAD * (half + 1))
            spare = lanes == HEAD * (1 - half)
            q_own.append(jnp.where(own, q_two, jnp.where(spare, 1.0, 0.0)).astype(BF16))
            k_own.append(jnp.where(own, k_two, jnp.where(spare, bias, 0.0)).astype(BF16))
            v_own.append(jnp.where(own, v_two, jnp.where(spare, 1.0, 0.0)).T.astype(BF16))

        def score(half, start):
            scores = nt(k_own[half], q_own[half][start : start + step])
            if causal:
                shape = (k_len, step)
                key_at = lax.broadcasted_iota(jnp.int32, shape, 0)
                query_at = lax.broadcasted_iota(jnp.int32, shape, 1) + start
                scores = jnp.where(key_at <= query_at, scores, -1000000000.0)
            return scores

        blocks = [(half, start) for half in range(2) for start in range(0, q_len, step)]
        parts = [[], []]
        scores = score(*blocks[0])
        for at, (half, start) in enumerate(blocks):
            later = score(*blocks[at + 1]) if at + 1 < len(blocks) else None
            highest = jnp.max(scores, axis=0, keepdims=True)
            weights = jnp.exp(scores - highest).astype(BF16)
            e_ref[0, :, half * q_len + start : half * q_len + start + step] = weights
            parts[half].append(nn(v_own[half], weights))
            scores = later
        mixed = []
        for half in range(2):
            out = jnp.concatenate(parts[half], axis=1) if len(parts[half]) > 1 else parts[half][0]
            at = HEAD * (1 - half)
            inverse = 1.0 / out[at : at + 1]
            own_rows = out[HEAD * half : HEAD * (half + 1)]
            mixed.append((own_rows * inverse, jnp.broadcast_to(inverse, own_rows.shape)))
        o_ref[...] = jnp.concatenate([mixed[0][0], mixed[1][0]], axis=0).T.astype(BF16)
        inv_ref[...] = jnp.concatenate([mixed[0][1], mixed[1][1]], axis=0).T

    def columns(rows, first):
        return pl.BlockSpec((rows, PAIR), lambda i: (0, first + i))

    return launch(
        body,
        name,
        (pairs,),
        [
            (limit, SCALAR),
            (queries[0], columns(q_len, queries[1])),
            (keys[0], columns(k_len, keys[1])),
            (values[0], columns(k_len, values[1])),
        ],
        [
            (
                (pairs, k_len, 2 * q_len),
                BF16,
                pl.BlockSpec((1, k_len, 2 * q_len), lambda i: (i, 0, 0)),
            ),
            ((q_len, 1024), BF16, columns(q_len, 0)),
            ((q_len, 1024), F32, columns(q_len, 0)),
        ],
        [],
        16 * pairs * q_len * k_len * PAIR,
        4 * pairs * q_len * k_len,
        **record,
    )


def attend_grad(name, queries, keys, values, weights, mixture, inverse, upstream, **record):
    q_len, k_len = queries[0].shape[0], keys[0].shape[0]
    pairs = 1024 // PAIR
    step = min(256, q_len)
    factor = 1.0 / math.sqrt(HEAD)

    def body(ins, outs, extra, poll):
        q_ref, k_ref, v_ref, e_ref, o_ref, inv_ref, do_ref = ins
        dq_ref, dk_ref, dv_ref = outs
        (ds_ref,) = extra
        poll(0)
        lanes = lax.broadcasted_iota(jnp.int32, (1, PAIR), 1)
        first = lanes < HEAD
        scaled = do_ref[...].astype(F32) * inv_ref[...]
        inner = scaled.astype(BF16).astype(F32) * o_ref[...].astype(F32)
        coarse = inner.astype(BF16)
        fine = (inner - coarse.astype(F32)).astype(BF16)
        picks = lax.broadcasted_iota(jnp.int32, (8, PAIR), 1)
        ones = [
            jnp.where(picks < HEAD, 1.0, 0.0).astype(BF16),
            jnp.where(picks < HEAD, 0.0, 1.0).astype(BF16),
        ]
        delta = [(nt(one, coarse) + nt(one, fine))[0:1] for one in ones]
        do_two = jnp.concatenate(
            [jnp.where(first, scaled, 0.0).astype(BF16), jnp.where(first, 0.0, scaled).astype(BF16)],
            axis=0,
        )
        q_all = q_ref[...].astype(F32) * factor
        q_two = jnp.concatenate(
            [jnp.where(first, q_all, 0.0).astype(BF16), jnp.where(first, 0.0, q_all).astype(BF16)],
            axis=0,
        )
        k_flip = k_ref[...].astype(F32).T.astype(BF16)
        v_all = v_ref[...]
        for half in range(2):
            for start in range(0, q_len, step):
                at = half * q_len + start
                probs_grad = nt(v_all, do_two[at : at + step])
                held = e_ref[0, :, at : at + step].astype(F32)
                ds_ref[:, at : at + step] = (
                    held * (probs_grad - delta[half][:, start : start + step])
                ).astype(BF16)
        dv_ref[...] = nn(e_ref[0], do_two).astype(BF16)
        dk_ref[...] = nn(ds_ref[...], q_two).astype(BF16)
        turned = nn(k_flip, ds_ref[...]) * factor
        rows = lax.broadcasted_iota(jnp.int32, (PAIR, 1), 0)
        dq_ref[...] = jnp.where(rows < HEAD, turned[:, :q_len], turned[:, q_len:]).T.astype(BF16)

    def columns(rows, at):
        return pl.BlockSpec((rows, PAIR), lambda i: (0, at + i))

    return launch(
        body,
        name,
        (pairs,),
        [
            (queries[0], columns(q_len, queries[1])),
            (keys[0], columns(k_len, keys[1])),
            (values[0], columns(k_len, values[1])),
            (weights, pl.BlockSpec((1, k_len, 2 * q_len), lambda i: (i, 0, 0))),
            (mixture, columns(q_len, 0)),
            (inverse, columns(q_len, 0)),
            (upstream, columns(q_len, 0)),
        ],
        [
            ((q_len, 1024), BF16, columns(q_len, 0)),
            ((k_len, 1024), BF16, columns(k_len, 0)),
            ((k_len, 1024), BF16, columns(k_len, 0)),
        ],
        [pltpu.VMEM((k_len, 2 * q_len), BF16)],
        32 * pairs * q_len * k_len * PAIR,
        4 * pairs * q_len * k_len,
        **record,
    )


def row_mask(limit, block):
    at = lax.broadcasted_iota(jnp.int32, (block, 1), 0) + pl.program_id(0) * block
    return (at < limit).astype(F32)


def add_squares(ref, row, entries, mask):
    sums = jnp.sum(entries * entries * mask, axis=0, keepdims=True)
    first = pl.program_id(0) == 0

    @pl.when(first)
    def _():
        ref[row : row + 1, :] = sums

    @pl.when(jnp.logical_not(first))
    def _():
        ref[row : row + 1, :] += sums


def spread_lanes(column):
    return jnp.broadcast_to(column, (column.shape[0], 128))


def out_norm(name, limit, mixture, residual, gain, mat, next_mat=None, residual_gain=None, **record):
    total, width = mixture.shape
    block = min(256, total)
    mats = [(mat, 1)] + ([] if next_mat is None else [(next_mat, 1)])

    def body(limit, fetches, ins, outs, extra, poll):
        poll(0)
        o_ref, r_ref, g_ref, rg_ref = ins
        fetches[0].wait_all()
        added = nn(o_ref[...], fetches[0].whole[...])
        base = r_ref[...].astype(F32)
        if residual_gain is not None:
            base = base * rg_ref[...]
        unit, inverse = standardize(base + added)
        outs[0][...] = unit.astype(BF16)
        outs[1][...] = spread_lanes(inverse)
        add_squares(outs[2], 0, added, row_mask(limit[0], block))
        if next_mat is not None:
            fetches[1].wait_all()
            hidden = (unit * g_ref[...]).astype(BF16)
            outs[3][...] = nn(hidden, fetches[1].whole[...]).astype(BF16)

    outs = [
        ((total, width), BF16, rows_spec(block, width)),
        ((total, 128), F32, rows_spec(block, 128)),
        ((8, width), F32, whole_spec((8, width))),
    ]
    if next_mat is not None:
        outs.append(((total, width), BF16, rows_spec(block, width)))
    return staged_call(
        body,
        name,
        (total // block,),
        limit,
        mats,
        [
            (mixture, rows_spec(block, width)),
            (residual, rows_spec(block, width)),
            (gain, whole_spec((1, width))),
            (gain if residual_gain is None else residual_gain, whole_spec((1, width))),
        ],
        outs,
        flops=2 * total * width * width * len(mats),
        **record,
    )


def branch(name, limit, unit, gain, gain_out, w_in, w_back, down_low, up_low, **record):
    total, width = unit.shape
    hidden_units = w_in.shape[1]
    adapter = down_low.shape[1]
    block = min(256, total)
    chunks = 4
    step = hidden_units // chunks

    def body(limit, fetches, ins, outs, extra, poll):
        u_ref, g_ref, go_ref, ad_ref, au_ref = ins
        y_ref, unit_ref, inv_ref, slope_ref, wa_ref, ad_slope_ref, sq_ref = outs
        (act,) = extra
        first, second = fetches
        hidden = u_ref[...].astype(F32) * g_ref[...]
        low = hidden.astype(BF16)
        pre = nn(low, ad_ref[...].astype(BF16))
        gate = jax.nn.sigmoid(pre)
        wa = (pre * gate).astype(BF16)
        wa_ref[...] = wa
        ad_slope_ref[...] = (gate * (1.0 + pre * (1.0 - gate))).astype(BF16)
        adapted = 4.0 * nn(wa, au_ref[...].astype(BF16))
        for chunk in range(chunks):
            if chunk % 2 == 0:
                poll(chunk // 2)
            first.wait(chunk)
            columns = slice(chunk * step, (chunk + 1) * step)
            fp = nn(low, first.whole[:, columns])
            cdf = 0.5 * (1.0 + lax.erf(fp * (1.0 / math.sqrt(2.0))))
            act[:, columns] = (fp * cdf).astype(BF16)
            bell = jnp.exp(-0.5 * fp * fp) * (1.0 / math.sqrt(2.0 * math.pi))
            slope_ref[:, columns] = (cdf + fp * bell).astype(BF16)
        second.wait_all()
        added = nn(act[...], second.whole[...]) + adapted
        out_unit, inverse = standardize(hidden + added)
        result = out_unit * go_ref[...]
        y_ref[...] = result.astype(BF16)
        unit_ref[...] = out_unit.astype(BF16)
        inv_ref[...] = spread_lanes(inverse)
        mask = row_mask(limit[0], block)
        add_squares(sq_ref, 0, added, mask)
        add_squares(sq_ref, 1, result, mask)

    return staged_call(
        body,
        name,
        (total // block,),
        limit,
        [(w_in, chunks), (w_back, 1)],
        [
            (unit, rows_spec(block, width)),
            (gain, whole_spec((1, width))),
            (gain_out, whole_spec((1, width))),
            (down_low, whole_spec(down_low.shape)),
            (up_low, whole_spec(up_low.shape)),
        ],
        [
            ((total, width), BF16, rows_spec(block, width)),
            ((total, width), BF16, rows_spec(block, width)),
            ((total, 128), F32, rows_spec(block, 128)),
            ((total, hidden_units), BF16, rows_spec(block, hidden_units)),
            ((total, adapter), BF16, rows_spec(block, adapter)),
            ((total, adapter), BF16, rows_spec(block, adapter)),
            ((8, width), F32, whole_spec((8, width))),
        ],
        scratch=[pltpu.VMEM((block, hidden_units), BF16)],
        flops=4 * total * width * (hidden_units + adapter),
        slots_of=("within", "back"),
        **record,
    )


def adapter_grad(upstream, refs):
    (uo_ref, io_ref, go_ref, ui_ref, gi_ref, wa_ref, as_ref, ad_ref, au_ref) = refs
    grad_two = standardize_grad(uo_ref[...].astype(F32), io_ref[:, 0:1], upstream * go_ref[...])
    dvd = (4.0 * grad_two).astype(BF16)
    low = (ui_ref[...].astype(F32) * gi_ref[...]).astype(BF16)
    du = (nt(dvd, au_ref[...].astype(BF16)) * as_ref[...].astype(F32)).astype(BF16)
    total = grad_two + nt(du, ad_ref[...].astype(BF16))
    return grad_two.astype(BF16), total, tn(low, du), tn(wa_ref[...], dvd)


def hidden_grad(dz, total, fetches, refs, dfp, chunks, poll=lambda slot: None):
    slope_ref, ui_ref, ii_ref, gi_ref = refs
    back, within, last = fetches
    step = dfp.shape[1] // chunks
    back.wait_all()
    poll(0)
    for chunk in range(chunks):
        columns = slice(chunk * step, (chunk + 1) * step)
        act_grad = nt(dz, back.whole[columns, :])
        dfp[:, columns] = (act_grad * slope_ref[:, columns].astype(F32)).astype(BF16)
    within.wait_all()
    poll(1)
    total = total + nt(dfp[...], within.whole[...])
    grad_one = standardize_grad(ui_ref[...].astype(F32), ii_ref[:, 0:1], total * gi_ref[...])
    last.wait_all()
    return grad_one, nt(grad_one.astype(BF16), last.whole[...]).astype(BF16)


def dec_branch_grad(
    name, limits, cot, saved_out, gain_out, saved_in, gain_in, slope, wa, ad_slope,
    w_back, w_in, w_out, down_low, up_low, squares, **record,
):
    total, width = cot.shape
    hidden_units = w_in.shape[1]
    adapter = down_low.shape[1]
    whole = [
        cot, saved_out[0], saved_out[1], gain_out, saved_in[0], gain_in, wa, ad_slope, down_low,
        up_low, slope, saved_in[1], *squares,
    ]

    def body(limit, fetches, ins, outs, extra, poll):
        grad_ref, mix_ref = outs[:2]
        if record:
            (down_ref, up_ref), tally_ref = poll.sums.totals, poll.sums.tallies[0].at[0]
        else:
            down_ref, up_ref, tally_ref = outs[2], outs[3].at[:adapter], outs[3].at[adapter:]
        (other,), cot_ref, slope_ref, ii_ref = ins[:1], ins[1], ins[11], ins[12]
        dz, part, down_ref[...], up_ref[...] = adapter_grad(cot_ref[...].astype(F32), ins[2:11])
        sums = [ref[row : row + 1, :] for ref, rows in zip(ins[13:], (1, 2, 1, 1, 2)) for row in range(rows)]
        lanes = lax.broadcasted_iota(jnp.int32, (1, width), 1)
        counts = jnp.where(lanes == 0, limit[0], jnp.where(lanes == 1, other[0], 0)).astype(F32)
        tally_ref[...] = jnp.concatenate([*sums, counts], axis=0)
        grad_ref[...], mix_ref[...] = hidden_grad(
            dz, part, fetches, (slope_ref, ins[5], ii_ref, ins[6]), extra[0], 4
        )

    return staged_call(
        body,
        name,
        (1,),
        limits[0],
        [(w_back, 1), (w_in, 1), (w_out, 1)],
        [(limits[1], SCALAR)] + [(a, whole_spec(a.shape)) for a in whole],
        [
            (cot.shape, F32, whole_spec(cot.shape)),
            (cot.shape, BF16, whole_spec(cot.shape)),
        ]
        + [
            (shape, F32, whole_spec(shape))
            for shape in (() if record else (down_low.shape, (adapter + 8, width)))
        ],
        scratch=[pltpu.VMEM((total, hidden_units), BF16)],
        flops=4 * total * width * (hidden_units + 2 * adapter),
        slots_of=("back", "within"),
        **record,
    )


def enc_adapter_grad(
    name, limit, cot, cross, cross_mat, saved_out, gain_out, saved_in, gain_in, wa, ad_slope,
    down_low, up_low, **record,
):
    total, width = cot.shape
    adapter = down_low.shape[1]
    block = min(256, total)
    rows = rows_spec(block, width)

    def body(limit, fetches, ins, outs, extra, poll):
        poll(0)
        dz_ref, part_ref = outs[:2]
        down_sum, up_sum = poll.sums.totals if record else extra
        fetches[0].wait_all()
        upstream = ins[0][...].astype(F32)
        for at in range(2):
            upstream = upstream + nt(ins[1 + at][...], fetches[0].whole[:, at * width : (at + 1) * width])
        dz_ref[...], part_ref[...], down_part, up_part = adapter_grad(upstream, ins[3:])
        at = pl.program_id(0)

        @pl.when(at == 0)
        def _():
            up_sum[...] = up_part
            down_sum[...] = down_part

        @pl.when(at > 0)
        def _():
            up_sum[...] += up_part
            down_sum[...] += down_part

        if not record:

            @pl.when(at == total // block - 1)
            def _():
                outs[2][...] = down_sum[...].astype(BF16)
                outs[3][...] = up_sum[...].astype(BF16)

    return staged_call(
        body,
        name,
        (total // block,),
        limit,
        [(cross_mat, 1)],
        [
            (cot, rows),
            (cross[0], rows),
            (cross[1], rows),
            (saved_out[0], rows),
            (saved_out[1], rows_spec(block, 128)),
            (gain_out, whole_spec((1, width))),
            (saved_in[0], rows),
            (gain_in, whole_spec((1, width))),
            (wa, rows_spec(block, adapter)),
            (ad_slope, rows_spec(block, adapter)),
            (down_low, whole_spec(down_low.shape)),
            (up_low, whole_spec(up_low.shape)),
        ],
        [
            ((total, width), BF16, rows),
            ((total, width), F32, rows),
        ]
        + [(a.shape, BF16, whole_spec(a.shape)) for a in (() if record else (down_low, up_low))],
        scratch=[pltpu.VMEM(a.shape, F32) for a in (() if record else (down_low, up_low))],
        flops=4 * total * width * (width + 2 * adapter),
        **record,
    )


def enc_hidden_grad(name, limit, dz, part, slope, saved_in, gain_in, w_back, w_in, w_out, **record):
    total, width = dz.shape
    hidden_units = w_in.shape[1]
    block = min(256, total)
    rows = rows_spec(block, width)

    def body(limit, fetches, ins, outs, extra, poll):
        outs[0][...], outs[1][...] = hidden_grad(
            ins[0][...], ins[1][...], fetches, ins[2:], extra[0], 4, poll
        )

    return staged_call(
        body,
        name,
        (total // block,),
        limit,
        [(w_back, 1), (w_in, 1), (w_out, 1)],
        [
            (dz, rows),
            (part, rows),
            (slope, rows_spec(block, hidden_units)),
            (saved_in[0], rows),
            (saved_in[1], rows_spec(block, 128)),
            (gain_in, whole_spec((1, width))),
        ],
        [((total, width), F32, rows), ((total, width), BF16, rows)],
        scratch=[pltpu.VMEM((block, hidden_units), BF16)],
        flops=4 * total * width * hidden_units,
        slots_of=("back", "within"),
        **record,
    )


def middle_grad(name, limit, grad_cross, dq, saved, gain, w_cq, w_so, **record):
    total, width = dq.shape
    block = min(256, total)
    unit, inv = saved

    def body(limit, fetches, ins, outs, extra, poll):
        poll(0)
        gc_ref, dq_ref, u_ref, i_ref, g_ref = ins
        fetches[0].wait_all()
        hidden_grad = gc_ref[...] + nt(dq_ref[...], fetches[0].whole[...])
        grad_self = standardize_grad(
            u_ref[...].astype(F32), i_ref[:, 0:1], hidden_grad * g_ref[...]
        )
        outs[0][...] = grad_self
        fetches[1].wait_all()
        outs[1][...] = nt(grad_self.astype(BF16), fetches[1].whole[...]).astype(BF16)

    return staged_call(
        body,
        name,
        (total // block,),
        limit,
        [(w_cq, 1), (w_so, 1)],
        [
            (grad_cross, rows_spec(block, width)),
            (dq, rows_spec(block, width)),
            (unit, rows_spec(block, width)),
            (inv, rows_spec(block, 128)),
            (gain, whole_spec((1, width))),
        ],
        [
            ((total, width), F32, rows_spec(block, width)),
            ((total, width), BF16, rows_spec(block, width)),
        ],
        flops=4 * total * width * width,
        **record,
    )


def input_grad(name, limit, base, parts, mat, narrow=(), tally=None):
    total, width = base.shape
    block = min(256, total)
    steps = total // block
    count = len(parts)

    def body(limit, fetches, ins, outs, extra, poll):
        (fetch,) = fetches
        result = ins[0][...]
        for at in range(count):
            fetch.wait(at)
            result = result + nt(ins[1 + at][...], fetch.whole[:, at * width : (at + 1) * width])
        outs[0][...] = result
        for at in range(len(narrow)):
            outs[1 + at][...] = ins[1 + count + at][...].astype(F32)
        if tally is not None:
            rows = ins[-1][...]
            at = lax.broadcasted_iota(jnp.int32, (8, 1), 0)
            numbers = jnp.where(at < 3, rows[7:8, 0:1], rows[7:8, 1:2])
            outs[-1][...] = spread_lanes(
                jnp.sqrt(jnp.sum(rows, axis=1, keepdims=True) / (numbers * width))
            )

    slices = [(a, rows_spec(a.shape[0] // steps, a.shape[1])) for a in narrow]
    tallies = [] if tally is None else [(tally, whole_spec(tally.shape))]
    return staged_call(
        body,
        name,
        (steps,),
        limit,
        [(mat, count)],
        [(base, rows_spec(block, width))] + [(p, rows_spec(block, width)) for p in parts] + slices + tallies,
        [((total, width), F32, rows_spec(block, width))]
        + [(a.shape, F32, spec) for a, spec in slices]
        + [((8, 128), F32, whole_spec((8, 128))) for _ in tallies],
        flops=2 * total * width * width * count,
    )


NAMES = (
    "enc_qkv",
    "enc_attn_out",
    "enc_ffn_in",
    "enc_ffn_out",
    "dec_self_qkv",
    "dec_self_out",
    "dec_cross_q",
    "dec_cross_kv",
    "dec_cross_out",
    "dec_ffn_in",
    "dec_ffn_out",
)


def layers(enc_limit, dec_limit, enc_input, dec_input, enc_cot, dec_cot, blocks, hosting, fsdp, gains, adapters):
    gain = [gains[k : k + 1] for k in range(5)]
    enc_down, enc_up, dec_down, dec_up = adapters
    if hosting:
        recorder = Recorder(blocks, fsdp)
        w = dict(zip(recorder.names, recorder.wholes))
    else:
        recorder = None
        w = {name: lax.all_gather(b, "fsdp", axis=0, tiled=True) for name, b in blocks.items()}

    def at(slots, time, sums=None):
        if not hosting:
            return {}
        return {"recorder": recorder, "slots": slots, "time": time, "sums": sums}

    enc_q, enc_k, enc_v = (
        project("enc_project", enc_limit, enc_input, w["enc_qkv"], 1, part, **at(1, 5.0))
        for part in range(3)
    )
    e_enc, o_enc, inv_enc = attend(
        "enc_attend", enc_limit, (enc_q, 0), (enc_k, 0), (enc_v, 0), False, **at(1, 34.0)
    )
    unit1, dev1, sq_a = out_norm(
        "enc_out_norm", enc_limit, o_enc, enc_input, gain[0], w["enc_attn_out"], **at(1, 9.0)
    )
    enc_out, unit2, dev2, slope_e, wa_e, ads_e, sq_b = branch(
        "enc_branch", enc_limit, unit1, gain[0], gain[1], w["enc_ffn_in"], w["enc_ffn_out"],
        enc_down, enc_up, **at(2, 33.0),
    )
    sqkv = project("dec_project", dec_limit, dec_input, w["dec_self_qkv"], 3, **at(3, 6.0))
    e_self, o_self, inv_self = attend(
        "dec_attend", dec_limit, (sqkv, 0), (sqkv, 8), (sqkv, 16), True, **at(1, 8.5)
    )
    unit3, dev3, sq_c, cross_q = out_norm(
        "dec_out_norm", dec_limit, o_self, dec_input, gain[2], w["dec_self_out"], w["dec_cross_q"],
        **at(1, 5.3),
    )
    kv = project("cross_project", enc_limit, enc_out, w["dec_cross_kv"], 2, **at(2, 9.5))
    e_cross, o_cross, inv_cross = attend(
        "cross_attend", enc_limit, (cross_q, 0), (kv, 0), (kv, 8), False, **at(1, 14.0)
    )
    unit4, dev4, sq_d = out_norm(
        "cross_out_norm", dec_limit, o_cross, unit3, gain[3], w["dec_cross_out"],
        residual_gain=gain[2], **at(1, 4.6),
    )
    dec_out, unit5, dev5, slope_d, wa_d, ads_d, sq_e = branch(
        "dec_branch", dec_limit, unit4, gain[3], gain[4], w["dec_ffn_in"], w["dec_ffn_out"],
        dec_down, dec_up, **at(2, 8.0),
    )
    dec_sums = recorder.reduce("dec", True) if hosting else []
    grad_cross, do_cross, *dec_grads = dec_branch_grad(
        "dec_branch_grad", (enc_limit, dec_limit), dec_cot, (unit5, dev5), gain[4], (unit4, dev4), gain[3],
        slope_d, wa_d, ads_d, w["dec_ffn_out"], w["dec_ffn_in"], w["dec_cross_out"], dec_down, dec_up,
        (sq_a, sq_b, sq_c, sq_d, sq_e), **at(1, 11.0, "dec"),
    )
    dcq, dck, dcv = attend_grad(
        "cross_attend_grad", (cross_q, 0), (kv, 0), (kv, 8), e_cross, o_cross, inv_cross, do_cross,
        **at(1, 13.0),
    )
    enc_sums = recorder.reduce("enc", False) if hosting else []
    dz, part, *enc_grads = enc_adapter_grad(
        "enc_adapter_grad", enc_limit, enc_cot, (dck, dcv), w["dec_cross_kv"], (unit2, dev2), gain[1],
        (unit1, dev1), gain[0], wa_e, ads_e, enc_down, enc_up, **at(1, 20.0, "enc"),
    )
    grad_one, do_enc = enc_hidden_grad(
        "enc_hidden_grad", enc_limit, dz, part, slope_e, (unit1, dev1), gain[0],
        w["enc_ffn_out"], w["enc_ffn_in"], w["enc_attn_out"], **at(2, 28.0),
    )
    deq, dek, dev = attend_grad(
        "enc_attend_grad", (enc_q, 0), (enc_k, 0), (enc_v, 0), e_enc, o_enc, inv_enc, do_enc, **at(1, 39.0)
    )
    grad_self, do_self = middle_grad(
        "dec_middle_grad", dec_limit, grad_cross, dcq, (unit3, dev3), gain[2], w["dec_cross_q"],
        w["dec_self_out"], **at(1, 6.0),
    )
    dsq, dsk, dsv = attend_grad(
        "dec_attend_grad", (sqkv, 0), (sqkv, 8), (sqkv, 16), e_self, o_self, inv_self, do_self,
        **at(1, 8.0),
    )
    if hosting:
        value = recorder.run()
        w = {name: value(mat) for name, mat in w.items()}
        enc_out, dec_out, grad_one, grad_self = map(value, (enc_out, dec_out, grad_one, grad_self))
        deq, dek, dev, dsq, dsk, dsv = map(value, (deq, dek, dev, dsq, dsk, dsv))
        *dec_grads, tally = map(value, dec_sums)
        enc_grads = [value(a) for a in enc_sums]
    else:
        everyone = ("fsdp", "dp")
        down, up = lax.psum(dec_grads, everyone)
        dec_grads, tally = [down, up[: dec_up.shape[0]]], up[dec_up.shape[0] :]
        enc_grads = lax.psum(enc_grads, everyone)
    dec_grad, *dec_grads = input_grad(
        "dec_input_grad", dec_limit, grad_self, [dsq, dsk, dsv], w["dec_self_qkv"], dec_grads
    )
    enc_grad, *enc_grads, rms = input_grad(
        "enc_input_grad", enc_limit, grad_one, [deq, dek, dev], w["enc_qkv"], enc_grads, tally
    )
    return enc_out, dec_out, enc_grad, dec_grad, *enc_grads, *dec_grads, rms[:7, 0]


def shards(fsdp, dp, enc_input, dec_input, enc_cot, dec_cot, *rest):
    mats, (gains, enc_down, enc_up, dec_down, dec_up, enc_lengths, dec_lengths) = rest[:11], rest[11:]
    return layers(
        enc_lengths, dec_lengths, enc_input, dec_input, enc_cot, dec_cot, dict(zip(NAMES, mats)),
        fsdp == 8 and dp == 4, fsdp, gains, (enc_down, enc_up, dec_down, dec_up),
    )


def solution(mesh):
    by_rows = P(("fsdp", "dp"), None)
    placed = (by_rows,) * 4 + (P("fsdp", None),) * 11 + (P(),) * 5 + (P(("fsdp", "dp")),) * 2
    return jax.shard_map(
        functools.partial(shards, mesh.shape["fsdp"], mesh.shape["dp"]),
        mesh=mesh,
        in_specs=placed,
        out_specs=(by_rows,) * 4 + (P(),) * 5,
        check_vma=False,
    )
```

```python
import functools
import math

import jax
import jax.numpy as jnp
from jax import lax
from jax.experimental import pallas as pl
from jax.experimental.pallas import tpu as pltpu
from jax.sharding import PartitionSpec as P

HEAD = 64
PAIR = 2 * HEAD
EPSILON = 1e-05
F32 = jnp.float32
BF16 = jnp.bfloat16
VMEM_BYTES = 58 * 2**20


def nn(former, latter):
    return jnp.dot(former, latter, preferred_element_type=F32)


def nt(former, latter):
    return lax.dot_general(
        former, latter, (((1,), (1,)), ((), ())), preferred_element_type=F32
    )


def tn(former, latter):
    return lax.dot_general(
        former, latter, (((0,), (0,)), ((), ())), preferred_element_type=F32
    )


def standardize(entries):
    centered = entries - jnp.mean(entries, axis=-1, keepdims=True)
    spread = jnp.mean(centered * centered, axis=-1, keepdims=True)
    inverse = lax.rsqrt(spread + EPSILON)
    return centered * inverse, inverse


def standardize_grad(unit, inverse, scaled):
    return inverse * (
        scaled
        - jnp.mean(scaled, axis=-1, keepdims=True)
        - unit * jnp.mean(scaled * unit, axis=-1, keepdims=True)
    )


class Fetch:
    def __init__(self, source, whole, sems, chunks, first=0):
        self.source, self.whole, self.sems, self.chunks = source, whole, sems, chunks
        self.first = first

    def copy(self, chunk):
        width = self.whole.shape[1] // self.chunks
        return pltpu.make_async_copy(
            self.source.at[:, pl.ds(self.first + chunk * width, width)],
            self.whole.at[:, pl.ds(chunk * width, width)],
            self.sems.at[chunk],
        )

    def start(self):
        for chunk in range(self.chunks):
            self.copy(chunk).start()

    def wait(self, chunk):
        @pl.when(pl.program_id(0) == 0)
        def _():
            self.copy(chunk).wait()

    def wait_all(self):
        for chunk in range(self.chunks):
            self.wait(chunk)


UNIT_US = 6.0
LEAD_US = 5.0


class Place:
    def __init__(self):
        f, z = lax.axis_index("fsdp"), lax.axis_index("dp")
        self.core, self.x, self.y = f % 2, (f // 2) % 2, f // 4
        self.odd, self.high = z % 2, z // 2
        self.own = f
        self.twin = {"fsdp": f + 1 - 2 * self.core}
        self.beside = {"fsdp": f + 2 - 4 * self.x}
        self.above = {"fsdp": f + 4 - 8 * self.y}
        self.partner = {"dp": z + 1 - 2 * self.odd}
        self.distant = {"dp": z + 2 - 4 * self.high}

    def meet(self):
        barrier = pltpu.get_barrier_semaphore()
        all_of_them = (self.twin, self.beside, self.above, self.partner, self.distant)
        for to in all_of_them:
            pl.semaphore_signal(barrier, inc=1, device_id=to, device_id_type=pl.DeviceIdType.MESH)
        pl.semaphore_wait(barrier, len(all_of_them))


class Gather:
    def __init__(self, place, owns, wholes, splits, sends, recvs, locals_):
        self.place, self.owns, self.wholes, self.splits = place, owns, wholes, splits
        self.sends, self.recvs, self.locals = sends, recvs, locals_
        self.units = [(m, part) for m, split in enumerate(splits) for part in range(split)]
        beside, above = place.beside["fsdp"], place.above["fsdp"]
        self.own = place.own
        self.direct = beside + place.odd * (above - beside)
        self.onward = above + place.odd * (beside - above)
        self.far = beside + 4 - 8 * place.y

    def transfer(self, unit, kind):
        m, part = self.units[unit]
        whole, own = self.wholes[m], self.owns[m]
        block, width = own.shape
        by_columns = width == 3072
        rows = block if by_columns else block // self.splits[m]
        wide = width // self.splits[m] if by_columns else width
        first_row, columns = (0, pl.ds(part * wide, wide)) if by_columns else (part * rows, pl.ds(0, wide))
        owner = (self.own, self.direct, self.direct, self.own, self.direct, self.far, self.onward)[kind]
        there = whole.at[pl.ds(pl.multiple_of(owner * block + first_row, 16), rows), columns]
        here = own.at[pl.ds(first_row, rows), columns] if kind in (0, 3) else there
        to = self.place.twin if kind >= 3 else self.place.partner
        if kind < 2:
            to = {"fsdp": (self.direct, self.onward)[kind]}
        return pltpu.make_async_remote_copy(
            src_ref=here,
            dst_ref=there,
            send_sem=self.sends.at[unit, kind],
            recv_sem=self.recvs.at[unit, kind],
            device_id=to,
            device_id_type=pl.DeviceIdType.MESH,
        )

    def keep(self, m):
        block = self.owns[m].shape[0]
        rows = pl.ds(pl.multiple_of(self.own * block, 16), block)
        return pltpu.make_async_copy(self.owns[m], self.wholes[m].at[rows, :], self.locals.at[m])

    def begin(self):
        for unit in range(len(self.units)):
            self.transfer(unit, 0).start()
        for unit in range(len(self.units)):
            self.transfer(unit, 3).start()
        for m in range(len(self.owns)):
            self.keep(m).start()

    def pass_on(self, unit):
        self.transfer(unit, 0).wait_recv()
        for kind in (1, 2, 4):
            self.transfer(unit, kind).start()

    def share(self, unit):
        self.transfer(unit, 1).wait_recv()
        self.transfer(unit, 5).start()
        self.transfer(unit, 2).wait_recv()
        self.transfer(unit, 6).start()

    def complete(self, m, part, first):
        for kind in (3, 4, 5, 6):
            self.transfer(self.units.index((m, part)), kind).wait_recv()
        if first:
            self.keep(m).wait()

    def finish(self):
        for unit in range(len(self.units)):
            for kind in range(7):
                self.transfer(unit, kind).wait_send()


LEVELS = 5
SHAPES = ((1024, 512), (512, 1024))


class Reduce:
    def __init__(self, place, totals, gives, takes, pieces, wholes, sems, tallies=None):
        self.place, self.totals, self.gives, self.takes = place, totals, gives, takes
        self.pieces, self.wholes, self.tallies = pieces, wholes, tallies
        self.sends, self.recvs, self.locals = sems
        p = place
        along = [(p.core, p.twin), (p.x, p.beside), (p.y, p.above), (p.odd, p.partner), (p.high, p.distant)]
        self.ways = [along, [along[0], along[2], along[1], along[3], along[4]]]

    def range(self, part, level):
        rows = SHAPES[part][0]
        first = 0
        for bit, _ in self.ways[part][:level]:
            rows = rows // 2
            first = first + bit * rows
        return first, rows

    def halves(self, part, level):
        first, rows = self.range(part, level)
        bit = self.ways[part][level][0]
        half = rows // 2
        return pl.multiple_of(first + bit * half, half), pl.multiple_of(first + (1 - bit) * half, half), half

    def slot(self, part, level):
        rows = SHAPES[part][0]
        return pl.ds(rows - (rows >> level), rows >> (level + 1))

    def remote(self, src, dst, part, level, back):
        return pltpu.make_async_remote_copy(
            src_ref=src,
            dst_ref=dst,
            send_sem=self.sends.at[part, level, back],
            recv_sem=self.recvs.at[part, level, back],
            device_id=self.ways[part if part < 2 else 0][level][1],
            device_id_type=pl.DeviceIdType.MESH,
        )

    def down(self, part, level):
        rows = self.slot(part, level)
        return self.remote(self.gives[part].at[rows, :], self.takes[part].at[rows, :], part, level, 0)

    def up(self, part, level):
        first, rows = self.range(part, level + 1)
        rows = pl.ds(pl.multiple_of(first, rows), rows)
        return self.remote(self.wholes[part].at[rows, :], self.wholes[part].at[rows, :], part, level, 1)

    def tally(self, level):
        return self.remote(self.tallies[0].at[level], self.tallies[1].at[level], 2, level, 0)

    def piece(self, part):
        first, rows = self.range(part, LEVELS)
        rows = pl.ds(pl.multiple_of(first, rows), rows)
        return pltpu.make_async_copy(self.pieces[part], self.wholes[part].at[rows, :], self.locals.at[part])

    def tally_out(self):
        return pltpu.make_async_copy(self.tallies[0].at[LEVELS], self.tallies[2], self.locals.at[2])

    def step(self, at):
        for part in range(2):
            if 0 < at <= LEVELS:
                keep, _, half = self.halves(part, at - 1)
                self.down(part, at - 1).wait_recv()
                rows = pl.ds(keep, half)
                taken = self.takes[part][self.slot(part, at - 1), :].astype(F32)
                self.totals[part][rows, :] = self.totals[part][rows, :] + taken
            if at < LEVELS:
                _, give, half = self.halves(part, at)
                self.gives[part][self.slot(part, at), :] = self.totals[part][pl.ds(give, half), :].astype(BF16)
                self.down(part, at).start()
            elif at == LEVELS:
                first, rows = self.range(part, LEVELS)
                last = pl.ds(pl.multiple_of(first, rows), rows)
                self.pieces[part][...] = self.totals[part][last, :].astype(BF16)
                self.piece(part).start()
                self.piece(part).wait()
                self.up(part, LEVELS - 1).start()
            else:
                level = 2 * LEVELS - at
                self.up(part, level).wait_recv()
                if level:
                    self.up(part, level - 1).start()
        if self.tallies and at <= LEVELS:
            if at:
                self.tally(at - 1).wait_recv()
                self.tallies[0][at] = self.tallies[0][at - 1] + self.tallies[1][at - 1]
            if at < LEVELS:
                self.tally(at).start()
            else:
                self.tally_out().start()

    def finish(self):
        for level in range(LEVELS):
            for part in range(2):
                self.down(part, level).wait_send()
                self.up(part, level).wait_send()
            if self.tallies:
                self.tally(level).wait_send()
        if self.tallies:
            self.tally_out().wait()


REDUCE_US = (0.0, 5.0, 9.0, 6.5, 6.0, 6.0, 6.0, 6.0, 6.5, 9.0, 5.0)


ANY = pl.BlockSpec(memory_space=pl.ANY)
SCALAR = pl.BlockSpec(memory_space=pltpu.SMEM)


def rows_spec(rows, width):
    return pl.BlockSpec((rows, width), lambda i: (i, 0))


def whole_spec(shape):
    return pl.BlockSpec(shape, lambda i: (0,) * len(shape))


class Later:
    def __init__(self, shape, dtype):
        self.shape, self.dtype = tuple(shape), jnp.dtype(dtype)
        self.size = math.prod(self.shape)


HELD = {"within": (1024, 4096), "back": (4096, 1024)}


class Recorder:
    def __init__(self, name, collective, blocks, fsdp):
        self.name, self.collective = name, collective
        self.loads = {}
        self.names = list(blocks)
        self.owns = list(blocks.values())
        self.wholes = [Later((a.shape[0] * fsdp, a.shape[1]), a.dtype) for a in self.owns]
        self.splits = [max(1, a.size // 131072) for a in self.owns]
        self.stages = []
        self.sums = {}

    def reduce(self, name, tallied):
        self.sums[name] = [Later(shape, BF16) for shape in SHAPES]
        if tallied:
            self.sums[name].append(Later((8, 1024), F32))
        return self.sums[name]

    def load(self, name, arrays):
        self.loads[name] = arrays

    def number(self, mat):
        found = [m for m, whole in enumerate(self.wholes) if whole is mat]
        return found[0] if found else None

    def add(self, **stage):
        stage["results"] = [Later(shape, dtype) for shape, dtype, _ in stage["outs"]]
        self.stages.append(stage)
        return stage["results"]

    def schedule(self):
        acts, unit, due = [], 0, LEAD_US
        last_of, come = {}, {}
        for m, split in enumerate(self.splits):
            for part in range(split):
                time = UNIT_US * self.owns[m].size / split / 131072
                due += time
                acts.append((due, "pass_on", unit))
                acts.append((due + time + 2.0, "share", unit))
                last_of[m, part] = unit
                come[m] = due + time + 6.0
                unit += 1
        acts.sort(key=lambda act: act[0])
        clock, plans, started = 0.0, [], []
        for slot in HELD:
            users = [stage for stage in self.stages if slot in stage["held"]]
            if users:
                mat = users[0]["held"][slot]
                acts.append((come.get(self.number(mat), 0.0), "fetch", (slot, mat)))
        for name in self.loads:
            started += [("load", name), ("step", (name, 0))]
            due = 0.0
            for at, time in enumerate(REDUCE_US):
                due += time
                if at:
                    acts.append((due, "step", (name, at)))
        acts.sort(key=lambda act: act[0])
        for index, stage in enumerate(self.stages):
            before, ticks = started, {}
            started = []
            needed = [last_of[m, part] for m, part in self.parts_of(stage)]
            if needed:
                while any(act[1] in ("pass_on", "share") and act[2] <= max(needed) for act in acts):
                    clock = max(clock, acts[0][0])
                    before.append(acts.pop(0)[1:])
            while any(act[1] == "fetch" and act[2][1] is stage["held"].get(act[2][0]) for act in acts):
                clock = max(clock, acts[0][0])
                before.append(acts.pop(0)[1:])
            pace = stage["time"] / stage["grid"][0] / stage["slots"]
            for tick in range(stage["grid"][0] * stage["slots"]):
                while acts and acts[0][0] <= clock:
                    ticks.setdefault(divmod(tick, stage["slots"]), []).append(acts.pop(0)[1:])
                clock += pace
            plans.append((before, ticks))
            for slot in stage["held"]:
                after = [at for at in range(index + 1, len(self.stages)) if slot in self.stages[at]["held"]]
                if after and self.stages[after[0]]["held"][slot] is not stage["held"][slot]:
                    mat = self.stages[after[0]]["held"][slot]
                    acts.append((max(clock, come.get(self.number(mat), 0.0)), "fetch", (slot, mat)))
                    acts.sort(key=lambda act: act[0])
            if stage["sums"]:
                started = [("step", (stage["sums"], 0))]
                due = clock
                for at, time in enumerate(REDUCE_US):
                    due += time
                    if at:
                        acts.append((due, "step", (stage["sums"], at)))
                acts.sort(key=lambda act: act[0])
        return self.completed(plans, [act[1:] for act in acts])

    def completed(self, plans, left):
        waited = []

        def waits(parts):
            found = []
            for m, part in parts:
                if (m, part) not in waited:
                    found.append(("complete", (m, part, not any(of == m for of, _ in waited))))
                    waited.append((m, part))
            return found

        def spread(acts):
            found = []
            for kind, unit in acts:
                m = self.number(unit[1]) if kind == "fetch" else None
                if m is not None:
                    found += waits((m, part) for part in range(self.splits[m]))
                found.append((kind, unit))
            return found

        full = []
        for stage, (before, ticks) in zip(self.stages, plans):
            before = spread(before) + waits(self.parts_of(stage))
            full.append((before, {tick: spread(ticks[tick]) for tick in sorted(ticks)}))
        every = [(m, part) for m, split in enumerate(self.splits) for part in range(split)]
        return full, spread(left) + waits(every)

    def parts_of(self, stage):
        found = []
        for mat, part in stage["needs"]:
            m = self.number(mat)
            if m is not None:
                found += [(m, part)] if part is not None else [(m, each) for each in range(self.splits[m])]
        return found

    def run(self):
        given = []
        for stage in self.stages:
            for array, spec in stage["ins"] + [(mat, ANY) for mat in stage["held"].values()]:
                if not isinstance(array, Later) and not any(array is g for g, _ in given):
                    given.append((array, SCALAR if spec is SCALAR else ANY))
        given += [(array, ANY) for arrays in self.loads.values() for array in arrays]
        results = self.wholes + [r for stage in self.stages for r in stage["results"]]
        results += [r for sums in self.sums.values() for r in sums]
        plans, left = self.schedule()
        units = sum(self.splits)

        def kernel(*refs):
            refs = list(refs)
            owns = refs[: len(self.owns)]
            of = {}
            for (array, _), ref in zip(given, refs[len(self.owns) :]):
                of[id(array)] = ref
            rest = refs[len(self.owns) + len(given) :]
            for result, ref in zip(results, rest):
                of[id(result)] = ref
            rest = rest[len(results) :]
            place = Place()
            gather = None
            if self.owns:
                gather = Gather(place, owns, [of[id(w)] for w in self.wholes], self.splits, *rest[:3])
                rest = rest[3:]
            sums = {}
            for name, whole in self.sums.items():
                tallies = [*rest[11:13], of[id(whole[2])]] if len(whole) > 2 else None
                sums[name] = Reduce(
                    place, rest[:2], rest[2:4], rest[4:6], rest[6:8], [of[id(w)] for w in whole[:2]],
                    rest[8:11], tallies,
                )
                rest = rest[13:] if tallies else rest[11:]
            held = {slot: (rest[2 * at], rest[2 * at + 1]) for at, slot in enumerate(HELD)}
            place.meet()
            if gather:
                gather.begin()

            def act(kind, unit):
                if kind == "step":
                    sums[unit[0]].step(unit[1])
                elif kind == "fetch":
                    slot, mat = unit
                    Fetch(of[id(mat)], *held[slot], 1).start()
                elif kind == "complete":
                    gather.complete(*unit)
                elif kind == "load":
                    first, second = (of[id(array)] for array in self.loads[unit])
                    into, rows = sums[unit], SHAPES[1][0]
                    pairs = [(first, into.totals[0]), (second.at[pl.ds(0, rows), :], into.totals[1])]
                    pairs.append((second.at[pl.ds(rows, 8), :], into.tallies[0].at[0]))
                    copies = [
                        pltpu.make_async_copy(source, goal, into.locals.at[at])
                        for at, (source, goal) in enumerate(pairs)
                    ]
                    for copy in copies:
                        copy.start()
                    for copy in copies:
                        copy.wait()
                else:
                    getattr(gather, kind)(unit)

            present = {}
            for stage, (before, ticks) in zip(self.stages, plans):
                for kind, unit in before:
                    act(kind, unit)
                for slot, mat in stage["held"].items():
                    if present.get(slot) is not mat:
                        Fetch(of[id(mat)], *held[slot], 1).copy(0).wait()
                        present[slot] = mat
                self.run_stage(stage, ticks, act, of, sums, held)
            for kind, unit in left:
                act(kind, unit)
            if gather:
                gather.finish()
            for each in sums.values():
                each.finish()

        ports = []
        if self.owns:
            ports = [pltpu.SemaphoreType.DMA((units, 7)), pltpu.SemaphoreType.DMA((units, 7))]
            ports.append(pltpu.SemaphoreType.DMA((len(self.owns),)))
        buffers = []
        for whole in self.sums.values():
            for kind, share in ((F32, 1), (BF16, 1), (BF16, 1), (BF16, 32)):
                buffers += [pltpu.VMEM((rows // share, width), kind) for rows, width in SHAPES]
            buffers += [pltpu.SemaphoreType.DMA((3, LEVELS, 2)), pltpu.SemaphoreType.DMA((3, LEVELS, 2))]
            buffers.append(pltpu.SemaphoreType.DMA((3,)))
            if len(whole) > 2:
                buffers.append(pltpu.VMEM((LEVELS + 1, 8, 1024), F32))
                buffers.append(pltpu.VMEM((LEVELS, 8, 1024), F32))

        for shape in HELD.values():
            buffers += [pltpu.VMEM(shape, BF16), pltpu.SemaphoreType.DMA((1,))]

        out = pl.pallas_call(
            kernel,
            in_specs=[ANY] * len(self.owns) + [spec for _, spec in given],
            out_specs=[ANY] * len(results),
            scratch_shapes=[*ports, *buffers],
            out_shape=[jax.ShapeDtypeStruct(r.shape, r.dtype) for r in results],
            compiler_params=pltpu.CompilerParams(
                vmem_limit_bytes=VMEM_BYTES, collective_id=self.collective, has_side_effects=True
            ),
            name=self.name,
        )(*self.owns, *[array for array, _ in given])
        arrays = {id(result): array for result, array in zip(results, out)}
        return lambda later: arrays[id(later)]

    def run_stage(self, stage, ticks, act, of, sums, held):
        ins, outs = stage["ins"], stage["outs"]
        piped = [at for at, (_, spec) in enumerate(ins) if spec is not ANY and spec is not SCALAR]
        fixed = {at: of[id(a)] for at, (a, _) in enumerate(ins) if at not in piped}

        def poll(slot):
            for (step, at), todo in ticks.items():
                if at == slot:

                    @pl.when(pl.program_id(0) == step)
                    def _(todo=todo):
                        for kind, unit in todo:
                            act(kind, unit)

        poll.sums = sums.get(stage["sums"])
        poll.held = held

        def scoped(*scratch):
            if stage["prepare"]:
                stage["prepare"]([fixed.get(at) for at in range(len(ins))], scratch)

            def body(*blocks):
                in_refs = [fixed.get(at) for at in range(len(ins))]
                for at, ref in zip(piped, blocks):
                    in_refs[at] = ref
                stage["body"](in_refs, list(blocks[len(piped) :]), scratch, poll)

            pltpu.emit_pipeline(
                body,
                grid=stage["grid"],
                in_specs=[ins[at][1] for at in piped],
                out_specs=[spec for _, _, spec in outs],
            )(*[of[id(ins[at][0])] for at in piped], *[of[id(r)] for r in stage["results"]])

        pl.run_scoped(scoped, *stage["scratch"])


def launch(
    body, name, grid, ins, outs, scratch, flops, moved, recorder=None, prepare=None, needs=(),
    slots=1, time=1.0, sums=None, held=(),
):
    if recorder is not None:
        return recorder.add(
            body=body, grid=grid, ins=ins, outs=outs, scratch=scratch, prepare=prepare, needs=needs,
            slots=slots, time=time, sums=sums, held=dict(held),
        )

    def kernel(*refs):
        in_refs, out_refs = list(refs[: len(ins)]), list(refs[len(ins) : len(ins) + len(outs)])
        rest = refs[len(ins) + len(outs) :]
        if prepare:

            @pl.when(pl.program_id(0) == 0)
            def _():
                prepare(in_refs, rest)

        body(in_refs, out_refs, rest, lambda slot: None)

    return pl.pallas_call(
        kernel,
        grid=grid,
        in_specs=[spec for _, spec in ins],
        out_specs=[spec for _, _, spec in outs],
        scratch_shapes=scratch,
        out_shape=[jax.ShapeDtypeStruct(s, d) for s, d, _ in outs],
        compiler_params=pltpu.CompilerParams(vmem_limit_bytes=VMEM_BYTES),
        cost_estimate=pl.CostEstimate(flops=flops, bytes_accessed=moved, transcendentals=0),
        name=name,
    )(*[a for a, _ in ins])


class Ready:
    def __init__(self, whole):
        self.whole = whole

    def wait(self, chunk):
        pass

    def wait_all(self):
        pass


def staged_call(body, name, grid, limit, mats, ins, outs, scratch=(), flops=0, part=None, slots_of=(), **record):
    held = dict(zip(slots_of, (mat for mat, _ in mats))) if record else {}
    own = mats[len(held) :]
    holders = []
    for mat, chunks in own:
        rows, width = mat.shape
        holders.append(pltpu.VMEM((rows, width if part is None else width // 3), mat.dtype))
        holders.append(pltpu.SemaphoreType.DMA((chunks,)))
    given = [mat for mat, _ in own]

    def fetches(in_refs, rest):
        return [
            Fetch(
                in_refs[1 + at], rest[2 * at], rest[2 * at + 1], chunks,
                0 if part is None else part * mat.shape[1] // 3,
            )
            for at, (mat, chunks) in enumerate(own)
        ]

    def prepare(in_refs, rest):
        for fetch in fetches(in_refs, rest):
            fetch.start()

    def staged(in_refs, out_refs, rest, poll):
        ready = [Ready(poll.held[slot][0]) for slot in held]
        args = (in_refs[0], ready + fetches(in_refs, rest), in_refs[1 + len(given) :], out_refs)
        body(*args, rest[2 * len(own) :], poll)

    moved = sum(a.size * a.dtype.itemsize for a in given)
    moved += sum(a.size * a.dtype.itemsize for a, _ in ins)
    moved += sum(math.prod(s) * jnp.dtype(d).itemsize for s, d, _ in outs)
    if record:
        record = dict(record, needs=[(mat, part) for mat in given], held=held)
    return launch(
        staged,
        name,
        grid,
        [(limit, SCALAR)] + [(mat, ANY) for mat in given] + list(ins),
        outs,
        [*holders, *scratch],
        flops,
        moved,
        prepare=prepare,
        **record,
    )


def project(name, limit, rows_in, mat, chunks, part=None, **record):
    total, depth = rows_in.shape
    width = mat.shape[1] if part is None else mat.shape[1] // 3
    block = min(256, total)
    step = width // chunks

    def body(limit, fetches, ins, outs, extra, poll):
        (fetch,) = fetches
        left = ins[0][...]
        for chunk in range(chunks):
            poll(chunk)
            fetch.wait(chunk)
            columns = slice(chunk * step, (chunk + 1) * step)
            outs[0][:, columns] = nn(left, fetch.whole[:, columns]).astype(BF16)

    return staged_call(
        body,
        name,
        (total // block,),
        limit,
        [(mat, chunks)],
        [(rows_in, rows_spec(block, depth))],
        [((total, width), BF16, rows_spec(block, width))],
        flops=2 * total * depth * width,
        part=part,
        **record,
    )[0]


def attend(name, limit, queries, keys, values, causal, **record):
    q_len, k_len = queries[0].shape[0], keys[0].shape[0]
    pairs = 1024 // PAIR
    step = min(512, q_len)

    def body(ins, outs, extra, poll):
        poll(0)
        limit_ref, q_ref, k_ref, v_ref = ins
        e_ref, o_ref, inv_ref = outs
        lanes = lax.broadcasted_iota(jnp.int32, (1, PAIR), 1)
        places = lax.broadcasted_iota(jnp.int32, (k_len, 1), 0)
        bias = jnp.where(places < limit_ref[0], 0.0, -1000000000.0)
        q_two = q_ref[...].astype(F32) * (1.0 / math.sqrt(HEAD))
        k_two = k_ref[...].astype(F32)
        v_two = v_ref[...].astype(F32)
        q_own, k_own, v_own = [], [], []
        for half in range(2):
            own = (lanes >= HEAD * half) & (lanes < HEAD * (half + 1))
            spare = lanes == HEAD * (1 - half)
            q_own.append(jnp.where(own, q_two, jnp.where(spare, 1.0, 0.0)).astype(BF16))
            k_own.append(jnp.where(own, k_two, jnp.where(spare, bias, 0.0)).astype(BF16))
            v_own.append(jnp.where(own, v_two, jnp.where(spare, 1.0, 0.0)).T.astype(BF16))

        def score(half, start):
            scores = nt(k_own[half], q_own[half][start : start + step])
            if causal:
                shape = (k_len, step)
                key_at = lax.broadcasted_iota(jnp.int32, shape, 0)
                query_at = lax.broadcasted_iota(jnp.int32, shape, 1) + start
                scores = jnp.where(key_at <= query_at, scores, -1000000000.0)
            return scores

        blocks = [(half, start) for half in range(2) for start in range(0, q_len, step)]
        parts = [[], []]
        scores = score(*blocks[0])
        for at, (half, start) in enumerate(blocks):
            later = score(*blocks[at + 1]) if at + 1 < len(blocks) else None
            highest = jnp.max(scores, axis=0, keepdims=True)
            weights = jnp.exp(scores - highest).astype(BF16)
            e_ref[0, :, half * q_len + start : half * q_len + start + step] = weights
            parts[half].append(nn(v_own[half], weights))
            scores = later
        mixed = []
        for half in range(2):
            out = jnp.concatenate(parts[half], axis=1) if len(parts[half]) > 1 else parts[half][0]
            at = HEAD * (1 - half)
            inverse = 1.0 / out[at : at + 1]
            own_rows = out[HEAD * half : HEAD * (half + 1)]
            mixed.append((own_rows * inverse, jnp.broadcast_to(inverse, own_rows.shape)))
        o_ref[...] = jnp.concatenate([mixed[0][0], mixed[1][0]], axis=0).T.astype(BF16)
        inv_ref[...] = jnp.concatenate([mixed[0][1], mixed[1][1]], axis=0).T

    def columns(rows, first):
        return pl.BlockSpec((rows, PAIR), lambda i: (0, first + i))

    return launch(
        body,
        name,
        (pairs,),
        [
            (limit, SCALAR),
            (queries[0], columns(q_len, queries[1])),
            (keys[0], columns(k_len, keys[1])),
            (values[0], columns(k_len, values[1])),
        ],
        [
            (
                (pairs, k_len, 2 * q_len),
                BF16,
                pl.BlockSpec((1, k_len, 2 * q_len), lambda i: (i, 0, 0)),
            ),
            ((q_len, 1024), BF16, columns(q_len, 0)),
            ((q_len, 1024), F32, columns(q_len, 0)),
        ],
        [],
        16 * pairs * q_len * k_len * PAIR,
        4 * pairs * q_len * k_len,
        **record,
    )


def attend_grad(name, queries, keys, values, weights, mixture, inverse, upstream, **record):
    q_len, k_len = queries[0].shape[0], keys[0].shape[0]
    pairs = 1024 // PAIR
    step = min(256, q_len)
    factor = 1.0 / math.sqrt(HEAD)

    def body(ins, outs, extra, poll):
        q_ref, k_ref, v_ref, e_ref, o_ref, inv_ref, do_ref = ins
        dq_ref, dk_ref, dv_ref = outs
        (ds_ref,) = extra
        poll(0)
        lanes = lax.broadcasted_iota(jnp.int32, (1, PAIR), 1)
        first = lanes < HEAD
        scaled = do_ref[...].astype(F32) * inv_ref[...]
        inner = scaled.astype(BF16).astype(F32) * o_ref[...].astype(F32)
        coarse = inner.astype(BF16)
        fine = (inner - coarse.astype(F32)).astype(BF16)
        picks = lax.broadcasted_iota(jnp.int32, (8, PAIR), 1)
        ones = [
            jnp.where(picks < HEAD, 1.0, 0.0).astype(BF16),
            jnp.where(picks < HEAD, 0.0, 1.0).astype(BF16),
        ]
        delta = [(nt(one, coarse) + nt(one, fine))[0:1] for one in ones]
        do_two = jnp.concatenate(
            [jnp.where(first, scaled, 0.0).astype(BF16), jnp.where(first, 0.0, scaled).astype(BF16)],
            axis=0,
        )
        q_all = q_ref[...].astype(F32) * factor
        q_two = jnp.concatenate(
            [jnp.where(first, q_all, 0.0).astype(BF16), jnp.where(first, 0.0, q_all).astype(BF16)],
            axis=0,
        )
        k_flip = k_ref[...].astype(F32).T.astype(BF16)
        v_all = v_ref[...]
        for half in range(2):
            for start in range(0, q_len, step):
                at = half * q_len + start
                probs_grad = nt(v_all, do_two[at : at + step])
                held = e_ref[0, :, at : at + step].astype(F32)
                ds_ref[:, at : at + step] = (
                    held * (probs_grad - delta[half][:, start : start + step])
                ).astype(BF16)
        dv_ref[...] = nn(e_ref[0], do_two).astype(BF16)
        dk_ref[...] = nn(ds_ref[...], q_two).astype(BF16)
        turned = nn(k_flip, ds_ref[...]) * factor
        rows = lax.broadcasted_iota(jnp.int32, (PAIR, 1), 0)
        dq_ref[...] = jnp.where(rows < HEAD, turned[:, :q_len], turned[:, q_len:]).T.astype(BF16)

    def columns(rows, at):
        return pl.BlockSpec((rows, PAIR), lambda i: (0, at + i))

    return launch(
        body,
        name,
        (pairs,),
        [
            (queries[0], columns(q_len, queries[1])),
            (keys[0], columns(k_len, keys[1])),
            (values[0], columns(k_len, values[1])),
            (weights, pl.BlockSpec((1, k_len, 2 * q_len), lambda i: (i, 0, 0))),
            (mixture, columns(q_len, 0)),
            (inverse, columns(q_len, 0)),
            (upstream, columns(q_len, 0)),
        ],
        [
            ((q_len, 1024), BF16, columns(q_len, 0)),
            ((k_len, 1024), BF16, columns(k_len, 0)),
            ((k_len, 1024), BF16, columns(k_len, 0)),
        ],
        [pltpu.VMEM((k_len, 2 * q_len), BF16)],
        32 * pairs * q_len * k_len * PAIR,
        4 * pairs * q_len * k_len,
        **record,
    )


def row_mask(limit, block):
    at = lax.broadcasted_iota(jnp.int32, (block, 1), 0) + pl.program_id(0) * block
    return (at < limit).astype(F32)


def add_squares(ref, row, entries, mask):
    sums = jnp.sum(entries * entries * mask, axis=0, keepdims=True)
    first = pl.program_id(0) == 0

    @pl.when(first)
    def _():
        ref[row : row + 1, :] = sums

    @pl.when(jnp.logical_not(first))
    def _():
        ref[row : row + 1, :] += sums


def spread_lanes(column):
    return jnp.broadcast_to(column, (column.shape[0], 128))


def out_norm(name, limit, mixture, residual, gain, mat, next_mat=None, residual_gain=None, **record):
    total, width = mixture.shape
    block = min(256, total)
    mats = [(mat, 1)] + ([] if next_mat is None else [(next_mat, 1)])

    def body(limit, fetches, ins, outs, extra, poll):
        poll(0)
        o_ref, r_ref, g_ref, rg_ref = ins
        fetches[0].wait_all()
        added = nn(o_ref[...], fetches[0].whole[...])
        base = r_ref[...].astype(F32)
        if residual_gain is not None:
            base = base * rg_ref[...]
        unit, inverse = standardize(base + added)
        outs[0][...] = unit.astype(BF16)
        outs[1][...] = spread_lanes(inverse)
        add_squares(outs[2], 0, added, row_mask(limit[0], block))
        if next_mat is not None:
            fetches[1].wait_all()
            hidden = (unit * g_ref[...]).astype(BF16)
            outs[3][...] = nn(hidden, fetches[1].whole[...]).astype(BF16)

    outs = [
        ((total, width), BF16, rows_spec(block, width)),
        ((total, 128), F32, rows_spec(block, 128)),
        ((8, width), F32, whole_spec((8, width))),
    ]
    if next_mat is not None:
        outs.append(((total, width), BF16, rows_spec(block, width)))
    return staged_call(
        body,
        name,
        (total // block,),
        limit,
        mats,
        [
            (mixture, rows_spec(block, width)),
            (residual, rows_spec(block, width)),
            (gain, whole_spec((1, width))),
            (gain if residual_gain is None else residual_gain, whole_spec((1, width))),
        ],
        outs,
        flops=2 * total * width * width * len(mats),
        **record,
    )


def branch(name, limit, unit, gain, gain_out, w_in, w_back, down_low, up_low, **record):
    total, width = unit.shape
    hidden_units = w_in.shape[1]
    adapter = down_low.shape[1]
    block = min(256, total)
    chunks = 4
    step = hidden_units // chunks

    def body(limit, fetches, ins, outs, extra, poll):
        u_ref, g_ref, go_ref, ad_ref, au_ref = ins
        y_ref, unit_ref, inv_ref, slope_ref, wa_ref, ad_slope_ref, sq_ref = outs
        (act,) = extra
        first, second = fetches
        hidden = u_ref[...].astype(F32) * g_ref[...]
        low = hidden.astype(BF16)
        pre = nn(low, ad_ref[...].astype(BF16))
        gate = jax.nn.sigmoid(pre)
        wa = (pre * gate).astype(BF16)
        wa_ref[...] = wa
        ad_slope_ref[...] = (gate * (1.0 + pre * (1.0 - gate))).astype(BF16)
        adapted = 4.0 * nn(wa, au_ref[...].astype(BF16))
        for chunk in range(chunks):
            if chunk % 2 == 0:
                poll(chunk // 2)
            first.wait(chunk)
            columns = slice(chunk * step, (chunk + 1) * step)
            fp = nn(low, first.whole[:, columns])
            cdf = 0.5 * (1.0 + lax.erf(fp * (1.0 / math.sqrt(2.0))))
            act[:, columns] = (fp * cdf).astype(BF16)
            bell = jnp.exp(-0.5 * fp * fp) * (1.0 / math.sqrt(2.0 * math.pi))
            slope_ref[:, columns] = (cdf + fp * bell).astype(BF16)
        second.wait_all()
        added = nn(act[...], second.whole[...]) + adapted
        out_unit, inverse = standardize(hidden + added)
        result = out_unit * go_ref[...]
        y_ref[...] = result.astype(BF16)
        unit_ref[...] = out_unit.astype(BF16)
        inv_ref[...] = spread_lanes(inverse)
        mask = row_mask(limit[0], block)
        add_squares(sq_ref, 0, added, mask)
        add_squares(sq_ref, 1, result, mask)

    return staged_call(
        body,
        name,
        (total // block,),
        limit,
        [(w_in, chunks), (w_back, 1)],
        [
            (unit, rows_spec(block, width)),
            (gain, whole_spec((1, width))),
            (gain_out, whole_spec((1, width))),
            (down_low, whole_spec(down_low.shape)),
            (up_low, whole_spec(up_low.shape)),
        ],
        [
            ((total, width), BF16, rows_spec(block, width)),
            ((total, width), BF16, rows_spec(block, width)),
            ((total, 128), F32, rows_spec(block, 128)),
            ((total, hidden_units), BF16, rows_spec(block, hidden_units)),
            ((total, adapter), BF16, rows_spec(block, adapter)),
            ((total, adapter), BF16, rows_spec(block, adapter)),
            ((8, width), F32, whole_spec((8, width))),
        ],
        scratch=[pltpu.VMEM((block, hidden_units), BF16)],
        flops=4 * total * width * (hidden_units + adapter),
        slots_of=("within", "back"),
        **record,
    )


def adapter_grad(upstream, refs):
    (uo_ref, io_ref, go_ref, ui_ref, gi_ref, wa_ref, as_ref, ad_ref, au_ref) = refs
    grad_two = standardize_grad(uo_ref[...].astype(F32), io_ref[:, 0:1], upstream * go_ref[...])
    dvd = (4.0 * grad_two).astype(BF16)
    low = (ui_ref[...].astype(F32) * gi_ref[...]).astype(BF16)
    du = (nt(dvd, au_ref[...].astype(BF16)) * as_ref[...].astype(F32)).astype(BF16)
    total = grad_two + nt(du, ad_ref[...].astype(BF16))
    return grad_two.astype(BF16), total, tn(low, du), tn(wa_ref[...], dvd)


def hidden_grad(dz, total, fetches, refs, dfp, chunks, poll=lambda slot: None):
    slope_ref, ui_ref, ii_ref, gi_ref = refs
    back, within, last = fetches
    step = dfp.shape[1] // chunks
    back.wait_all()
    poll(0)
    for chunk in range(chunks):
        columns = slice(chunk * step, (chunk + 1) * step)
        act_grad = nt(dz, back.whole[columns, :])
        dfp[:, columns] = (act_grad * slope_ref[:, columns].astype(F32)).astype(BF16)
    within.wait_all()
    poll(1)
    total = total + nt(dfp[...], within.whole[...])
    grad_one = standardize_grad(ui_ref[...].astype(F32), ii_ref[:, 0:1], total * gi_ref[...])
    last.wait_all()
    return grad_one, nt(grad_one.astype(BF16), last.whole[...]).astype(BF16)


def dec_branch_grad(
    name, limits, cot, saved_out, gain_out, saved_in, gain_in, slope, wa, ad_slope,
    w_back, w_in, w_out, down_low, up_low, squares, **record,
):
    total, width = cot.shape
    hidden_units = w_in.shape[1]
    adapter = down_low.shape[1]
    whole = [
        cot, saved_out[0], saved_out[1], gain_out, saved_in[0], gain_in, wa, ad_slope, down_low,
        up_low, slope, saved_in[1], *squares,
    ]

    def body(limit, fetches, ins, outs, extra, poll):
        grad_ref, mix_ref = outs[:2]
        if record:
            (down_ref, up_ref), tally_ref = poll.sums.totals, poll.sums.tallies[0].at[0]
        else:
            down_ref, up_ref, tally_ref = outs[2], outs[3].at[:adapter], outs[3].at[adapter:]
        (other,), cot_ref, slope_ref, ii_ref = ins[:1], ins[1], ins[11], ins[12]
        dz, part, down_ref[...], up_ref[...] = adapter_grad(cot_ref[...].astype(F32), ins[2:11])
        sums = [ref[row : row + 1, :] for ref, rows in zip(ins[13:], (1, 2, 1, 1, 2)) for row in range(rows)]
        lanes = lax.broadcasted_iota(jnp.int32, (1, width), 1)
        counts = jnp.where(lanes == 0, limit[0], jnp.where(lanes == 1, other[0], 0)).astype(F32)
        tally_ref[...] = jnp.concatenate([*sums, counts], axis=0)
        grad_ref[...], mix_ref[...] = hidden_grad(
            dz, part, fetches, (slope_ref, ins[5], ii_ref, ins[6]), extra[0], 4
        )

    return staged_call(
        body,
        name,
        (1,),
        limits[0],
        [(w_back, 1), (w_in, 1), (w_out, 1)],
        [(limits[1], SCALAR)] + [(a, whole_spec(a.shape)) for a in whole],
        [
            (cot.shape, F32, whole_spec(cot.shape)),
            (cot.shape, BF16, whole_spec(cot.shape)),
        ]
        + [
            (shape, F32, whole_spec(shape))
            for shape in (() if record else (down_low.shape, (adapter + 8, width)))
        ],
        scratch=[pltpu.VMEM((total, hidden_units), BF16)],
        flops=4 * total * width * (hidden_units + 2 * adapter),
        slots_of=("back", "within"),
        **record,
    )


def enc_adapter_grad(
    name, limit, cot, cross, cross_mat, saved_out, gain_out, saved_in, gain_in, wa, ad_slope,
    down_low, up_low, **record,
):
    total, width = cot.shape
    adapter = down_low.shape[1]
    block = min(256, total)
    rows = rows_spec(block, width)

    def body(limit, fetches, ins, outs, extra, poll):
        poll(0)
        dz_ref, part_ref = outs[:2]
        down_sum, up_sum = poll.sums.totals if record else extra
        fetches[0].wait_all()
        upstream = ins[0][...].astype(F32)
        for at in range(2):
            upstream = upstream + nt(ins[1 + at][...], fetches[0].whole[:, at * width : (at + 1) * width])
        dz_ref[...], part_ref[...], down_part, up_part = adapter_grad(upstream, ins[3:])
        at = pl.program_id(0)

        @pl.when(at == 0)
        def _():
            up_sum[...] = up_part
            down_sum[...] = down_part

        @pl.when(at > 0)
        def _():
            up_sum[...] += up_part
            down_sum[...] += down_part

        if not record:

            @pl.when(at == total // block - 1)
            def _():
                outs[2][...] = down_sum[...].astype(BF16)
                outs[3][...] = up_sum[...].astype(BF16)

    return staged_call(
        body,
        name,
        (total // block,),
        limit,
        [(cross_mat, 1)],
        [
            (cot, rows),
            (cross[0], rows),
            (cross[1], rows),
            (saved_out[0], rows),
            (saved_out[1], rows_spec(block, 128)),
            (gain_out, whole_spec((1, width))),
            (saved_in[0], rows),
            (gain_in, whole_spec((1, width))),
            (wa, rows_spec(block, adapter)),
            (ad_slope, rows_spec(block, adapter)),
            (down_low, whole_spec(down_low.shape)),
            (up_low, whole_spec(up_low.shape)),
        ],
        [
            ((total, width), BF16, rows),
            ((total, width), F32, rows),
        ]
        + [(a.shape, BF16, whole_spec(a.shape)) for a in (() if record else (down_low, up_low))],
        scratch=[pltpu.VMEM(a.shape, F32) for a in (() if record else (down_low, up_low))],
        flops=4 * total * width * (width + 2 * adapter),
        **record,
    )


def enc_hidden_grad(name, limit, dz, part, slope, saved_in, gain_in, w_back, w_in, w_out, **record):
    total, width = dz.shape
    hidden_units = w_in.shape[1]
    block = min(256, total)
    rows = rows_spec(block, width)

    def body(limit, fetches, ins, outs, extra, poll):
        outs[0][...], outs[1][...] = hidden_grad(
            ins[0][...], ins[1][...], fetches, ins[2:], extra[0], 4, poll
        )

    return staged_call(
        body,
        name,
        (total // block,),
        limit,
        [(w_back, 1), (w_in, 1), (w_out, 1)],
        [
            (dz, rows),
            (part, rows),
            (slope, rows_spec(block, hidden_units)),
            (saved_in[0], rows),
            (saved_in[1], rows_spec(block, 128)),
            (gain_in, whole_spec((1, width))),
        ],
        [((total, width), F32, rows), ((total, width), BF16, rows)],
        scratch=[pltpu.VMEM((block, hidden_units), BF16)],
        flops=4 * total * width * hidden_units,
        slots_of=("back", "within"),
        **record,
    )


def middle_grad(name, limit, grad_cross, dq, saved, gain, w_cq, w_so, **record):
    total, width = dq.shape
    block = min(256, total)
    unit, inv = saved

    def body(limit, fetches, ins, outs, extra, poll):
        poll(0)
        gc_ref, dq_ref, u_ref, i_ref, g_ref = ins
        fetches[0].wait_all()
        hidden_grad = gc_ref[...] + nt(dq_ref[...], fetches[0].whole[...])
        grad_self = standardize_grad(
            u_ref[...].astype(F32), i_ref[:, 0:1], hidden_grad * g_ref[...]
        )
        outs[0][...] = grad_self
        fetches[1].wait_all()
        outs[1][...] = nt(grad_self.astype(BF16), fetches[1].whole[...]).astype(BF16)

    return staged_call(
        body,
        name,
        (total // block,),
        limit,
        [(w_cq, 1), (w_so, 1)],
        [
            (grad_cross, rows_spec(block, width)),
            (dq, rows_spec(block, width)),
            (unit, rows_spec(block, width)),
            (inv, rows_spec(block, 128)),
            (gain, whole_spec((1, width))),
        ],
        [
            ((total, width), F32, rows_spec(block, width)),
            ((total, width), BF16, rows_spec(block, width)),
        ],
        flops=4 * total * width * width,
        **record,
    )


def input_grad(name, limit, base, parts, mat, narrow=(), tally=None):
    total, width = base.shape
    block = min(256, total)
    steps = total // block
    count = len(parts)

    def body(limit, fetches, ins, outs, extra, poll):
        (fetch,) = fetches
        result = ins[0][...]
        for at in range(count):
            fetch.wait(at)
            result = result + nt(ins[1 + at][...], fetch.whole[:, at * width : (at + 1) * width])
        outs[0][...] = result
        for at in range(len(narrow)):
            outs[1 + at][...] = ins[1 + count + at][...].astype(F32)
        if tally is not None:
            rows = ins[-1][...]
            at = lax.broadcasted_iota(jnp.int32, (8, 1), 0)
            numbers = jnp.where(at < 3, rows[7:8, 0:1], rows[7:8, 1:2])
            outs[-1][...] = spread_lanes(
                jnp.sqrt(jnp.sum(rows, axis=1, keepdims=True) / (numbers * width))
            )

    slices = [(a, rows_spec(a.shape[0] // steps, a.shape[1])) for a in narrow]
    tallies = [] if tally is None else [(tally, whole_spec(tally.shape))]
    return staged_call(
        body,
        name,
        (steps,),
        limit,
        [(mat, count)],
        [(base, rows_spec(block, width))] + [(p, rows_spec(block, width)) for p in parts] + slices + tallies,
        [((total, width), F32, rows_spec(block, width))]
        + [(a.shape, F32, spec) for a, spec in slices]
        + [((8, 128), F32, whole_spec((8, 128))) for _ in tallies],
        flops=2 * total * width * width * count,
    )


NAMES = (
    "enc_qkv",
    "enc_attn_out",
    "enc_ffn_in",
    "enc_ffn_out",
    "dec_self_qkv",
    "dec_self_out",
    "dec_cross_q",
    "dec_cross_kv",
    "dec_cross_out",
    "dec_ffn_in",
    "dec_ffn_out",
)


def layers(enc_limit, dec_limit, enc_input, dec_input, enc_cot, dec_cot, blocks, hosting, fsdp, gains, adapters):
    gain = [gains[k : k + 1] for k in range(5)]
    enc_down, enc_up, dec_down, dec_up = adapters
    if hosting:
        recorder = Recorder("forward", 1, blocks, fsdp)
        w = dict(zip(recorder.names, recorder.wholes))
    else:
        recorder = None
        w = {name: lax.all_gather(b, "fsdp", axis=0, tiled=True) for name, b in blocks.items()}

    def at(slots, time, sums=None):
        if not hosting:
            return {}
        return {"recorder": recorder, "slots": slots, "time": time, "sums": sums}

    enc_q, enc_k, enc_v = (
        project("enc_project", enc_limit, enc_input, w["enc_qkv"], 1, part, **at(1, 5.0))
        for part in range(3)
    )
    e_enc, o_enc, inv_enc = attend(
        "enc_attend", enc_limit, (enc_q, 0), (enc_k, 0), (enc_v, 0), False, **at(1, 34.0)
    )
    unit1, dev1, sq_a = out_norm(
        "enc_out_norm", enc_limit, o_enc, enc_input, gain[0], w["enc_attn_out"], **at(1, 9.0)
    )
    enc_out, unit2, dev2, slope_e, wa_e, ads_e, sq_b = branch(
        "enc_branch", enc_limit, unit1, gain[0], gain[1], w["enc_ffn_in"], w["enc_ffn_out"],
        enc_down, enc_up, **at(2, 33.0),
    )
    sqkv = project("dec_project", dec_limit, dec_input, w["dec_self_qkv"], 3, **at(3, 6.0))
    e_self, o_self, inv_self = attend(
        "dec_attend", dec_limit, (sqkv, 0), (sqkv, 8), (sqkv, 16), True, **at(1, 8.5)
    )
    unit3, dev3, sq_c, cross_q = out_norm(
        "dec_out_norm", dec_limit, o_self, dec_input, gain[2], w["dec_self_out"], w["dec_cross_q"],
        **at(1, 5.3),
    )
    kv = project("cross_project", enc_limit, enc_out, w["dec_cross_kv"], 2, **at(2, 9.5))
    e_cross, o_cross, inv_cross = attend(
        "cross_attend", enc_limit, (cross_q, 0), (kv, 0), (kv, 8), False, **at(1, 14.0)
    )
    if hosting:
        value = recorder.run()
        w = {name: value(mat) for name, mat in w.items()}
        enc_q, enc_k, enc_v, e_enc, o_enc, inv_enc = map(value, (enc_q, enc_k, enc_v, e_enc, o_enc, inv_enc))
        unit1, dev1, sq_a = map(value, (unit1, dev1, sq_a))
        enc_out, unit2, dev2, slope_e, wa_e, ads_e, sq_b = map(
            value, (enc_out, unit2, dev2, slope_e, wa_e, ads_e, sq_b)
        )
        sqkv, e_self, o_self, inv_self = map(value, (sqkv, e_self, o_self, inv_self))
        unit3, dev3, sq_c, cross_q = map(value, (unit3, dev3, sq_c, cross_q))
        kv, e_cross, o_cross, inv_cross = map(value, (kv, e_cross, o_cross, inv_cross))
        recorder = Recorder("encoder_grad", 2, {}, fsdp)
    unit4, dev4, sq_d = out_norm(
        "cross_out_norm", dec_limit, o_cross, unit3, gain[3], w["dec_cross_out"], residual_gain=gain[2]
    )
    dec_out, unit5, dev5, slope_d, wa_d, ads_d, sq_e = branch(
        "dec_branch", dec_limit, unit4, gain[3], gain[4], w["dec_ffn_in"], w["dec_ffn_out"],
        dec_down, dec_up,
    )
    grad_cross, do_cross, *dec_grads = dec_branch_grad(
        "dec_branch_grad", (enc_limit, dec_limit), dec_cot, (unit5, dev5), gain[4], (unit4, dev4), gain[3],
        slope_d, wa_d, ads_d, w["dec_ffn_out"], w["dec_ffn_in"], w["dec_cross_out"], dec_down, dec_up,
        (sq_a, sq_b, sq_c, sq_d, sq_e),
    )
    dcq, dck, dcv = attend_grad(
        "cross_attend_grad", (cross_q, 0), (kv, 0), (kv, 8), e_cross, o_cross, inv_cross, do_cross
    )
    if hosting:
        dec_sums = recorder.reduce("dec", True)
        recorder.load("dec", dec_grads)
        enc_sums = recorder.reduce("enc", False)
    dz, part, *enc_grads = enc_adapter_grad(
        "enc_adapter_grad", enc_limit, enc_cot, (dck, dcv), w["dec_cross_kv"], (unit2, dev2), gain[1],
        (unit1, dev1), gain[0], wa_e, ads_e, enc_down, enc_up, **at(1, 20.0, "enc"),
    )
    grad_one, do_enc = enc_hidden_grad(
        "enc_hidden_grad", enc_limit, dz, part, slope_e, (unit1, dev1), gain[0],
        w["enc_ffn_out"], w["enc_ffn_in"], w["enc_attn_out"], **at(2, 28.0),
    )
    deq, dek, dev = attend_grad(
        "enc_attend_grad", (enc_q, 0), (enc_k, 0), (enc_v, 0), e_enc, o_enc, inv_enc, do_enc, **at(1, 37.0)
    )
    if hosting:
        value = recorder.run()
        grad_one, deq, dek, dev = map(value, (grad_one, deq, dek, dev))
        *dec_grads, tally = map(value, dec_sums)
        enc_grads = [value(a) for a in enc_sums]
    else:
        everyone = ("fsdp", "dp")
        down, up = lax.psum(dec_grads, everyone)
        dec_grads, tally = [down, up[: dec_up.shape[0]]], up[dec_up.shape[0] :]
        enc_grads = lax.psum(enc_grads, everyone)
    grad_self, do_self = middle_grad(
        "dec_middle_grad", dec_limit, grad_cross, dcq, (unit3, dev3), gain[2], w["dec_cross_q"],
        w["dec_self_out"],
    )
    dsq, dsk, dsv = attend_grad(
        "dec_attend_grad", (sqkv, 0), (sqkv, 8), (sqkv, 16), e_self, o_self, inv_self, do_self
    )
    dec_grad, *dec_grads = input_grad(
        "dec_input_grad", dec_limit, grad_self, [dsq, dsk, dsv], w["dec_self_qkv"], dec_grads
    )
    enc_grad, *enc_grads, rms = input_grad(
        "enc_input_grad", enc_limit, grad_one, [deq, dek, dev], w["enc_qkv"], enc_grads, tally
    )
    return enc_out, dec_out, enc_grad, dec_grad, *enc_grads, *dec_grads, rms[:7, 0]


def shards(fsdp, dp, enc_input, dec_input, enc_cot, dec_cot, *rest):
    mats, (gains, enc_down, enc_up, dec_down, dec_up, enc_lengths, dec_lengths) = rest[:11], rest[11:]
    return layers(
        enc_lengths, dec_lengths, enc_input, dec_input, enc_cot, dec_cot, dict(zip(NAMES, mats)),
        fsdp == 8 and dp == 4, fsdp, gains, (enc_down, enc_up, dec_down, dec_up),
    )


def solution(mesh):
    by_rows = P(("fsdp", "dp"), None)
    placed = (by_rows,) * 4 + (P("fsdp", None),) * 11 + (P(),) * 5 + (P(("fsdp", "dp")),) * 2
    return jax.shard_map(
        functools.partial(shards, mesh.shape["fsdp"], mesh.shape["dp"]),
        mesh=mesh,
        in_specs=placed,
        out_specs=(by_rows,) * 4 + (P(),) * 5,
        check_vma=False,
    )
```

```python
import functools
import math
import types

import jax
import jax.numpy as jnp
from jax import lax
from jax.experimental import pallas as pl
from jax.experimental.pallas import tpu as pltpu
from jax.sharding import PartitionSpec as P

HEAD = 64
PAIR = 2 * HEAD
EPSILON = 1e-05
F32 = jnp.float32
BF16 = jnp.bfloat16
VMEM_BYTES = 58 * 2**20


def nn(former, latter):
    return jnp.dot(former, latter, preferred_element_type=F32)


def nt(former, latter):
    return lax.dot_general(
        former, latter, (((1,), (1,)), ((), ())), preferred_element_type=F32
    )


def tn(former, latter):
    return lax.dot_general(
        former, latter, (((0,), (0,)), ((), ())), preferred_element_type=F32
    )


def standardize(entries):
    centered = entries - jnp.mean(entries, axis=-1, keepdims=True)
    spread = jnp.mean(centered * centered, axis=-1, keepdims=True)
    inverse = lax.rsqrt(spread + EPSILON)
    return centered * inverse, inverse


def standardize_grad(unit, inverse, scaled):
    return inverse * (
        scaled
        - jnp.mean(scaled, axis=-1, keepdims=True)
        - unit * jnp.mean(scaled * unit, axis=-1, keepdims=True)
    )


class Fetch:
    def __init__(self, source, whole, sems, chunks, first=0):
        self.source, self.whole, self.sems, self.chunks = source, whole, sems, chunks
        self.first = first

    def copy(self, chunk):
        width = self.whole.shape[1] // self.chunks
        return pltpu.make_async_copy(
            self.source.at[:, pl.ds(self.first + chunk * width, width)],
            self.whole.at[:, pl.ds(chunk * width, width)],
            self.sems.at[chunk],
        )

    def start(self):
        for chunk in range(self.chunks):
            self.copy(chunk).start()

    def wait(self, chunk):
        @pl.when(pl.program_id(0) == 0)
        def _():
            self.copy(chunk).wait()

    def wait_all(self):
        for chunk in range(self.chunks):
            self.wait(chunk)


UNIT_US = 6.0
LEAD_US = 5.0


class Place:
    def __init__(self):
        f, z = lax.axis_index("fsdp"), lax.axis_index("dp")
        self.core, self.x, self.y = f % 2, (f // 2) % 2, f // 4
        self.odd, self.high = z % 2, z // 2
        self.own = f
        self.twin = {"fsdp": f + 1 - 2 * self.core}
        self.beside = {"fsdp": f + 2 - 4 * self.x}
        self.above = {"fsdp": f + 4 - 8 * self.y}
        self.partner = {"dp": z + 1 - 2 * self.odd}
        self.distant = {"dp": z + 2 - 4 * self.high}

    def meet(self):
        barrier = pltpu.get_barrier_semaphore()
        all_of_them = (self.twin, self.beside, self.above, self.partner, self.distant)
        for to in all_of_them:
            pl.semaphore_signal(barrier, inc=1, device_id=to, device_id_type=pl.DeviceIdType.MESH)
        pl.semaphore_wait(barrier, len(all_of_them))


class Gather:
    def __init__(self, place, owns, wholes, splits, sends, recvs, locals_):
        self.place, self.owns, self.wholes, self.splits = place, owns, wholes, splits
        self.sends, self.recvs, self.locals = sends, recvs, locals_
        self.units = [(m, part) for m, split in enumerate(splits) for part in range(split)]
        beside, above = place.beside["fsdp"], place.above["fsdp"]
        self.own = place.own
        self.direct = beside + place.odd * (above - beside)
        self.onward = above + place.odd * (beside - above)
        self.far = beside + 4 - 8 * place.y

    def transfer(self, unit, kind):
        m, part = self.units[unit]
        whole, own = self.wholes[m], self.owns[m]
        block, width = own.shape
        by_columns = width == 3072
        rows = block if by_columns else block // self.splits[m]
        wide = width // self.splits[m] if by_columns else width
        first_row, columns = (0, pl.ds(part * wide, wide)) if by_columns else (part * rows, pl.ds(0, wide))
        owner = (self.own, self.direct, self.direct, self.own, self.direct, self.far, self.onward)[kind]
        there = whole.at[pl.ds(pl.multiple_of(owner * block + first_row, 16), rows), columns]
        here = own.at[pl.ds(first_row, rows), columns] if kind in (0, 3) else there
        to = self.place.twin if kind >= 3 else self.place.partner
        if kind < 2:
            to = {"fsdp": (self.direct, self.onward)[kind]}
        return pltpu.make_async_remote_copy(
            src_ref=here,
            dst_ref=there,
            send_sem=self.sends.at[unit, kind],
            recv_sem=self.recvs.at[unit, kind],
            device_id=to,
            device_id_type=pl.DeviceIdType.MESH,
        )

    def keep(self, m):
        block = self.owns[m].shape[0]
        rows = pl.ds(pl.multiple_of(self.own * block, 16), block)
        return pltpu.make_async_copy(self.owns[m], self.wholes[m].at[rows, :], self.locals.at[m])

    def begin(self):
        for unit in range(len(self.units)):
            self.transfer(unit, 0).start()
        for unit in range(len(self.units)):
            self.transfer(unit, 3).start()
        for m in range(len(self.owns)):
            self.keep(m).start()

    def pass_on(self, unit):
        self.transfer(unit, 0).wait_recv()
        for kind in (1, 2, 4):
            self.transfer(unit, kind).start()

    def share(self, unit):
        self.transfer(unit, 1).wait_recv()
        self.transfer(unit, 5).start()
        self.transfer(unit, 2).wait_recv()
        self.transfer(unit, 6).start()

    def complete(self, m, part, first):
        for kind in (3, 4, 5, 6):
            self.transfer(self.units.index((m, part)), kind).wait_recv()
        if first:
            self.keep(m).wait()

    def finish(self):
        for unit in range(len(self.units)):
            for kind in range(7):
                self.transfer(unit, kind).wait_send()


LEVELS = 5
SHAPES = ((1024, 512), (512, 1024))


class Reduce:
    def __init__(self, place, totals, gives, takes, pieces, wholes, sems, tallies=None):
        self.place, self.totals, self.gives, self.takes = place, totals, gives, takes
        self.pieces, self.wholes, self.tallies = pieces, wholes, tallies
        self.sends, self.recvs, self.locals = sems
        p = place
        along = [(p.core, p.twin), (p.x, p.beside), (p.y, p.above), (p.odd, p.partner), (p.high, p.distant)]
        self.ways = [along, [along[0], along[2], along[1], along[3], along[4]]]

    def range(self, part, level):
        rows = SHAPES[part][0]
        first = 0
        for bit, _ in self.ways[part][:level]:
            rows = rows // 2
            first = first + bit * rows
        return first, rows

    def halves(self, part, level):
        first, rows = self.range(part, level)
        bit = self.ways[part][level][0]
        half = rows // 2
        return pl.multiple_of(first + bit * half, half), pl.multiple_of(first + (1 - bit) * half, half), half

    def slot(self, part, level):
        rows = SHAPES[part][0]
        return pl.ds(rows - (rows >> level), rows >> (level + 1))

    def remote(self, src, dst, part, level, back):
        return pltpu.make_async_remote_copy(
            src_ref=src,
            dst_ref=dst,
            send_sem=self.sends.at[part, level, back],
            recv_sem=self.recvs.at[part, level, back],
            device_id=self.ways[part if part < 2 else 0][level][1],
            device_id_type=pl.DeviceIdType.MESH,
        )

    def down(self, part, level):
        rows = self.slot(part, level)
        return self.remote(self.gives[part].at[rows, :], self.takes[part].at[rows, :], part, level, 0)

    def up(self, part, level):
        first, rows = self.range(part, level + 1)
        rows = pl.ds(pl.multiple_of(first, rows), rows)
        return self.remote(self.wholes[part].at[rows, :], self.wholes[part].at[rows, :], part, level, 1)

    def tally(self, level):
        return self.remote(self.tallies[0].at[level], self.tallies[1].at[level], 2, level, 0)

    def piece(self, part):
        first, rows = self.range(part, LEVELS)
        rows = pl.ds(pl.multiple_of(first, rows), rows)
        return pltpu.make_async_copy(self.pieces[part], self.wholes[part].at[rows, :], self.locals.at[part])

    def tally_out(self):
        return pltpu.make_async_copy(self.tallies[0].at[LEVELS], self.tallies[2], self.locals.at[2])

    def step(self, at):
        for part in range(2):
            if 0 < at <= LEVELS:
                keep, _, half = self.halves(part, at - 1)
                self.down(part, at - 1).wait_recv()
                rows = pl.ds(keep, half)
                taken = self.takes[part][self.slot(part, at - 1), :].astype(F32)
                self.totals[part][rows, :] = self.totals[part][rows, :] + taken
            if at < LEVELS:
                _, give, half = self.halves(part, at)
                self.gives[part][self.slot(part, at), :] = self.totals[part][pl.ds(give, half), :].astype(BF16)
                self.down(part, at).start()
            elif at == LEVELS:
                first, rows = self.range(part, LEVELS)
                last = pl.ds(pl.multiple_of(first, rows), rows)
                self.pieces[part][...] = self.totals[part][last, :].astype(BF16)
                self.piece(part).start()
                self.piece(part).wait()
                self.up(part, LEVELS - 1).start()
            else:
                level = 2 * LEVELS - at
                self.up(part, level).wait_recv()
                if level:
                    self.up(part, level - 1).start()
        if self.tallies and at <= LEVELS:
            if at:
                self.tally(at - 1).wait_recv()
                self.tallies[0][at] = self.tallies[0][at - 1] + self.tallies[1][at - 1]
            if at < LEVELS:
                self.tally(at).start()
            else:
                self.tally_out().start()

    def finish(self):
        for level in range(LEVELS):
            for part in range(2):
                self.down(part, level).wait_send()
                self.up(part, level).wait_send()
            if self.tallies:
                self.tally(level).wait_send()
        if self.tallies:
            self.tally_out().wait()


REDUCE_US = (0.0, 5.0, 9.0, 6.5, 6.0, 6.0, 6.0, 6.0, 6.5, 9.0, 5.0)


ANY = pl.BlockSpec(memory_space=pl.ANY)
SCALAR = pl.BlockSpec(memory_space=pltpu.SMEM)


def rows_spec(rows, width):
    return pl.BlockSpec((rows, width), lambda i: (i, 0))


def whole_spec(shape):
    return pl.BlockSpec(shape, lambda i: (0,) * len(shape))


class Later:
    def __init__(self, shape, dtype):
        self.shape, self.dtype = tuple(shape), jnp.dtype(dtype)
        self.size = math.prod(self.shape)


HELD = {"within": (1024, 4096), "back": (4096, 1024)}


class Recorder:
    def __init__(self, name, collective, blocks, fsdp):
        self.name, self.collective = name, collective
        self.loads = {}
        self.names = list(blocks)
        self.owns = list(blocks.values())
        self.wholes = [Later((a.shape[0] * fsdp, a.shape[1]), a.dtype) for a in self.owns]
        self.splits = [max(1, a.size // 131072) for a in self.owns]
        self.stages = []
        self.sums = {}

    def reduce(self, name, tallied):
        self.sums[name] = [Later(shape, BF16) for shape in SHAPES]
        if tallied:
            self.sums[name].append(Later((8, 1024), F32))
        return self.sums[name]

    def load(self, name, arrays):
        self.loads[name] = arrays

    def number(self, mat):
        found = [m for m, whole in enumerate(self.wholes) if whole is mat]
        return found[0] if found else None

    def add(self, **stage):
        stage = types.SimpleNamespace(**stage)
        stage.results = [Later(shape, dtype) for shape, dtype, _ in stage.outs]
        self.stages.append(stage)
        return stage.results

    def schedule(self):
        acts, unit, due = [], 0, LEAD_US
        last_of, come = {}, {}
        for m, split in enumerate(self.splits):
            for part in range(split):
                time = UNIT_US * self.owns[m].size / split / 131072
                due += time
                acts.append((due, "pass_on", unit))
                acts.append((due + time + 2.0, "share", unit))
                last_of[m, part] = unit
                come[m] = due + time + 6.0
                unit += 1
        acts.sort(key=lambda act: act[0])
        clock, plans, started = 0.0, [], []
        for slot in HELD:
            users = [stage for stage in self.stages if slot in stage.held]
            if users:
                mat = users[0].held[slot]
                acts.append((come.get(self.number(mat), 0.0), "fetch", (slot, mat)))
        for name in self.loads:
            started += [("load", name), ("step", (name, 0))]
            due = 0.0
            for at, time in enumerate(REDUCE_US):
                due += time
                if at:
                    acts.append((due, "step", (name, at)))
        acts.sort(key=lambda act: act[0])
        for index, stage in enumerate(self.stages):
            before, ticks = started, {}
            started = []
            needed = [last_of[m, part] for m, part in self.parts_of(stage)]
            if needed:
                while any(act[1] in ("pass_on", "share") and act[2] <= max(needed) for act in acts):
                    clock = max(clock, acts[0][0])
                    before.append(acts.pop(0)[1:])
            while any(act[1] == "fetch" and act[2][1] is stage.held.get(act[2][0]) for act in acts):
                clock = max(clock, acts[0][0])
                before.append(acts.pop(0)[1:])
            pace = stage.time / stage.grid[0] / stage.slots
            for tick in range(stage.grid[0] * stage.slots):
                while acts and acts[0][0] <= clock:
                    ticks.setdefault(divmod(tick, stage.slots), []).append(acts.pop(0)[1:])
                clock += pace
            plans.append((before, ticks))
            for slot in stage.held:
                after = [at for at in range(index + 1, len(self.stages)) if slot in self.stages[at].held]
                if after and self.stages[after[0]].held[slot] is not stage.held[slot]:
                    mat = self.stages[after[0]].held[slot]
                    acts.append((max(clock, come.get(self.number(mat), 0.0)), "fetch", (slot, mat)))
                    acts.sort(key=lambda act: act[0])
            if stage.sums:
                started = [("step", (stage.sums, 0))]
                due = clock
                for at, time in enumerate(REDUCE_US):
                    due += time
                    if at:
                        acts.append((due, "step", (stage.sums, at)))
                acts.sort(key=lambda act: act[0])
        return self.completed(plans, [act[1:] for act in acts])

    def completed(self, plans, left):
        waited = []

        def waits(parts):
            found = []
            for m, part in parts:
                if (m, part) not in waited:
                    found.append(("complete", (m, part, not any(of == m for of, _ in waited))))
                    waited.append((m, part))
            return found

        def spread(acts):
            found = []
            for kind, unit in acts:
                m = self.number(unit[1]) if kind == "fetch" else None
                if m is not None:
                    found += waits((m, part) for part in range(self.splits[m]))
                found.append((kind, unit))
            return found

        full = []
        for stage, (before, ticks) in zip(self.stages, plans):
            before = spread(before) + waits(self.parts_of(stage))
            full.append((before, {tick: spread(ticks[tick]) for tick in sorted(ticks)}))
        every = [(m, part) for m, split in enumerate(self.splits) for part in range(split)]
        return full, spread(left) + waits(every)

    def parts_of(self, stage):
        found = []
        for mat, part in stage.needs:
            m = self.number(mat)
            if m is not None:
                found += [(m, part)] if part is not None else [(m, each) for each in range(self.splits[m])]
        return found

    def run(self):
        given = []
        for stage in self.stages:
            for array, spec in stage.ins + [(mat, ANY) for mat in stage.held.values()]:
                if not isinstance(array, Later) and not any(array is g for g, _ in given):
                    given.append((array, SCALAR if spec is SCALAR else ANY))
        given += [(array, ANY) for arrays in self.loads.values() for array in arrays]
        results = self.wholes + [r for stage in self.stages for r in stage.results]
        results += [r for sums in self.sums.values() for r in sums]
        plans, left = self.schedule()
        units = sum(self.splits)

        def kernel(*refs):
            refs = list(refs)
            owns = refs[: len(self.owns)]
            of = {}
            for (array, _), ref in zip(given, refs[len(self.owns) :]):
                of[id(array)] = ref
            rest = refs[len(self.owns) + len(given) :]
            for result, ref in zip(results, rest):
                of[id(result)] = ref
            rest = rest[len(results) :]
            place = Place()
            gather = None
            if self.owns:
                gather = Gather(place, owns, [of[id(w)] for w in self.wholes], self.splits, *rest[:3])
                rest = rest[3:]
            sums = {}
            for name, whole in self.sums.items():
                tallies = [*rest[11:13], of[id(whole[2])]] if len(whole) > 2 else None
                sums[name] = Reduce(
                    place, rest[:2], rest[2:4], rest[4:6], rest[6:8], [of[id(w)] for w in whole[:2]],
                    rest[8:11], tallies,
                )
                rest = rest[13:] if tallies else rest[11:]
            held = {slot: (rest[2 * at], rest[2 * at + 1]) for at, slot in enumerate(HELD)}
            place.meet()
            if gather:
                gather.begin()

            def act(kind, unit):
                if kind == "step":
                    sums[unit[0]].step(unit[1])
                elif kind == "fetch":
                    slot, mat = unit
                    Fetch(of[id(mat)], *held[slot], 1).start()
                elif kind == "complete":
                    gather.complete(*unit)
                elif kind == "load":
                    first, second = (of[id(array)] for array in self.loads[unit])
                    into, rows = sums[unit], SHAPES[1][0]
                    pairs = [(first, into.totals[0]), (second.at[pl.ds(0, rows), :], into.totals[1])]
                    pairs.append((second.at[pl.ds(rows, 8), :], into.tallies[0].at[0]))
                    copies = [
                        pltpu.make_async_copy(source, goal, into.locals.at[at])
                        for at, (source, goal) in enumerate(pairs)
                    ]
                    for copy in copies:
                        copy.start()
                    for copy in copies:
                        copy.wait()
                else:
                    getattr(gather, kind)(unit)

            present = {}
            for stage, (before, ticks) in zip(self.stages, plans):
                for kind, unit in before:
                    act(kind, unit)
                for slot, mat in stage.held.items():
                    if present.get(slot) is not mat:
                        Fetch(of[id(mat)], *held[slot], 1).copy(0).wait()
                        present[slot] = mat
                self.run_stage(stage, ticks, act, of, sums, held)
            for kind, unit in left:
                act(kind, unit)
            if gather:
                gather.finish()
            for each in sums.values():
                each.finish()

        ports = []
        if self.owns:
            ports = [pltpu.SemaphoreType.DMA((units, 7)), pltpu.SemaphoreType.DMA((units, 7))]
            ports.append(pltpu.SemaphoreType.DMA((len(self.owns),)))
        buffers = []
        for whole in self.sums.values():
            for kind, share in ((F32, 1), (BF16, 1), (BF16, 1), (BF16, 32)):
                buffers += [pltpu.VMEM((rows // share, width), kind) for rows, width in SHAPES]
            buffers += [pltpu.SemaphoreType.DMA((3, LEVELS, 2)), pltpu.SemaphoreType.DMA((3, LEVELS, 2))]
            buffers.append(pltpu.SemaphoreType.DMA((3,)))
            if len(whole) > 2:
                buffers.append(pltpu.VMEM((LEVELS + 1, 8, 1024), F32))
                buffers.append(pltpu.VMEM((LEVELS, 8, 1024), F32))

        for shape in HELD.values():
            buffers += [pltpu.VMEM(shape, BF16), pltpu.SemaphoreType.DMA((1,))]

        out = pl.pallas_call(
            kernel,
            in_specs=[ANY] * len(self.owns) + [spec for _, spec in given],
            out_specs=[ANY] * len(results),
            scratch_shapes=[*ports, *buffers],
            out_shape=[jax.ShapeDtypeStruct(r.shape, r.dtype) for r in results],
            compiler_params=pltpu.CompilerParams(
                vmem_limit_bytes=VMEM_BYTES, collective_id=self.collective, has_side_effects=True
            ),
            name=self.name,
        )(*self.owns, *[array for array, _ in given])
        arrays = {id(result): array for result, array in zip(results, out)}
        return lambda later: arrays[id(later)]

    def run_stage(self, stage, ticks, act, of, sums, held):
        ins, outs = stage.ins, stage.outs
        piped = [at for at, (_, spec) in enumerate(ins) if spec is not ANY and spec is not SCALAR]
        fixed = {at: of[id(a)] for at, (a, _) in enumerate(ins) if at not in piped}

        def poll(slot):
            for (step, at), todo in ticks.items():
                if at == slot:

                    @pl.when(pl.program_id(0) == step)
                    def _(todo=todo):
                        for kind, unit in todo:
                            act(kind, unit)

        poll.sums = sums.get(stage.sums)
        poll.held = held

        def scoped(*scratch):
            if stage.prepare:
                stage.prepare([fixed.get(at) for at in range(len(ins))], scratch)

            def body(*blocks):
                in_refs = [fixed.get(at) for at in range(len(ins))]
                for at, ref in zip(piped, blocks):
                    in_refs[at] = ref
                stage.body(in_refs, list(blocks[len(piped) :]), scratch, poll)

            pltpu.emit_pipeline(
                body,
                grid=stage.grid,
                in_specs=[ins[at][1] for at in piped],
                out_specs=[spec for _, _, spec in outs],
            )(*[of[id(ins[at][0])] for at in piped], *[of[id(r)] for r in stage.results])

        pl.run_scoped(scoped, *stage.scratch)


def launch(
    body, name, grid, ins, outs, scratch, flops, moved, recorder=None, prepare=None, needs=(),
    slots=1, time=1.0, sums=None, held=(),
):
    if recorder is not None:
        return recorder.add(
            body=body, grid=grid, ins=ins, outs=outs, scratch=scratch, prepare=prepare, needs=needs,
            slots=slots, time=time, sums=sums, held=dict(held),
        )

    def kernel(*refs):
        in_refs, out_refs = list(refs[: len(ins)]), list(refs[len(ins) : len(ins) + len(outs)])
        rest = refs[len(ins) + len(outs) :]
        if prepare:

            @pl.when(pl.program_id(0) == 0)
            def _():
                prepare(in_refs, rest)

        body(in_refs, out_refs, rest, lambda slot: None)

    return pl.pallas_call(
        kernel,
        grid=grid,
        in_specs=[spec for _, spec in ins],
        out_specs=[spec for _, _, spec in outs],
        scratch_shapes=scratch,
        out_shape=[jax.ShapeDtypeStruct(s, d) for s, d, _ in outs],
        compiler_params=pltpu.CompilerParams(vmem_limit_bytes=VMEM_BYTES),
        cost_estimate=pl.CostEstimate(flops=flops, bytes_accessed=moved, transcendentals=0),
        name=name,
    )(*[a for a, _ in ins])


class Ready:
    def __init__(self, whole):
        self.whole = whole

    def wait(self, chunk):
        pass

    def wait_all(self):
        pass


def staged_call(body, name, grid, limit, mats, ins, outs, scratch=(), flops=0, part=None, slots_of=(), **record):
    held = dict(zip(slots_of, (mat for mat, _ in mats))) if record else {}
    own = mats[len(held) :]
    holders = []
    for mat, chunks in own:
        rows, width = mat.shape
        holders.append(pltpu.VMEM((rows, width if part is None else width // 3), mat.dtype))
        holders.append(pltpu.SemaphoreType.DMA((chunks,)))
    given = [mat for mat, _ in own]

    def fetches(in_refs, rest):
        return [
            Fetch(
                in_refs[1 + at], rest[2 * at], rest[2 * at + 1], chunks,
                0 if part is None else part * mat.shape[1] // 3,
            )
            for at, (mat, chunks) in enumerate(own)
        ]

    def prepare(in_refs, rest):
        for fetch in fetches(in_refs, rest):
            fetch.start()

    def staged(in_refs, out_refs, rest, poll):
        ready = [Ready(poll.held[slot][0]) for slot in held]
        args = (in_refs[0], ready + fetches(in_refs, rest), in_refs[1 + len(given) :], out_refs)
        body(*args, rest[2 * len(own) :], poll)

    moved = sum(a.size * a.dtype.itemsize for a in given)
    moved += sum(a.size * a.dtype.itemsize for a, _ in ins)
    moved += sum(math.prod(s) * jnp.dtype(d).itemsize for s, d, _ in outs)
    if record:
        record = dict(record, needs=[(mat, part) for mat in given], held=held)
    return launch(
        staged,
        name,
        grid,
        [(limit, SCALAR)] + [(mat, ANY) for mat in given] + list(ins),
        outs,
        [*holders, *scratch],
        flops,
        moved,
        prepare=prepare,
        **record,
    )


def project(name, limit, rows_in, mat, chunks, part=None, **record):
    total, depth = rows_in.shape
    width = mat.shape[1] if part is None else mat.shape[1] // 3
    block = min(256, total)
    step = width // chunks

    def body(limit, fetches, ins, outs, extra, poll):
        (fetch,) = fetches
        left = ins[0][...]
        for chunk in range(chunks):
            poll(chunk)
            fetch.wait(chunk)
            columns = slice(chunk * step, (chunk + 1) * step)
            outs[0][:, columns] = nn(left, fetch.whole[:, columns]).astype(BF16)

    return staged_call(
        body,
        name,
        (total // block,),
        limit,
        [(mat, chunks)],
        [(rows_in, rows_spec(block, depth))],
        [((total, width), BF16, rows_spec(block, width))],
        flops=2 * total * depth * width,
        part=part,
        **record,
    )[0]


def attend(name, limit, queries, keys, values, causal, **record):
    q_len, k_len = queries[0].shape[0], keys[0].shape[0]
    pairs = 1024 // PAIR
    step = min(512, q_len)

    def body(ins, outs, extra, poll):
        poll(0)
        limit_ref, q_ref, k_ref, v_ref = ins
        e_ref, o_ref, inv_ref = outs
        lanes = lax.broadcasted_iota(jnp.int32, (1, PAIR), 1)
        places = lax.broadcasted_iota(jnp.int32, (k_len, 1), 0)
        bias = jnp.where(places < limit_ref[0], 0.0, -1000000000.0)
        q_two = q_ref[...].astype(F32) * (1.0 / math.sqrt(HEAD))
        k_two = k_ref[...].astype(F32)
        v_two = v_ref[...].astype(F32)
        q_own, k_own, v_own = [], [], []
        for half in range(2):
            own = (lanes >= HEAD * half) & (lanes < HEAD * (half + 1))
            spare = lanes == HEAD * (1 - half)
            q_own.append(jnp.where(own, q_two, jnp.where(spare, 1.0, 0.0)).astype(BF16))
            k_own.append(jnp.where(own, k_two, jnp.where(spare, bias, 0.0)).astype(BF16))
            v_own.append(jnp.where(own, v_two, jnp.where(spare, 1.0, 0.0)).T.astype(BF16))

        def score(half, start):
            scores = nt(k_own[half], q_own[half][start : start + step])
            if causal:
                shape = (k_len, step)
                key_at = lax.broadcasted_iota(jnp.int32, shape, 0)
                query_at = lax.broadcasted_iota(jnp.int32, shape, 1) + start
                scores = jnp.where(key_at <= query_at, scores, -1000000000.0)
            return scores

        blocks = [(half, start) for half in range(2) for start in range(0, q_len, step)]
        parts = [[], []]
        scores = score(*blocks[0])
        for at, (half, start) in enumerate(blocks):
            later = score(*blocks[at + 1]) if at + 1 < len(blocks) else None
            highest = jnp.max(scores, axis=0, keepdims=True)
            weights = jnp.exp(scores - highest).astype(BF16)
            e_ref[0, :, half * q_len + start : half * q_len + start + step] = weights
            parts[half].append(nn(v_own[half], weights))
            scores = later
        mixed = []
        for half in range(2):
            out = jnp.concatenate(parts[half], axis=1) if len(parts[half]) > 1 else parts[half][0]
            at = HEAD * (1 - half)
            inverse = 1.0 / out[at : at + 1]
            own_rows = out[HEAD * half : HEAD * (half + 1)]
            mixed.append((own_rows * inverse, jnp.broadcast_to(inverse, own_rows.shape)))
        o_ref[...] = jnp.concatenate([mixed[0][0], mixed[1][0]], axis=0).T.astype(BF16)
        inv_ref[...] = jnp.concatenate([mixed[0][1], mixed[1][1]], axis=0).T

    def columns(rows, first):
        return pl.BlockSpec((rows, PAIR), lambda i: (0, first + i))

    return launch(
        body,
        name,
        (pairs,),
        [
            (limit, SCALAR),
            (queries[0], columns(q_len, queries[1])),
            (keys[0], columns(k_len, keys[1])),
            (values[0], columns(k_len, values[1])),
        ],
        [
            (
                (pairs, k_len, 2 * q_len),
                BF16,
                pl.BlockSpec((1, k_len, 2 * q_len), lambda i: (i, 0, 0)),
            ),
            ((q_len, 1024), BF16, columns(q_len, 0)),
            ((q_len, 1024), F32, columns(q_len, 0)),
        ],
        [],
        16 * pairs * q_len * k_len * PAIR,
        4 * pairs * q_len * k_len,
        **record,
    )


def attend_grad(name, queries, keys, values, weights, mixture, inverse, upstream, **record):
    q_len, k_len = queries[0].shape[0], keys[0].shape[0]
    pairs = 1024 // PAIR
    step = min(256, q_len)
    factor = 1.0 / math.sqrt(HEAD)

    def body(ins, outs, extra, poll):
        q_ref, k_ref, v_ref, e_ref, o_ref, inv_ref, do_ref = ins
        dq_ref, dk_ref, dv_ref = outs
        (ds_ref,) = extra
        poll(0)
        lanes = lax.broadcasted_iota(jnp.int32, (1, PAIR), 1)
        first = lanes < HEAD
        scaled = do_ref[...].astype(F32) * inv_ref[...]
        inner = scaled.astype(BF16).astype(F32) * o_ref[...].astype(F32)
        coarse = inner.astype(BF16)
        fine = (inner - coarse.astype(F32)).astype(BF16)
        picks = lax.broadcasted_iota(jnp.int32, (8, PAIR), 1)
        ones = [
            jnp.where(picks < HEAD, 1.0, 0.0).astype(BF16),
            jnp.where(picks < HEAD, 0.0, 1.0).astype(BF16),
        ]
        delta = [(nt(one, coarse) + nt(one, fine))[0:1] for one in ones]
        do_two = jnp.concatenate(
            [jnp.where(first, scaled, 0.0).astype(BF16), jnp.where(first, 0.0, scaled).astype(BF16)],
            axis=0,
        )
        q_all = q_ref[...].astype(F32) * factor
        q_two = jnp.concatenate(
            [jnp.where(first, q_all, 0.0).astype(BF16), jnp.where(first, 0.0, q_all).astype(BF16)],
            axis=0,
        )
        k_flip = k_ref[...].astype(F32).T.astype(BF16)
        v_all = v_ref[...]
        for half in range(2):
            for start in range(0, q_len, step):
                at = half * q_len + start
                probs_grad = nt(v_all, do_two[at : at + step])
                held = e_ref[0, :, at : at + step].astype(F32)
                ds_ref[:, at : at + step] = (
                    held * (probs_grad - delta[half][:, start : start + step])
                ).astype(BF16)
        dv_ref[...] = nn(e_ref[0], do_two).astype(BF16)
        dk_ref[...] = nn(ds_ref[...], q_two).astype(BF16)
        turned = nn(k_flip, ds_ref[...]) * factor
        rows = lax.broadcasted_iota(jnp.int32, (PAIR, 1), 0)
        dq_ref[...] = jnp.where(rows < HEAD, turned[:, :q_len], turned[:, q_len:]).T.astype(BF16)

    def columns(rows, at):
        return pl.BlockSpec((rows, PAIR), lambda i: (0, at + i))

    return launch(
        body,
        name,
        (pairs,),
        [
            (queries[0], columns(q_len, queries[1])),
            (keys[0], columns(k_len, keys[1])),
            (values[0], columns(k_len, values[1])),
            (weights, pl.BlockSpec((1, k_len, 2 * q_len), lambda i: (i, 0, 0))),
            (mixture, columns(q_len, 0)),
            (inverse, columns(q_len, 0)),
            (upstream, columns(q_len, 0)),
        ],
        [
            ((q_len, 1024), BF16, columns(q_len, 0)),
            ((k_len, 1024), BF16, columns(k_len, 0)),
            ((k_len, 1024), BF16, columns(k_len, 0)),
        ],
        [pltpu.VMEM((k_len, 2 * q_len), BF16)],
        32 * pairs * q_len * k_len * PAIR,
        4 * pairs * q_len * k_len,
        **record,
    )


def row_mask(limit, block):
    at = lax.broadcasted_iota(jnp.int32, (block, 1), 0) + pl.program_id(0) * block
    return (at < limit).astype(F32)


def add_squares(ref, row, entries, mask):
    sums = jnp.sum(entries * entries * mask, axis=0, keepdims=True)
    first = pl.program_id(0) == 0

    @pl.when(first)
    def _():
        ref[row : row + 1, :] = sums

    @pl.when(jnp.logical_not(first))
    def _():
        ref[row : row + 1, :] += sums


def spread_lanes(column):
    return jnp.broadcast_to(column, (column.shape[0], 128))


def out_norm(name, limit, mixture, residual, gain, mat, next_mat=None, residual_gain=None, **record):
    total, width = mixture.shape
    block = min(256, total)
    mats = [(mat, 1)] + ([] if next_mat is None else [(next_mat, 1)])

    def body(limit, fetches, ins, outs, extra, poll):
        poll(0)
        o_ref, r_ref, g_ref, rg_ref = ins
        fetches[0].wait_all()
        added = nn(o_ref[...], fetches[0].whole[...])
        base = r_ref[...].astype(F32)
        if residual_gain is not None:
            base = base * rg_ref[...]
        unit, inverse = standardize(base + added)
        outs[0][...] = unit.astype(BF16)
        outs[1][...] = spread_lanes(inverse)
        add_squares(outs[2], 0, added, row_mask(limit[0], block))
        if next_mat is not None:
            fetches[1].wait_all()
            hidden = (unit * g_ref[...]).astype(BF16)
            outs[3][...] = nn(hidden, fetches[1].whole[...]).astype(BF16)

    outs = [
        ((total, width), BF16, rows_spec(block, width)),
        ((total, 128), F32, rows_spec(block, 128)),
        ((8, width), F32, whole_spec((8, width))),
    ]
    if next_mat is not None:
        outs.append(((total, width), BF16, rows_spec(block, width)))
    return staged_call(
        body,
        name,
        (total // block,),
        limit,
        mats,
        [
            (mixture, rows_spec(block, width)),
            (residual, rows_spec(block, width)),
            (gain, whole_spec((1, width))),
            (gain if residual_gain is None else residual_gain, whole_spec((1, width))),
        ],
        outs,
        flops=2 * total * width * width * len(mats),
        **record,
    )


def branch(name, limit, unit, gain, gain_out, w_in, w_back, down_low, up_low, **record):
    total, width = unit.shape
    hidden_units = w_in.shape[1]
    adapter = down_low.shape[1]
    block = min(256, total)
    chunks = 4
    step = hidden_units // chunks

    def body(limit, fetches, ins, outs, extra, poll):
        u_ref, g_ref, go_ref, ad_ref, au_ref = ins
        y_ref, unit_ref, inv_ref, slope_ref, wa_ref, ad_slope_ref, sq_ref = outs
        (act,) = extra
        first, second = fetches
        hidden = u_ref[...].astype(F32) * g_ref[...]
        low = hidden.astype(BF16)
        pre = nn(low, ad_ref[...].astype(BF16))
        gate = jax.nn.sigmoid(pre)
        wa = (pre * gate).astype(BF16)
        wa_ref[...] = wa
        ad_slope_ref[...] = (gate * (1.0 + pre * (1.0 - gate))).astype(BF16)
        adapted = 4.0 * nn(wa, au_ref[...].astype(BF16))
        for chunk in range(chunks):
            if chunk % 2 == 0:
                poll(chunk // 2)
            first.wait(chunk)
            columns = slice(chunk * step, (chunk + 1) * step)
            fp = nn(low, first.whole[:, columns])
            cdf = 0.5 * (1.0 + lax.erf(fp * (1.0 / math.sqrt(2.0))))
            act[:, columns] = (fp * cdf).astype(BF16)
            bell = jnp.exp(-0.5 * fp * fp) * (1.0 / math.sqrt(2.0 * math.pi))
            slope_ref[:, columns] = (cdf + fp * bell).astype(BF16)
        second.wait_all()
        added = nn(act[...], second.whole[...]) + adapted
        out_unit, inverse = standardize(hidden + added)
        result = out_unit * go_ref[...]
        y_ref[...] = result.astype(BF16)
        unit_ref[...] = out_unit.astype(BF16)
        inv_ref[...] = spread_lanes(inverse)
        mask = row_mask(limit[0], block)
        add_squares(sq_ref, 0, added, mask)
        add_squares(sq_ref, 1, result, mask)

    return staged_call(
        body,
        name,
        (total // block,),
        limit,
        [(w_in, chunks), (w_back, 1)],
        [
            (unit, rows_spec(block, width)),
            (gain, whole_spec((1, width))),
            (gain_out, whole_spec((1, width))),
            (down_low, whole_spec(down_low.shape)),
            (up_low, whole_spec(up_low.shape)),
        ],
        [
            ((total, width), BF16, rows_spec(block, width)),
            ((total, width), BF16, rows_spec(block, width)),
            ((total, 128), F32, rows_spec(block, 128)),
            ((total, hidden_units), BF16, rows_spec(block, hidden_units)),
            ((total, adapter), BF16, rows_spec(block, adapter)),
            ((total, adapter), BF16, rows_spec(block, adapter)),
            ((8, width), F32, whole_spec((8, width))),
        ],
        scratch=[pltpu.VMEM((block, hidden_units), BF16)],
        flops=4 * total * width * (hidden_units + adapter),
        slots_of=("within", "back"),
        **record,
    )


def adapter_grad(upstream, refs):
    (uo_ref, io_ref, go_ref, ui_ref, gi_ref, wa_ref, as_ref, ad_ref, au_ref) = refs
    grad_two = standardize_grad(uo_ref[...].astype(F32), io_ref[:, 0:1], upstream * go_ref[...])
    dvd = (4.0 * grad_two).astype(BF16)
    low = (ui_ref[...].astype(F32) * gi_ref[...]).astype(BF16)
    du = (nt(dvd, au_ref[...].astype(BF16)) * as_ref[...].astype(F32)).astype(BF16)
    total = grad_two + nt(du, ad_ref[...].astype(BF16))
    return grad_two.astype(BF16), total, tn(low, du), tn(wa_ref[...], dvd)


def hidden_grad(dz, total, fetches, refs, dfp, chunks, poll=lambda slot: None):
    slope_ref, ui_ref, ii_ref, gi_ref = refs
    back, within, last = fetches
    step = dfp.shape[1] // chunks
    back.wait_all()
    poll(0)
    for chunk in range(chunks):
        columns = slice(chunk * step, (chunk + 1) * step)
        act_grad = nt(dz, back.whole[columns, :])
        dfp[:, columns] = (act_grad * slope_ref[:, columns].astype(F32)).astype(BF16)
    within.wait_all()
    poll(1)
    total = total + nt(dfp[...], within.whole[...])
    grad_one = standardize_grad(ui_ref[...].astype(F32), ii_ref[:, 0:1], total * gi_ref[...])
    last.wait_all()
    return grad_one, nt(grad_one.astype(BF16), last.whole[...]).astype(BF16)


def dec_branch_grad(
    name, limits, cot, saved_out, gain_out, saved_in, gain_in, slope, wa, ad_slope,
    w_back, w_in, w_out, down_low, up_low, squares, **record,
):
    total, width = cot.shape
    hidden_units = w_in.shape[1]
    adapter = down_low.shape[1]
    whole = [
        cot, saved_out[0], saved_out[1], gain_out, saved_in[0], gain_in, wa, ad_slope, down_low,
        up_low, slope, saved_in[1], *squares,
    ]

    def body(limit, fetches, ins, outs, extra, poll):
        grad_ref, mix_ref = outs[:2]
        if record:
            (down_ref, up_ref), tally_ref = poll.sums.totals, poll.sums.tallies[0].at[0]
        else:
            down_ref, up_ref, tally_ref = outs[2], outs[3].at[:adapter], outs[3].at[adapter:]
        (other,), cot_ref, slope_ref, ii_ref = ins[:1], ins[1], ins[11], ins[12]
        dz, part, down_ref[...], up_ref[...] = adapter_grad(cot_ref[...].astype(F32), ins[2:11])
        sums = [ref[row : row + 1, :] for ref, rows in zip(ins[13:], (1, 2, 1, 1, 2)) for row in range(rows)]
        lanes = lax.broadcasted_iota(jnp.int32, (1, width), 1)
        counts = jnp.where(lanes == 0, limit[0], jnp.where(lanes == 1, other[0], 0)).astype(F32)
        tally_ref[...] = jnp.concatenate([*sums, counts], axis=0)
        grad_ref[...], mix_ref[...] = hidden_grad(
            dz, part, fetches, (slope_ref, ins[5], ii_ref, ins[6]), extra[0], 4
        )

    return staged_call(
        body,
        name,
        (1,),
        limits[0],
        [(w_back, 1), (w_in, 1), (w_out, 1)],
        [(limits[1], SCALAR)] + [(a, whole_spec(a.shape)) for a in whole],
        [
            (cot.shape, F32, whole_spec(cot.shape)),
            (cot.shape, BF16, whole_spec(cot.shape)),
        ]
        + [
            (shape, F32, whole_spec(shape))
            for shape in (() if record else (down_low.shape, (adapter + 8, width)))
        ],
        scratch=[pltpu.VMEM((total, hidden_units), BF16)],
        flops=4 * total * width * (hidden_units + 2 * adapter),
        slots_of=("back", "within"),
        **record,
    )


def enc_adapter_grad(
    name, limit, cot, cross, cross_mat, saved_out, gain_out, saved_in, gain_in, wa, ad_slope,
    down_low, up_low, **record,
):
    total, width = cot.shape
    adapter = down_low.shape[1]
    block = min(256, total)
    rows = rows_spec(block, width)

    def body(limit, fetches, ins, outs, extra, poll):
        poll(0)
        dz_ref, part_ref = outs[:2]
        down_sum, up_sum = poll.sums.totals if record else extra
        fetches[0].wait_all()
        upstream = ins[0][...].astype(F32)
        for at in range(2):
            upstream = upstream + nt(ins[1 + at][...], fetches[0].whole[:, at * width : (at + 1) * width])
        dz_ref[...], part_ref[...], down_part, up_part = adapter_grad(upstream, ins[3:])
        at = pl.program_id(0)

        @pl.when(at == 0)
        def _():
            up_sum[...] = up_part
            down_sum[...] = down_part

        @pl.when(at > 0)
        def _():
            up_sum[...] += up_part
            down_sum[...] += down_part

        if not record:

            @pl.when(at == total // block - 1)
            def _():
                outs[2][...] = down_sum[...].astype(BF16)
                outs[3][...] = up_sum[...].astype(BF16)

    return staged_call(
        body,
        name,
        (total // block,),
        limit,
        [(cross_mat, 1)],
        [
            (cot, rows),
            (cross[0], rows),
            (cross[1], rows),
            (saved_out[0], rows),
            (saved_out[1], rows_spec(block, 128)),
            (gain_out, whole_spec((1, width))),
            (saved_in[0], rows),
            (gain_in, whole_spec((1, width))),
            (wa, rows_spec(block, adapter)),
            (ad_slope, rows_spec(block, adapter)),
            (down_low, whole_spec(down_low.shape)),
            (up_low, whole_spec(up_low.shape)),
        ],
        [
            ((total, width), BF16, rows),
            ((total, width), F32, rows),
        ]
        + [(a.shape, BF16, whole_spec(a.shape)) for a in (() if record else (down_low, up_low))],
        scratch=[pltpu.VMEM(a.shape, F32) for a in (() if record else (down_low, up_low))],
        flops=4 * total * width * (width + 2 * adapter),
        **record,
    )


def enc_hidden_grad(name, limit, dz, part, slope, saved_in, gain_in, w_back, w_in, w_out, **record):
    total, width = dz.shape
    hidden_units = w_in.shape[1]
    block = min(256, total)
    rows = rows_spec(block, width)

    def body(limit, fetches, ins, outs, extra, poll):
        outs[0][...], outs[1][...] = hidden_grad(
            ins[0][...], ins[1][...], fetches, ins[2:], extra[0], 4, poll
        )

    return staged_call(
        body,
        name,
        (total // block,),
        limit,
        [(w_back, 1), (w_in, 1), (w_out, 1)],
        [
            (dz, rows),
            (part, rows),
            (slope, rows_spec(block, hidden_units)),
            (saved_in[0], rows),
            (saved_in[1], rows_spec(block, 128)),
            (gain_in, whole_spec((1, width))),
        ],
        [((total, width), F32, rows), ((total, width), BF16, rows)],
        scratch=[pltpu.VMEM((block, hidden_units), BF16)],
        flops=4 * total * width * hidden_units,
        slots_of=("back", "within"),
        **record,
    )


def middle_grad(name, limit, grad_cross, dq, saved, gain, w_cq, w_so, **record):
    total, width = dq.shape
    block = min(256, total)
    unit, inv = saved

    def body(limit, fetches, ins, outs, extra, poll):
        poll(0)
        gc_ref, dq_ref, u_ref, i_ref, g_ref = ins
        fetches[0].wait_all()
        hidden_grad = gc_ref[...] + nt(dq_ref[...], fetches[0].whole[...])
        grad_self = standardize_grad(
            u_ref[...].astype(F32), i_ref[:, 0:1], hidden_grad * g_ref[...]
        )
        outs[0][...] = grad_self
        fetches[1].wait_all()
        outs[1][...] = nt(grad_self.astype(BF16), fetches[1].whole[...]).astype(BF16)

    return staged_call(
        body,
        name,
        (total // block,),
        limit,
        [(w_cq, 1), (w_so, 1)],
        [
            (grad_cross, rows_spec(block, width)),
            (dq, rows_spec(block, width)),
            (unit, rows_spec(block, width)),
            (inv, rows_spec(block, 128)),
            (gain, whole_spec((1, width))),
        ],
        [
            ((total, width), F32, rows_spec(block, width)),
            ((total, width), BF16, rows_spec(block, width)),
        ],
        flops=4 * total * width * width,
        **record,
    )


def input_grad(name, limit, base, parts, mat, narrow=(), tally=None):
    total, width = base.shape
    block = min(256, total)
    steps = total // block
    count = len(parts)

    def body(limit, fetches, ins, outs, extra, poll):
        (fetch,) = fetches
        result = ins[0][...]
        for at in range(count):
            fetch.wait(at)
            result = result + nt(ins[1 + at][...], fetch.whole[:, at * width : (at + 1) * width])
        outs[0][...] = result
        for at in range(len(narrow)):
            outs[1 + at][...] = ins[1 + count + at][...].astype(F32)
        if tally is not None:
            rows = ins[-1][...]
            at = lax.broadcasted_iota(jnp.int32, (8, 1), 0)
            numbers = jnp.where(at < 3, rows[7:8, 0:1], rows[7:8, 1:2])
            outs[-1][...] = spread_lanes(
                jnp.sqrt(jnp.sum(rows, axis=1, keepdims=True) / (numbers * width))
            )

    slices = [(a, rows_spec(a.shape[0] // steps, a.shape[1])) for a in narrow]
    tallies = [] if tally is None else [(tally, whole_spec(tally.shape))]
    return staged_call(
        body,
        name,
        (steps,),
        limit,
        [(mat, count)],
        [(base, rows_spec(block, width))] + [(p, rows_spec(block, width)) for p in parts] + slices + tallies,
        [((total, width), F32, rows_spec(block, width))]
        + [(a.shape, F32, spec) for a, spec in slices]
        + [((8, 128), F32, whole_spec((8, 128))) for _ in tallies],
        flops=2 * total * width * width * count,
    )


NAMES = (
    "enc_qkv",
    "enc_attn_out",
    "enc_ffn_in",
    "enc_ffn_out",
    "dec_self_qkv",
    "dec_self_out",
    "dec_cross_q",
    "dec_cross_kv",
    "dec_cross_out",
    "dec_ffn_in",
    "dec_ffn_out",
)


def layers(enc_limit, dec_limit, enc_input, dec_input, enc_cot, dec_cot, blocks, hosting, fsdp, gains, adapters):
    gain = [gains[k : k + 1] for k in range(5)]
    enc_down, enc_up, dec_down, dec_up = adapters
    if hosting:
        recorder = Recorder("forward", 1, blocks, fsdp)
        w = types.SimpleNamespace(**dict(zip(recorder.names, recorder.wholes)))
    else:
        recorder = None
        w = types.SimpleNamespace(
            **{name: lax.all_gather(b, "fsdp", axis=0, tiled=True) for name, b in blocks.items()}
        )

    def at(slots, time, sums=None):
        if not hosting:
            return {}
        return {"recorder": recorder, "slots": slots, "time": time, "sums": sums}

    enc_q, enc_k, enc_v = (
        project("enc_project", enc_limit, enc_input, w.enc_qkv, 1, part, **at(1, 5.0))
        for part in range(3)
    )
    e_enc, o_enc, inv_enc = attend(
        "enc_attend", enc_limit, (enc_q, 0), (enc_k, 0), (enc_v, 0), False, **at(1, 34.0)
    )
    unit1, dev1, sq_a = out_norm(
        "enc_out_norm", enc_limit, o_enc, enc_input, gain[0], w.enc_attn_out, **at(1, 9.0)
    )
    enc_out, unit2, dev2, slope_e, wa_e, ads_e, sq_b = branch(
        "enc_branch", enc_limit, unit1, gain[0], gain[1], w.enc_ffn_in, w.enc_ffn_out,
        enc_down, enc_up, **at(2, 33.0),
    )
    sqkv = project("dec_project", dec_limit, dec_input, w.dec_self_qkv, 3, **at(3, 6.0))
    e_self, o_self, inv_self = attend(
        "dec_attend", dec_limit, (sqkv, 0), (sqkv, 8), (sqkv, 16), True, **at(1, 8.5)
    )
    unit3, dev3, sq_c, cross_q = out_norm(
        "dec_out_norm", dec_limit, o_self, dec_input, gain[2], w.dec_self_out, w.dec_cross_q,
        **at(1, 5.3),
    )
    kv = project("cross_project", enc_limit, enc_out, w.dec_cross_kv, 2, **at(2, 9.5))
    e_cross, o_cross, inv_cross = attend(
        "cross_attend", enc_limit, (cross_q, 0), (kv, 0), (kv, 8), False, **at(1, 14.0)
    )
    if hosting:
        value = recorder.run()
        w = types.SimpleNamespace(**{name: value(mat) for name, mat in vars(w).items()})
        enc_q, enc_k, enc_v, e_enc, o_enc, inv_enc = map(value, (enc_q, enc_k, enc_v, e_enc, o_enc, inv_enc))
        unit1, dev1, sq_a = map(value, (unit1, dev1, sq_a))
        enc_out, unit2, dev2, slope_e, wa_e, ads_e, sq_b = map(
            value, (enc_out, unit2, dev2, slope_e, wa_e, ads_e, sq_b)
        )
        sqkv, e_self, o_self, inv_self = map(value, (sqkv, e_self, o_self, inv_self))
        unit3, dev3, sq_c, cross_q = map(value, (unit3, dev3, sq_c, cross_q))
        kv, e_cross, o_cross, inv_cross = map(value, (kv, e_cross, o_cross, inv_cross))
        recorder = Recorder("encoder_grad", 2, {}, fsdp)
    unit4, dev4, sq_d = out_norm(
        "cross_out_norm", dec_limit, o_cross, unit3, gain[3], w.dec_cross_out, residual_gain=gain[2]
    )
    dec_out, unit5, dev5, slope_d, wa_d, ads_d, sq_e = branch(
        "dec_branch", dec_limit, unit4, gain[3], gain[4], w.dec_ffn_in, w.dec_ffn_out,
        dec_down, dec_up,
    )
    grad_cross, do_cross, *dec_grads = dec_branch_grad(
        "dec_branch_grad", (enc_limit, dec_limit), dec_cot, (unit5, dev5), gain[4], (unit4, dev4), gain[3],
        slope_d, wa_d, ads_d, w.dec_ffn_out, w.dec_ffn_in, w.dec_cross_out, dec_down, dec_up,
        (sq_a, sq_b, sq_c, sq_d, sq_e),
    )
    dcq, dck, dcv = attend_grad(
        "cross_attend_grad", (cross_q, 0), (kv, 0), (kv, 8), e_cross, o_cross, inv_cross, do_cross
    )
    if hosting:
        dec_sums = recorder.reduce("dec", True)
        recorder.load("dec", dec_grads)
        enc_sums = recorder.reduce("enc", False)
    dz, part, *enc_grads = enc_adapter_grad(
        "enc_adapter_grad", enc_limit, enc_cot, (dck, dcv), w.dec_cross_kv, (unit2, dev2), gain[1],
        (unit1, dev1), gain[0], wa_e, ads_e, enc_down, enc_up, **at(1, 20.0, "enc"),
    )
    grad_one, do_enc = enc_hidden_grad(
        "enc_hidden_grad", enc_limit, dz, part, slope_e, (unit1, dev1), gain[0],
        w.enc_ffn_out, w.enc_ffn_in, w.enc_attn_out, **at(2, 28.0),
    )
    deq, dek, dev = attend_grad(
        "enc_attend_grad", (enc_q, 0), (enc_k, 0), (enc_v, 0), e_enc, o_enc, inv_enc, do_enc, **at(1, 37.0)
    )
    if hosting:
        value = recorder.run()
        grad_one, deq, dek, dev = map(value, (grad_one, deq, dek, dev))
        *dec_grads, tally = map(value, dec_sums)
        enc_grads = [value(a) for a in enc_sums]
    else:
        everyone = ("fsdp", "dp")
        down, up = lax.psum(dec_grads, everyone)
        dec_grads, tally = [down, up[: dec_up.shape[0]]], up[dec_up.shape[0] :]
        enc_grads = lax.psum(enc_grads, everyone)
    grad_self, do_self = middle_grad(
        "dec_middle_grad", dec_limit, grad_cross, dcq, (unit3, dev3), gain[2], w.dec_cross_q,
        w.dec_self_out,
    )
    dsq, dsk, dsv = attend_grad(
        "dec_attend_grad", (sqkv, 0), (sqkv, 8), (sqkv, 16), e_self, o_self, inv_self, do_self
    )
    dec_grad, *dec_grads = input_grad(
        "dec_input_grad", dec_limit, grad_self, [dsq, dsk, dsv], w.dec_self_qkv, dec_grads
    )
    enc_grad, *enc_grads, rms = input_grad(
        "enc_input_grad", enc_limit, grad_one, [deq, dek, dev], w.enc_qkv, enc_grads, tally
    )
    return enc_out, dec_out, enc_grad, dec_grad, *enc_grads, *dec_grads, rms[:7, 0]


def shards(fsdp, dp, enc_input, dec_input, enc_cot, dec_cot, *rest):
    mats, (gains, enc_down, enc_up, dec_down, dec_up, enc_lengths, dec_lengths) = rest[:11], rest[11:]
    return layers(
        enc_lengths, dec_lengths, enc_input, dec_input, enc_cot, dec_cot, dict(zip(NAMES, mats)),
        fsdp == 8 and dp == 4, fsdp, gains, (enc_down, enc_up, dec_down, dec_up),
    )


def solution(mesh):
    by_rows = P(("fsdp", "dp"), None)
    placed = (by_rows,) * 4 + (P("fsdp", None),) * 11 + (P(),) * 5 + (P(("fsdp", "dp")),) * 2
    return jax.shard_map(
        functools.partial(shards, mesh.shape["fsdp"], mesh.shape["dp"]),
        mesh=mesh,
        in_specs=placed,
        out_specs=(by_rows,) * 4 + (P(),) * 5,
        check_vma=False,
    )
```

```python
import functools
import math
import types

import jax
import jax.numpy as jnp
from jax import lax
from jax.experimental import pallas as pl
from jax.experimental.pallas import tpu as pltpu
from jax.sharding import PartitionSpec as P

HEAD = 64
PAIR = 2 * HEAD
EPSILON = 1e-05
F32 = jnp.float32
BF16 = jnp.bfloat16
VMEM_BYTES = 58 * 2**20


def nn(former, latter):
    return jnp.dot(former, latter, preferred_element_type=F32)


def nt(former, latter):
    return lax.dot_general(
        former, latter, (((1,), (1,)), ((), ())), preferred_element_type=F32
    )


def tn(former, latter):
    return lax.dot_general(
        former, latter, (((0,), (0,)), ((), ())), preferred_element_type=F32
    )


def standardize(entries):
    centered = entries - jnp.mean(entries, axis=-1, keepdims=True)
    spread = jnp.mean(centered * centered, axis=-1, keepdims=True)
    inverse = lax.rsqrt(spread + EPSILON)
    return centered * inverse, inverse


def standardize_grad(unit, inverse, scaled):
    return inverse * (
        scaled
        - jnp.mean(scaled, axis=-1, keepdims=True)
        - unit * jnp.mean(scaled * unit, axis=-1, keepdims=True)
    )


class Fetch:
    def __init__(self, source, whole, sems, chunks, first=0):
        self.source, self.whole, self.sems, self.chunks = source, whole, sems, chunks
        self.first = first

    def copy(self, chunk):
        width = self.whole.shape[1] // self.chunks
        return pltpu.make_async_copy(
            self.source.at[:, pl.ds(self.first + chunk * width, width)],
            self.whole.at[:, pl.ds(chunk * width, width)],
            self.sems.at[chunk],
        )

    def start(self):
        for chunk in range(self.chunks):
            self.copy(chunk).start()

    def wait(self, chunk):
        @pl.when(pl.program_id(0) == 0)
        def _():
            self.copy(chunk).wait()

    def wait_all(self):
        for chunk in range(self.chunks):
            self.wait(chunk)


UNIT_US = 6.0
LEAD_US = 5.0


class Place:
    def __init__(self):
        f, z = lax.axis_index("fsdp"), lax.axis_index("dp")
        self.core, self.x, self.y = f % 2, (f // 2) % 2, f // 4
        self.odd, self.high = z % 2, z // 2
        self.own = f
        self.twin = {"fsdp": f + 1 - 2 * self.core}
        self.beside = {"fsdp": f + 2 - 4 * self.x}
        self.above = {"fsdp": f + 4 - 8 * self.y}
        self.partner = {"dp": z + 1 - 2 * self.odd}
        self.distant = {"dp": z + 2 - 4 * self.high}

    def meet(self):
        barrier = pltpu.get_barrier_semaphore()
        all_of_them = (self.twin, self.beside, self.above, self.partner, self.distant)
        for to in all_of_them:
            pl.semaphore_signal(barrier, inc=1, device_id=to, device_id_type=pl.DeviceIdType.MESH)
        pl.semaphore_wait(barrier, len(all_of_them))


class Gather:
    def __init__(self, place, owns, wholes, splits, sends, recvs, locals_):
        self.place, self.owns, self.wholes, self.splits = place, owns, wholes, splits
        self.sends, self.recvs, self.locals = sends, recvs, locals_
        self.units = [(m, part) for m, split in enumerate(splits) for part in range(split)]
        beside, above = place.beside["fsdp"], place.above["fsdp"]
        self.own = place.own
        self.direct = beside + place.odd * (above - beside)
        self.onward = above + place.odd * (beside - above)
        self.far = beside + 4 - 8 * place.y

    def transfer(self, unit, kind):
        m, part = self.units[unit]
        whole, own = self.wholes[m], self.owns[m]
        block, width = own.shape
        by_columns = width == 3072
        rows = block if by_columns else block // self.splits[m]
        wide = width // self.splits[m] if by_columns else width
        first_row, columns = (0, pl.ds(part * wide, wide)) if by_columns else (part * rows, pl.ds(0, wide))
        owner = (self.own, self.direct, self.direct, self.own, self.direct, self.far, self.onward)[kind]
        there = whole.at[pl.ds(pl.multiple_of(owner * block + first_row, 16), rows), columns]
        here = own.at[pl.ds(first_row, rows), columns] if kind in (0, 3) else there
        to = self.place.twin if kind >= 3 else self.place.partner
        if kind < 2:
            to = {"fsdp": (self.direct, self.onward)[kind]}
        return pltpu.make_async_remote_copy(
            src_ref=here,
            dst_ref=there,
            send_sem=self.sends.at[unit, kind],
            recv_sem=self.recvs.at[unit, kind],
            device_id=to,
            device_id_type=pl.DeviceIdType.MESH,
        )

    def keep(self, m):
        block = self.owns[m].shape[0]
        rows = pl.ds(pl.multiple_of(self.own * block, 16), block)
        return pltpu.make_async_copy(self.owns[m], self.wholes[m].at[rows, :], self.locals.at[m])

    def begin(self):
        for unit in range(len(self.units)):
            self.transfer(unit, 0).start()
        for unit in range(len(self.units)):
            self.transfer(unit, 3).start()
        for m in range(len(self.owns)):
            self.keep(m).start()

    def pass_on(self, unit):
        self.transfer(unit, 0).wait_recv()
        for kind in (1, 2, 4):
            self.transfer(unit, kind).start()

    def share(self, unit):
        self.transfer(unit, 1).wait_recv()
        self.transfer(unit, 5).start()
        self.transfer(unit, 2).wait_recv()
        self.transfer(unit, 6).start()

    def complete(self, m, part, first):
        for kind in (3, 4, 5, 6):
            self.transfer(self.units.index((m, part)), kind).wait_recv()
        if first:
            self.keep(m).wait()

    def finish(self):
        for unit in range(len(self.units)):
            for kind in range(7):
                self.transfer(unit, kind).wait_send()


LEVELS = 5
SHAPES = ((1024, 512), (512, 1024))


class Reduce:
    def __init__(self, place, totals, gives, takes, pieces, wholes, sems, tallies=None):
        self.place, self.totals, self.gives, self.takes = place, totals, gives, takes
        self.pieces, self.wholes, self.tallies = pieces, wholes, tallies
        self.sends, self.recvs, self.locals = sems
        p = place
        along = [(p.core, p.twin), (p.x, p.beside), (p.y, p.above), (p.odd, p.partner), (p.high, p.distant)]
        self.ways = [along, [along[0], along[2], along[1], along[3], along[4]]]

    def range(self, part, level):
        rows = SHAPES[part][0]
        first = 0
        for bit, _ in self.ways[part][:level]:
            rows = rows // 2
            first = first + bit * rows
        return first, rows

    def halves(self, part, level):
        first, rows = self.range(part, level)
        bit = self.ways[part][level][0]
        half = rows // 2
        return pl.multiple_of(first + bit * half, half), pl.multiple_of(first + (1 - bit) * half, half), half

    def slot(self, part, level):
        rows = SHAPES[part][0]
        return pl.ds(rows - (rows >> level), rows >> (level + 1))

    def remote(self, src, dst, part, level, back):
        return pltpu.make_async_remote_copy(
            src_ref=src,
            dst_ref=dst,
            send_sem=self.sends.at[part, level, back],
            recv_sem=self.recvs.at[part, level, back],
            device_id=self.ways[part if part < 2 else 0][level][1],
            device_id_type=pl.DeviceIdType.MESH,
        )

    def down(self, part, level):
        rows = self.slot(part, level)
        return self.remote(self.gives[part].at[rows, :], self.takes[part].at[rows, :], part, level, 0)

    def up(self, part, level):
        first, rows = self.range(part, level + 1)
        rows = pl.ds(pl.multiple_of(first, rows), rows)
        return self.remote(self.wholes[part].at[rows, :], self.wholes[part].at[rows, :], part, level, 1)

    def tally(self, level):
        return self.remote(self.tallies[0].at[level], self.tallies[1].at[level], 2, level, 0)

    def piece(self, part):
        first, rows = self.range(part, LEVELS)
        rows = pl.ds(pl.multiple_of(first, rows), rows)
        return pltpu.make_async_copy(self.pieces[part], self.wholes[part].at[rows, :], self.locals.at[part])

    def tally_out(self):
        return pltpu.make_async_copy(self.tallies[0].at[LEVELS], self.tallies[2], self.locals.at[2])

    def step(self, at):
        for part in range(2):
            if 0 < at <= LEVELS:
                keep, _, half = self.halves(part, at - 1)
                self.down(part, at - 1).wait_recv()
                rows = pl.ds(keep, half)
                taken = self.takes[part][self.slot(part, at - 1), :].astype(F32)
                self.totals[part][rows, :] = self.totals[part][rows, :] + taken
            if at < LEVELS:
                _, give, half = self.halves(part, at)
                self.gives[part][self.slot(part, at), :] = self.totals[part][pl.ds(give, half), :].astype(BF16)
                self.down(part, at).start()
            elif at == LEVELS:
                first, rows = self.range(part, LEVELS)
                last = pl.ds(pl.multiple_of(first, rows), rows)
                self.pieces[part][...] = self.totals[part][last, :].astype(BF16)
                self.piece(part).start()
                self.piece(part).wait()
                self.up(part, LEVELS - 1).start()
            else:
                level = 2 * LEVELS - at
                self.up(part, level).wait_recv()
                if level:
                    self.up(part, level - 1).start()
        if self.tallies and at <= LEVELS:
            if at:
                self.tally(at - 1).wait_recv()
                self.tallies[0][at] = self.tallies[0][at - 1] + self.tallies[1][at - 1]
            if at < LEVELS:
                self.tally(at).start()
            else:
                self.tally_out().start()

    def finish(self):
        for level in range(LEVELS):
            for part in range(2):
                self.down(part, level).wait_send()
                self.up(part, level).wait_send()
            if self.tallies:
                self.tally(level).wait_send()
        if self.tallies:
            self.tally_out().wait()


REDUCE_US = (0.0, 5.0, 9.0, 6.5, 6.0, 6.0, 6.0, 6.0, 6.5, 9.0, 5.0)


ANY = pl.BlockSpec(memory_space=pl.ANY)
SCALAR = pl.BlockSpec(memory_space=pltpu.SMEM)


def rows_spec(rows, width):
    return pl.BlockSpec((rows, width), lambda i: (i, 0))


def whole_spec(shape):
    return pl.BlockSpec(shape, lambda i: (0,) * len(shape))


class Later:
    def __init__(self, shape, dtype):
        self.shape, self.dtype = tuple(shape), jnp.dtype(dtype)
        self.size = math.prod(self.shape)


HELD = {"within": (1024, 4096), "back": (4096, 1024)}


class Recorder:
    def __init__(self, name, collective, blocks, fsdp):
        self.name, self.collective = name, collective
        self.loads = {}
        self.names = list(blocks)
        self.owns = list(blocks.values())
        self.wholes = [Later((a.shape[0] * fsdp, a.shape[1]), a.dtype) for a in self.owns]
        self.splits = [max(1, a.size // 131072) for a in self.owns]
        self.stages = []
        self.sums = {}

    def reduce(self, name, tallied):
        self.sums[name] = [Later(shape, BF16) for shape in SHAPES]
        if tallied:
            self.sums[name].append(Later((8, 1024), F32))
        return self.sums[name]

    def load(self, name, arrays):
        self.loads[name] = arrays

    def number(self, mat):
        found = [m for m, whole in enumerate(self.wholes) if whole is mat]
        return found[0] if found else None

    def add(self, **stage):
        stage = types.SimpleNamespace(**stage)
        stage.results = [Later(shape, dtype) for shape, dtype, _ in stage.outs]
        self.stages.append(stage)
        return stage.results

    def schedule(self):
        acts, unit, due = [], 0, LEAD_US
        last_of, come = {}, {}
        for m, split in enumerate(self.splits):
            for part in range(split):
                time = UNIT_US * self.owns[m].size / split / 131072
                due += time
                acts.append((due, "pass_on", unit))
                acts.append((due + time + 2.0, "share", unit))
                last_of[m, part] = unit
                come[m] = due + time + 6.0
                unit += 1
        acts.sort(key=lambda act: act[0])
        clock, plans, started = 0.0, [], []
        for slot in HELD:
            users = [stage for stage in self.stages if slot in stage.held]
            if users:
                mat = users[0].held[slot]
                acts.append((come.get(self.number(mat), 0.0), "fetch", (slot, mat)))
        for name in self.loads:
            started += [("load", name), ("step", (name, 0))]
            due = 0.0
            for at, time in enumerate(REDUCE_US):
                due += time
                if at:
                    acts.append((due, "step", (name, at)))
        acts.sort(key=lambda act: act[0])
        for index, stage in enumerate(self.stages):
            before, ticks = started, {}
            started = []
            needed = [last_of[m, part] for m, part in self.parts_of(stage)]
            if needed:
                while any(act[1] in ("pass_on", "share") and act[2] <= max(needed) for act in acts):
                    clock = max(clock, acts[0][0])
                    before.append(acts.pop(0)[1:])
            while any(act[1] == "fetch" and act[2][1] is stage.held.get(act[2][0]) for act in acts):
                clock = max(clock, acts[0][0])
                before.append(acts.pop(0)[1:])
            pace = stage.time / stage.grid[0] / stage.slots
            for tick in range(stage.grid[0] * stage.slots):
                while acts and acts[0][0] <= clock:
                    ticks.setdefault(divmod(tick, stage.slots), []).append(acts.pop(0)[1:])
                clock += pace
            plans.append((before, ticks))
            for slot in stage.held:
                after = [at for at in range(index + 1, len(self.stages)) if slot in self.stages[at].held]
                if after and self.stages[after[0]].held[slot] is not stage.held[slot]:
                    mat = self.stages[after[0]].held[slot]
                    acts.append((max(clock, come.get(self.number(mat), 0.0)), "fetch", (slot, mat)))
                    acts.sort(key=lambda act: act[0])
            if stage.sums:
                started = [("step", (stage.sums, 0))]
                due = clock
                for at, time in enumerate(REDUCE_US):
                    due += time
                    if at:
                        acts.append((due, "step", (stage.sums, at)))
                acts.sort(key=lambda act: act[0])
        return self.completed(plans, [act[1:] for act in acts])

    def completed(self, plans, left):
        waited = []

        def waits(parts):
            found = []
            for m, part in parts:
                if (m, part) not in waited:
                    found.append(("complete", (m, part, not any(of == m for of, _ in waited))))
                    waited.append((m, part))
            return found

        def spread(acts):
            found = []
            for kind, unit in acts:
                m = self.number(unit[1]) if kind == "fetch" else None
                if m is not None:
                    found += waits((m, part) for part in range(self.splits[m]))
                found.append((kind, unit))
            return found

        full = []
        for stage, (before, ticks) in zip(self.stages, plans):
            before = spread(before) + waits(self.parts_of(stage))
            full.append((before, {tick: spread(ticks[tick]) for tick in sorted(ticks)}))
        every = [(m, part) for m, split in enumerate(self.splits) for part in range(split)]
        return full, spread(left) + waits(every)

    def parts_of(self, stage):
        found = []
        for mat, part in stage.needs:
            m = self.number(mat)
            if m is not None:
                found += [(m, part)] if part is not None else [(m, each) for each in range(self.splits[m])]
        return found

    def run(self):
        given = []
        for stage in self.stages:
            for array, spec in stage.ins + [(mat, ANY) for mat in stage.held.values()]:
                if not isinstance(array, Later) and not any(array is g for g, _ in given):
                    given.append((array, SCALAR if spec is SCALAR else ANY))
        given += [(array, ANY) for arrays in self.loads.values() for array in arrays]
        results = self.wholes + [r for stage in self.stages for r in stage.results]
        results += [r for sums in self.sums.values() for r in sums]
        plans, left = self.schedule()
        units = sum(self.splits)

        def kernel(*refs):
            refs = list(refs)
            owns = refs[: len(self.owns)]
            of = {}
            for (array, _), ref in zip(given, refs[len(self.owns) :]):
                of[id(array)] = ref
            rest = refs[len(self.owns) + len(given) :]
            for result, ref in zip(results, rest):
                of[id(result)] = ref
            rest = rest[len(results) :]
            place = Place()
            gather = None
            if self.owns:
                gather = Gather(place, owns, [of[id(w)] for w in self.wholes], self.splits, *rest[:3])
                rest = rest[3:]
            sums = {}
            for name, whole in self.sums.items():
                tallies = [*rest[11:13], of[id(whole[2])]] if len(whole) > 2 else None
                sums[name] = Reduce(
                    place, rest[:2], rest[2:4], rest[4:6], rest[6:8], [of[id(w)] for w in whole[:2]],
                    rest[8:11], tallies,
                )
                rest = rest[13:] if tallies else rest[11:]
            held = {slot: (rest[2 * at], rest[2 * at + 1]) for at, slot in enumerate(HELD)}
            place.meet()
            if gather:
                gather.begin()

            def act(kind, unit):
                if kind == "step":
                    sums[unit[0]].step(unit[1])
                elif kind == "fetch":
                    slot, mat = unit
                    Fetch(of[id(mat)], *held[slot], 1).start()
                elif kind == "complete":
                    gather.complete(*unit)
                elif kind == "load":
                    first, second = (of[id(array)] for array in self.loads[unit])
                    into, rows = sums[unit], SHAPES[1][0]
                    pairs = [(first, into.totals[0]), (second.at[pl.ds(0, rows), :], into.totals[1])]
                    pairs.append((second.at[pl.ds(rows, 8), :], into.tallies[0].at[0]))
                    copies = [
                        pltpu.make_async_copy(source, goal, into.locals.at[at])
                        for at, (source, goal) in enumerate(pairs)
                    ]
                    for copy in copies:
                        copy.start()
                    for copy in copies:
                        copy.wait()
                else:
                    getattr(gather, kind)(unit)

            present = {}
            for stage, (before, ticks) in zip(self.stages, plans):
                for kind, unit in before:
                    act(kind, unit)
                for slot, mat in stage.held.items():
                    if present.get(slot) is not mat:
                        Fetch(of[id(mat)], *held[slot], 1).copy(0).wait()
                        present[slot] = mat
                self.run_stage(stage, ticks, act, of, sums, held)
            for kind, unit in left:
                act(kind, unit)
            if gather:
                gather.finish()
            for each in sums.values():
                each.finish()

        ports = []
        if self.owns:
            ports = [pltpu.SemaphoreType.DMA((units, 7)), pltpu.SemaphoreType.DMA((units, 7))]
            ports.append(pltpu.SemaphoreType.DMA((len(self.owns),)))
        buffers = []
        for whole in self.sums.values():
            for kind, share in ((F32, 1), (BF16, 1), (BF16, 1), (BF16, 32)):
                buffers += [pltpu.VMEM((rows // share, width), kind) for rows, width in SHAPES]
            buffers += [pltpu.SemaphoreType.DMA((3, LEVELS, 2)), pltpu.SemaphoreType.DMA((3, LEVELS, 2))]
            buffers.append(pltpu.SemaphoreType.DMA((3,)))
            if len(whole) > 2:
                buffers.append(pltpu.VMEM((LEVELS + 1, 8, 1024), F32))
                buffers.append(pltpu.VMEM((LEVELS, 8, 1024), F32))

        for shape in HELD.values():
            buffers += [pltpu.VMEM(shape, BF16), pltpu.SemaphoreType.DMA((1,))]

        out = pl.pallas_call(
            kernel,
            in_specs=[ANY] * len(self.owns) + [spec for _, spec in given],
            out_specs=[ANY] * len(results),
            scratch_shapes=[*ports, *buffers],
            out_shape=[jax.ShapeDtypeStruct(r.shape, r.dtype) for r in results],
            compiler_params=pltpu.CompilerParams(
                vmem_limit_bytes=VMEM_BYTES, collective_id=self.collective, has_side_effects=True
            ),
            name=self.name,
        )(*self.owns, *[array for array, _ in given])
        arrays = {id(result): array for result, array in zip(results, out)}
        return lambda later: arrays[id(later)]

    def run_stage(self, stage, ticks, act, of, sums, held):
        ins, outs = stage.ins, stage.outs
        piped = [at for at, (_, spec) in enumerate(ins) if spec is not ANY and spec is not SCALAR]
        fixed = {at: of[id(a)] for at, (a, _) in enumerate(ins) if at not in piped}

        def poll(slot):
            for (step, at), todo in ticks.items():
                if at == slot:

                    @pl.when(pl.program_id(0) == step)
                    def _(todo=todo):
                        for kind, unit in todo:
                            act(kind, unit)

        poll.sums = sums.get(stage.sums)
        poll.held = held

        def scoped(*scratch):
            if stage.prepare:
                stage.prepare([fixed.get(at) for at in range(len(ins))], scratch)

            def body(*blocks):
                in_refs = [fixed.get(at) for at in range(len(ins))]
                for at, ref in zip(piped, blocks):
                    in_refs[at] = ref
                stage.body(in_refs, list(blocks[len(piped) :]), scratch, poll)

            pltpu.emit_pipeline(
                body,
                grid=stage.grid,
                in_specs=[ins[at][1] for at in piped],
                out_specs=[spec for _, _, spec in outs],
            )(*[of[id(ins[at][0])] for at in piped], *[of[id(r)] for r in stage.results])

        pl.run_scoped(scoped, *stage.scratch)


def launch(
    body, name, grid, ins, outs, scratch, flops, moved, recorder=None, prepare=None, needs=(),
    slots=1, time=1.0, sums=None, held=(),
):
    if recorder is not None:
        return recorder.add(
            body=body, grid=grid, ins=ins, outs=outs, scratch=scratch, prepare=prepare, needs=needs,
            slots=slots, time=time, sums=sums, held=dict(held),
        )

    def kernel(*refs):
        in_refs, out_refs = list(refs[: len(ins)]), list(refs[len(ins) : len(ins) + len(outs)])
        rest = refs[len(ins) + len(outs) :]
        if prepare:

            @pl.when(pl.program_id(0) == 0)
            def _():
                prepare(in_refs, rest)

        body(in_refs, out_refs, rest, lambda slot: None)

    return pl.pallas_call(
        kernel,
        grid=grid,
        in_specs=[spec for _, spec in ins],
        out_specs=[spec for _, _, spec in outs],
        scratch_shapes=scratch,
        out_shape=[jax.ShapeDtypeStruct(s, d) for s, d, _ in outs],
        compiler_params=pltpu.CompilerParams(vmem_limit_bytes=VMEM_BYTES),
        cost_estimate=pl.CostEstimate(flops=flops, bytes_accessed=moved, transcendentals=0),
        name=name,
    )(*[a for a, _ in ins])


class Ready:
    def __init__(self, whole):
        self.whole = whole

    def wait(self, chunk):
        pass

    def wait_all(self):
        pass


def staged_call(body, name, grid, limit, mats, ins, outs, scratch=(), flops=0, part=None, slots_of=(), **record):
    held = dict(zip(slots_of, (mat for mat, _ in mats))) if record else {}
    own = mats[len(held) :]
    holders = []
    for mat, chunks in own:
        rows, width = mat.shape
        holders.append(pltpu.VMEM((rows, width if part is None else width // 3), mat.dtype))
        holders.append(pltpu.SemaphoreType.DMA((chunks,)))
    given = [mat for mat, _ in own]

    def fetches(in_refs, rest):
        return [
            Fetch(
                in_refs[1 + at], rest[2 * at], rest[2 * at + 1], chunks,
                0 if part is None else part * mat.shape[1] // 3,
            )
            for at, (mat, chunks) in enumerate(own)
        ]

    def prepare(in_refs, rest):
        for fetch in fetches(in_refs, rest):
            fetch.start()

    def staged(in_refs, out_refs, rest, poll):
        ready = [Ready(poll.held[slot][0]) for slot in held]
        args = (in_refs[0], ready + fetches(in_refs, rest), in_refs[1 + len(given) :], out_refs)
        body(*args, rest[2 * len(own) :], poll)

    moved = sum(a.size * a.dtype.itemsize for a in given)
    moved += sum(a.size * a.dtype.itemsize for a, _ in ins)
    moved += sum(math.prod(s) * jnp.dtype(d).itemsize for s, d, _ in outs)
    if record:
        record = dict(record, needs=[(mat, part) for mat in given], held=held)
    return launch(
        staged,
        name,
        grid,
        [(limit, SCALAR)] + [(mat, ANY) for mat in given] + list(ins),
        outs,
        [*holders, *scratch],
        flops,
        moved,
        prepare=prepare,
        **record,
    )


def project(name, limit, rows_in, mat, chunks, part=None, **record):
    total, depth = rows_in.shape
    width = mat.shape[1] if part is None else mat.shape[1] // 3
    block = min(256, total)
    step = width // chunks

    def body(limit, fetches, ins, outs, extra, poll):
        (fetch,) = fetches
        left = ins[0][...]
        for chunk in range(chunks):
            poll(chunk)
            fetch.wait(chunk)
            columns = slice(chunk * step, (chunk + 1) * step)
            outs[0][:, columns] = nn(left, fetch.whole[:, columns]).astype(BF16)

    return staged_call(
        body,
        name,
        (total // block,),
        limit,
        [(mat, chunks)],
        [(rows_in, rows_spec(block, depth))],
        [((total, width), BF16, rows_spec(block, width))],
        flops=2 * total * depth * width,
        part=part,
        **record,
    )[0]


def attend(name, limit, queries, keys, values, causal, **record):
    q_len, k_len = queries[0].shape[0], keys[0].shape[0]
    pairs = 1024 // PAIR
    step = min(512, q_len)

    def body(ins, outs, extra, poll):
        poll(0)
        limit_ref, q_ref, k_ref, v_ref = ins
        e_ref, o_ref, inv_ref = outs
        lanes = lax.broadcasted_iota(jnp.int32, (1, PAIR), 1)
        places = lax.broadcasted_iota(jnp.int32, (k_len, 1), 0)
        bias = jnp.where(places < limit_ref[0], 0.0, -1000000000.0)
        q_two = q_ref[...].astype(F32) * (1.0 / math.sqrt(HEAD))
        k_two = k_ref[...].astype(F32)
        v_two = v_ref[...].astype(F32)
        q_own, k_own, v_own = [], [], []
        for half in range(2):
            own = (lanes >= HEAD * half) & (lanes < HEAD * (half + 1))
            spare = lanes == HEAD * (1 - half)
            q_own.append(jnp.where(own, q_two, jnp.where(spare, 1.0, 0.0)).astype(BF16))
            k_own.append(jnp.where(own, k_two, jnp.where(spare, bias, 0.0)).astype(BF16))
            v_own.append(jnp.where(own, v_two, jnp.where(spare, 1.0, 0.0)).T.astype(BF16))

        def score(half, start):
            scores = nt(k_own[half], q_own[half][start : start + step])
            if causal:
                shape = (k_len, step)
                key_at = lax.broadcasted_iota(jnp.int32, shape, 0)
                query_at = lax.broadcasted_iota(jnp.int32, shape, 1) + start
                scores = jnp.where(key_at <= query_at, scores, -1000000000.0)
            return scores

        blocks = [(half, start) for half in range(2) for start in range(0, q_len, step)]
        parts = [[], []]
        scores = score(*blocks[0])
        for at, (half, start) in enumerate(blocks):
            later = score(*blocks[at + 1]) if at + 1 < len(blocks) else None
            highest = jnp.max(scores, axis=0, keepdims=True)
            weights = jnp.exp(scores - highest).astype(BF16)
            e_ref[0, :, half * q_len + start : half * q_len + start + step] = weights
            parts[half].append(nn(v_own[half], weights))
            scores = later
        mixed = []
        for half in range(2):
            out = jnp.concatenate(parts[half], axis=1) if len(parts[half]) > 1 else parts[half][0]
            at = HEAD * (1 - half)
            inverse = 1.0 / out[at : at + 1]
            own_rows = out[HEAD * half : HEAD * (half + 1)]
            mixed.append((own_rows * inverse, jnp.broadcast_to(inverse, own_rows.shape)))
        o_ref[...] = jnp.concatenate([mixed[0][0], mixed[1][0]], axis=0).T.astype(BF16)
        inv_ref[...] = jnp.concatenate([mixed[0][1], mixed[1][1]], axis=0).T

    def columns(rows, first):
        return pl.BlockSpec((rows, PAIR), lambda i: (0, first + i))

    return launch(
        body,
        name,
        (pairs,),
        [
            (limit, SCALAR),
            (queries[0], columns(q_len, queries[1])),
            (keys[0], columns(k_len, keys[1])),
            (values[0], columns(k_len, values[1])),
        ],
        [
            (
                (pairs, k_len, 2 * q_len),
                BF16,
                pl.BlockSpec((1, k_len, 2 * q_len), lambda i: (i, 0, 0)),
            ),
            ((q_len, 1024), BF16, columns(q_len, 0)),
            ((q_len, 1024), F32, columns(q_len, 0)),
        ],
        [],
        16 * pairs * q_len * k_len * PAIR,
        4 * pairs * q_len * k_len,
        **record,
    )


def attend_grad(name, queries, keys, values, weights, mixture, inverse, upstream, **record):
    q_len, k_len = queries[0].shape[0], keys[0].shape[0]
    pairs = 1024 // PAIR
    step = min(256, q_len)
    factor = 1.0 / math.sqrt(HEAD)

    def body(ins, outs, extra, poll):
        q_ref, k_ref, v_ref, e_ref, o_ref, inv_ref, do_ref = ins
        dq_ref, dk_ref, dv_ref = outs
        (ds_ref,) = extra
        poll(0)
        lanes = lax.broadcasted_iota(jnp.int32, (1, PAIR), 1)
        first = lanes < HEAD
        scaled = do_ref[...].astype(F32) * inv_ref[...]
        inner = scaled.astype(BF16).astype(F32) * o_ref[...].astype(F32)
        coarse = inner.astype(BF16)
        fine = (inner - coarse.astype(F32)).astype(BF16)
        picks = lax.broadcasted_iota(jnp.int32, (8, PAIR), 1)
        ones = [
            jnp.where(picks < HEAD, 1.0, 0.0).astype(BF16),
            jnp.where(picks < HEAD, 0.0, 1.0).astype(BF16),
        ]
        delta = [(nt(one, coarse) + nt(one, fine))[0:1] for one in ones]
        do_two = jnp.concatenate(
            [jnp.where(first, scaled, 0.0).astype(BF16), jnp.where(first, 0.0, scaled).astype(BF16)],
            axis=0,
        )
        q_all = q_ref[...].astype(F32) * factor
        q_two = jnp.concatenate(
            [jnp.where(first, q_all, 0.0).astype(BF16), jnp.where(first, 0.0, q_all).astype(BF16)],
            axis=0,
        )
        k_flip = k_ref[...].astype(F32).T.astype(BF16)
        v_all = v_ref[...]
        for half in range(2):
            for start in range(0, q_len, step):
                at = half * q_len + start
                probs_grad = nt(v_all, do_two[at : at + step])
                held = e_ref[0, :, at : at + step].astype(F32)
                ds_ref[:, at : at + step] = (
                    held * (probs_grad - delta[half][:, start : start + step])
                ).astype(BF16)
        dv_ref[...] = nn(e_ref[0], do_two).astype(BF16)
        dk_ref[...] = nn(ds_ref[...], q_two).astype(BF16)
        turned = nn(k_flip, ds_ref[...]) * factor
        rows = lax.broadcasted_iota(jnp.int32, (PAIR, 1), 0)
        dq_ref[...] = jnp.where(rows < HEAD, turned[:, :q_len], turned[:, q_len:]).T.astype(BF16)

    def columns(rows, at):
        return pl.BlockSpec((rows, PAIR), lambda i: (0, at + i))

    return launch(
        body,
        name,
        (pairs,),
        [
            (queries[0], columns(q_len, queries[1])),
            (keys[0], columns(k_len, keys[1])),
            (values[0], columns(k_len, values[1])),
            (weights, pl.BlockSpec((1, k_len, 2 * q_len), lambda i: (i, 0, 0))),
            (mixture, columns(q_len, 0)),
            (inverse, columns(q_len, 0)),
            (upstream, columns(q_len, 0)),
        ],
        [
            ((q_len, 1024), BF16, columns(q_len, 0)),
            ((k_len, 1024), BF16, columns(k_len, 0)),
            ((k_len, 1024), BF16, columns(k_len, 0)),
        ],
        [pltpu.VMEM((k_len, 2 * q_len), BF16)],
        32 * pairs * q_len * k_len * PAIR,
        4 * pairs * q_len * k_len,
        **record,
    )


def row_mask(limit, block):
    at = lax.broadcasted_iota(jnp.int32, (block, 1), 0) + pl.program_id(0) * block
    return (at < limit).astype(F32)


def add_squares(ref, row, entries, mask):
    sums = jnp.sum(entries * entries * mask, axis=0, keepdims=True)
    first = pl.program_id(0) == 0

    @pl.when(first)
    def _():
        ref[row : row + 1, :] = sums

    @pl.when(jnp.logical_not(first))
    def _():
        ref[row : row + 1, :] += sums


def spread_lanes(column):
    return jnp.broadcast_to(column, (column.shape[0], 128))


def out_norm(name, limit, mixture, residual, gain, mat, next_mat=None, residual_gain=None, **record):
    total, width = mixture.shape
    block = min(256, total)
    mats = [(mat, 1)] + ([] if next_mat is None else [(next_mat, 1)])

    def body(limit, fetches, ins, outs, extra, poll):
        poll(0)
        o_ref, r_ref, g_ref, rg_ref = ins
        fetches[0].wait_all()
        added = nn(o_ref[...], fetches[0].whole[...])
        base = r_ref[...].astype(F32)
        if residual_gain is not None:
            base = base * rg_ref[...]
        unit, inverse = standardize(base + added)
        outs[0][...] = unit.astype(BF16)
        outs[1][...] = spread_lanes(inverse)
        add_squares(outs[2], 0, added, row_mask(limit[0], block))
        if next_mat is not None:
            fetches[1].wait_all()
            hidden = (unit * g_ref[...]).astype(BF16)
            outs[3][...] = nn(hidden, fetches[1].whole[...]).astype(BF16)

    outs = [
        ((total, width), BF16, rows_spec(block, width)),
        ((total, 128), F32, rows_spec(block, 128)),
        ((8, width), F32, whole_spec((8, width))),
    ]
    if next_mat is not None:
        outs.append(((total, width), BF16, rows_spec(block, width)))
    return staged_call(
        body,
        name,
        (total // block,),
        limit,
        mats,
        [
            (mixture, rows_spec(block, width)),
            (residual, rows_spec(block, width)),
            (gain, whole_spec((1, width))),
            (gain if residual_gain is None else residual_gain, whole_spec((1, width))),
        ],
        outs,
        flops=2 * total * width * width * len(mats),
        **record,
    )


def branch(name, limit, unit, gain, gain_out, w_in, w_back, down_low, up_low, **record):
    total, width = unit.shape
    hidden_units = w_in.shape[1]
    adapter = down_low.shape[1]
    block = min(256, total)
    chunks = 4
    step = hidden_units // chunks

    def body(limit, fetches, ins, outs, extra, poll):
        u_ref, g_ref, go_ref, ad_ref, au_ref = ins
        y_ref, unit_ref, inv_ref, slope_ref, wa_ref, ad_slope_ref, sq_ref = outs
        (act,) = extra
        first, second = fetches
        hidden = u_ref[...].astype(F32) * g_ref[...]
        low = hidden.astype(BF16)
        pre = nn(low, ad_ref[...].astype(BF16))
        gate = jax.nn.sigmoid(pre)
        wa = (pre * gate).astype(BF16)
        wa_ref[...] = wa
        ad_slope_ref[...] = (gate * (1.0 + pre * (1.0 - gate))).astype(BF16)
        adapted = 4.0 * nn(wa, au_ref[...].astype(BF16))
        for chunk in range(chunks):
            if chunk % 2 == 0:
                poll(chunk // 2)
            first.wait(chunk)
            columns = slice(chunk * step, (chunk + 1) * step)
            fp = nn(low, first.whole[:, columns])
            cdf = 0.5 * (1.0 + lax.erf(fp * (1.0 / math.sqrt(2.0))))
            act[:, columns] = (fp * cdf).astype(BF16)
            bell = jnp.exp(-0.5 * fp * fp) * (1.0 / math.sqrt(2.0 * math.pi))
            slope_ref[:, columns] = (cdf + fp * bell).astype(BF16)
        second.wait_all()
        added = nn(act[...], second.whole[...]) + adapted
        out_unit, inverse = standardize(hidden + added)
        result = out_unit * go_ref[...]
        y_ref[...] = result.astype(BF16)
        unit_ref[...] = out_unit.astype(BF16)
        inv_ref[...] = spread_lanes(inverse)
        mask = row_mask(limit[0], block)
        add_squares(sq_ref, 0, added, mask)
        add_squares(sq_ref, 1, result, mask)

    return staged_call(
        body,
        name,
        (total // block,),
        limit,
        [(w_in, chunks), (w_back, 1)],
        [
            (unit, rows_spec(block, width)),
            (gain, whole_spec((1, width))),
            (gain_out, whole_spec((1, width))),
            (down_low, whole_spec(down_low.shape)),
            (up_low, whole_spec(up_low.shape)),
        ],
        [
            ((total, width), BF16, rows_spec(block, width)),
            ((total, width), BF16, rows_spec(block, width)),
            ((total, 128), F32, rows_spec(block, 128)),
            ((total, hidden_units), BF16, rows_spec(block, hidden_units)),
            ((total, adapter), BF16, rows_spec(block, adapter)),
            ((total, adapter), BF16, rows_spec(block, adapter)),
            ((8, width), F32, whole_spec((8, width))),
        ],
        scratch=[pltpu.VMEM((block, hidden_units), BF16)],
        flops=4 * total * width * (hidden_units + adapter),
        slots_of=("within", "back"),
        **record,
    )


def adapter_grad(upstream, refs):
    (uo_ref, io_ref, go_ref, ui_ref, gi_ref, wa_ref, as_ref, ad_ref, au_ref) = refs
    grad_two = standardize_grad(uo_ref[...].astype(F32), io_ref[:, 0:1], upstream * go_ref[...])
    dvd = (4.0 * grad_two).astype(BF16)
    low = (ui_ref[...].astype(F32) * gi_ref[...]).astype(BF16)
    du = (nt(dvd, au_ref[...].astype(BF16)) * as_ref[...].astype(F32)).astype(BF16)
    total = grad_two + nt(du, ad_ref[...].astype(BF16))
    return grad_two.astype(BF16), total, tn(low, du), tn(wa_ref[...], dvd)


def hidden_grad(dz, total, fetches, refs, dfp, chunks, poll=lambda slot: None):
    slope_ref, ui_ref, ii_ref, gi_ref = refs
    back, within, last = fetches
    step = dfp.shape[1] // chunks
    back.wait_all()
    poll(0)
    for chunk in range(chunks):
        columns = slice(chunk * step, (chunk + 1) * step)
        act_grad = nt(dz, back.whole[columns, :])
        dfp[:, columns] = (act_grad * slope_ref[:, columns].astype(F32)).astype(BF16)
    within.wait_all()
    poll(1)
    total = total + nt(dfp[...], within.whole[...])
    grad_one = standardize_grad(ui_ref[...].astype(F32), ii_ref[:, 0:1], total * gi_ref[...])
    last.wait_all()
    return grad_one, nt(grad_one.astype(BF16), last.whole[...]).astype(BF16)


def dec_branch_grad(
    name, limits, cot, saved_out, gain_out, saved_in, gain_in, slope, wa, ad_slope,
    w_back, w_in, w_out, down_low, up_low, squares, **record,
):
    total, width = cot.shape
    hidden_units = w_in.shape[1]
    adapter = down_low.shape[1]
    whole = [
        cot, saved_out[0], saved_out[1], gain_out, saved_in[0], gain_in, wa, ad_slope, down_low,
        up_low, slope, saved_in[1], *squares,
    ]

    def body(limit, fetches, ins, outs, extra, poll):
        grad_ref, mix_ref = outs[:2]
        if record:
            (down_ref, up_ref), tally_ref = poll.sums.totals, poll.sums.tallies[0].at[0]
        else:
            down_ref, up_ref, tally_ref = outs[2], outs[3].at[:adapter], outs[3].at[adapter:]
        (other,), cot_ref, slope_ref, ii_ref = ins[:1], ins[1], ins[11], ins[12]
        dz, part, down_ref[...], up_ref[...] = adapter_grad(cot_ref[...].astype(F32), ins[2:11])
        sums = [ref[row : row + 1, :] for ref, rows in zip(ins[13:], (1, 2, 1, 1, 2)) for row in range(rows)]
        lanes = lax.broadcasted_iota(jnp.int32, (1, width), 1)
        counts = jnp.where(lanes == 0, limit[0], jnp.where(lanes == 1, other[0], 0)).astype(F32)
        tally_ref[...] = jnp.concatenate([*sums, counts], axis=0)
        grad_ref[...], mix_ref[...] = hidden_grad(
            dz, part, fetches, (slope_ref, ins[5], ii_ref, ins[6]), extra[0], 4
        )

    return staged_call(
        body,
        name,
        (1,),
        limits[0],
        [(w_back, 1), (w_in, 1), (w_out, 1)],
        [(limits[1], SCALAR)] + [(a, whole_spec(a.shape)) for a in whole],
        [
            (cot.shape, F32, whole_spec(cot.shape)),
            (cot.shape, BF16, whole_spec(cot.shape)),
        ]
        + [
            (shape, F32, whole_spec(shape))
            for shape in (() if record else (down_low.shape, (adapter + 8, width)))
        ],
        scratch=[pltpu.VMEM((total, hidden_units), BF16)],
        flops=4 * total * width * (hidden_units + 2 * adapter),
        slots_of=("back", "within"),
        **record,
    )


def enc_adapter_grad(
    name, limit, cot, cross, cross_mat, saved_out, gain_out, saved_in, gain_in, wa, ad_slope,
    down_low, up_low, **record,
):
    total, width = cot.shape
    adapter = down_low.shape[1]
    block = min(256, total)
    rows = rows_spec(block, width)

    def body(limit, fetches, ins, outs, extra, poll):
        poll(0)
        dz_ref, part_ref = outs[:2]
        down_sum, up_sum = poll.sums.totals if record else extra
        fetches[0].wait_all()
        upstream = ins[0][...].astype(F32)
        for at in range(2):
            upstream = upstream + nt(ins[1 + at][...], fetches[0].whole[:, at * width : (at + 1) * width])
        dz_ref[...], part_ref[...], down_part, up_part = adapter_grad(upstream, ins[3:])
        at = pl.program_id(0)

        @pl.when(at == 0)
        def _():
            up_sum[...] = up_part
            down_sum[...] = down_part

        @pl.when(at > 0)
        def _():
            up_sum[...] += up_part
            down_sum[...] += down_part

        if not record:

            @pl.when(at == total // block - 1)
            def _():
                outs[2][...] = down_sum[...].astype(BF16)
                outs[3][...] = up_sum[...].astype(BF16)

    return staged_call(
        body,
        name,
        (total // block,),
        limit,
        [(cross_mat, 1)],
        [
            (cot, rows),
            (cross[0], rows),
            (cross[1], rows),
            (saved_out[0], rows),
            (saved_out[1], rows_spec(block, 128)),
            (gain_out, whole_spec((1, width))),
            (saved_in[0], rows),
            (gain_in, whole_spec((1, width))),
            (wa, rows_spec(block, adapter)),
            (ad_slope, rows_spec(block, adapter)),
            (down_low, whole_spec(down_low.shape)),
            (up_low, whole_spec(up_low.shape)),
        ],
        [
            ((total, width), BF16, rows),
            ((total, width), F32, rows),
        ]
        + [(a.shape, BF16, whole_spec(a.shape)) for a in (() if record else (down_low, up_low))],
        scratch=[pltpu.VMEM(a.shape, F32) for a in (() if record else (down_low, up_low))],
        flops=4 * total * width * (width + 2 * adapter),
        **record,
    )


def enc_hidden_grad(name, limit, dz, part, slope, saved_in, gain_in, w_back, w_in, w_out, **record):
    total, width = dz.shape
    hidden_units = w_in.shape[1]
    block = min(256, total)
    rows = rows_spec(block, width)

    def body(limit, fetches, ins, outs, extra, poll):
        outs[0][...], outs[1][...] = hidden_grad(
            ins[0][...], ins[1][...], fetches, ins[2:], extra[0], 4, poll
        )

    return staged_call(
        body,
        name,
        (total // block,),
        limit,
        [(w_back, 1), (w_in, 1), (w_out, 1)],
        [
            (dz, rows),
            (part, rows),
            (slope, rows_spec(block, hidden_units)),
            (saved_in[0], rows),
            (saved_in[1], rows_spec(block, 128)),
            (gain_in, whole_spec((1, width))),
        ],
        [((total, width), F32, rows), ((total, width), BF16, rows)],
        scratch=[pltpu.VMEM((block, hidden_units), BF16)],
        flops=4 * total * width * hidden_units,
        slots_of=("back", "within"),
        **record,
    )


def middle_grad(name, limit, grad_cross, dq, saved, gain, w_cq, w_so, **record):
    total, width = dq.shape
    block = min(256, total)
    unit, inv = saved

    def body(limit, fetches, ins, outs, extra, poll):
        poll(0)
        gc_ref, dq_ref, u_ref, i_ref, g_ref = ins
        fetches[0].wait_all()
        hidden_grad = gc_ref[...] + nt(dq_ref[...], fetches[0].whole[...])
        grad_self = standardize_grad(
            u_ref[...].astype(F32), i_ref[:, 0:1], hidden_grad * g_ref[...]
        )
        outs[0][...] = grad_self
        fetches[1].wait_all()
        outs[1][...] = nt(grad_self.astype(BF16), fetches[1].whole[...]).astype(BF16)

    return staged_call(
        body,
        name,
        (total // block,),
        limit,
        [(w_cq, 1), (w_so, 1)],
        [
            (grad_cross, rows_spec(block, width)),
            (dq, rows_spec(block, width)),
            (unit, rows_spec(block, width)),
            (inv, rows_spec(block, 128)),
            (gain, whole_spec((1, width))),
        ],
        [
            ((total, width), F32, rows_spec(block, width)),
            ((total, width), BF16, rows_spec(block, width)),
        ],
        flops=4 * total * width * width,
        **record,
    )


def input_grad(name, limit, base, parts, mat, narrow=(), tally=None):
    total, width = base.shape
    block = min(256, total)
    steps = total // block
    count = len(parts)

    def body(limit, fetches, ins, outs, extra, poll):
        (fetch,) = fetches
        result = ins[0][...]
        for at in range(count):
            fetch.wait(at)
            result = result + nt(ins[1 + at][...], fetch.whole[:, at * width : (at + 1) * width])
        outs[0][...] = result
        for at in range(len(narrow)):
            outs[1 + at][...] = ins[1 + count + at][...].astype(F32)
        if tally is not None:
            rows = ins[-1][...]
            at = lax.broadcasted_iota(jnp.int32, (8, 1), 0)
            numbers = jnp.where(at < 3, rows[7:8, 0:1], rows[7:8, 1:2])
            outs[-1][...] = spread_lanes(
                jnp.sqrt(jnp.sum(rows, axis=1, keepdims=True) / (numbers * width))
            )

    slices = [(a, rows_spec(a.shape[0] // steps, a.shape[1])) for a in narrow]
    tallies = [] if tally is None else [(tally, whole_spec(tally.shape))]
    return staged_call(
        body,
        name,
        (steps,),
        limit,
        [(mat, count)],
        [(base, rows_spec(block, width))] + [(p, rows_spec(block, width)) for p in parts] + slices + tallies,
        [((total, width), F32, rows_spec(block, width))]
        + [(a.shape, F32, spec) for a, spec in slices]
        + [((8, 128), F32, whole_spec((8, 128))) for _ in tallies],
        flops=2 * total * width * width * count,
    )


NAMES = (
    "enc_qkv",
    "enc_attn_out",
    "enc_ffn_in",
    "enc_ffn_out",
    "dec_self_qkv",
    "dec_self_out",
    "dec_cross_q",
    "dec_cross_kv",
    "dec_cross_out",
    "dec_ffn_in",
    "dec_ffn_out",
)


def layers(enc_limit, dec_limit, enc_input, dec_input, enc_cot, dec_cot, blocks, hosting, fsdp, gains, adapters):
    gain = [gains[k : k + 1] for k in range(5)]
    enc_down, enc_up, dec_down, dec_up = adapters
    if hosting:
        order = (0, 1, 4, 5, 6, 2, 3, 7, 8, 9, 10)
        recorder = Recorder("forward", 1, {NAMES[k]: blocks[NAMES[k]] for k in order}, fsdp)
        w = types.SimpleNamespace(**dict(zip(recorder.names, recorder.wholes)))
    else:
        recorder = None
        w = types.SimpleNamespace(
            **{name: lax.all_gather(b, "fsdp", axis=0, tiled=True) for name, b in blocks.items()}
        )

    def at(slots, time, sums=None):
        if not hosting:
            return {}
        return {"recorder": recorder, "slots": slots, "time": time, "sums": sums}

    enc_q, enc_k, enc_v = (
        project("enc_project", enc_limit, enc_input, w.enc_qkv, 1, part, **at(1, 5.0))
        for part in range(3)
    )
    e_enc, o_enc, inv_enc = attend(
        "enc_attend", enc_limit, (enc_q, 0), (enc_k, 0), (enc_v, 0), False, **at(1, 34.0)
    )
    unit1, dev1, sq_a = out_norm(
        "enc_out_norm", enc_limit, o_enc, enc_input, gain[0], w.enc_attn_out, **at(1, 9.0)
    )
    sqkv = project("dec_project", dec_limit, dec_input, w.dec_self_qkv, 3, **at(3, 6.0))
    e_self, o_self, inv_self = attend(
        "dec_attend", dec_limit, (sqkv, 0), (sqkv, 8), (sqkv, 16), True, **at(1, 8.5)
    )
    unit3, dev3, sq_c, cross_q = out_norm(
        "dec_out_norm", dec_limit, o_self, dec_input, gain[2], w.dec_self_out, w.dec_cross_q,
        **at(1, 5.3),
    )
    enc_out, unit2, dev2, slope_e, wa_e, ads_e, sq_b = branch(
        "enc_branch", enc_limit, unit1, gain[0], gain[1], w.enc_ffn_in, w.enc_ffn_out,
        enc_down, enc_up, **at(2, 33.0),
    )
    kv = project("cross_project", enc_limit, enc_out, w.dec_cross_kv, 2, **at(2, 9.5))
    e_cross, o_cross, inv_cross = attend(
        "cross_attend", enc_limit, (cross_q, 0), (kv, 0), (kv, 8), False, **at(1, 14.0)
    )
    if hosting:
        value = recorder.run()
        w = types.SimpleNamespace(**{name: value(mat) for name, mat in vars(w).items()})
        enc_q, enc_k, enc_v, e_enc, o_enc, inv_enc = map(value, (enc_q, enc_k, enc_v, e_enc, o_enc, inv_enc))
        unit1, dev1, sq_a = map(value, (unit1, dev1, sq_a))
        enc_out, unit2, dev2, slope_e, wa_e, ads_e, sq_b = map(
            value, (enc_out, unit2, dev2, slope_e, wa_e, ads_e, sq_b)
        )
        sqkv, e_self, o_self, inv_self = map(value, (sqkv, e_self, o_self, inv_self))
        unit3, dev3, sq_c, cross_q = map(value, (unit3, dev3, sq_c, cross_q))
        kv, e_cross, o_cross, inv_cross = map(value, (kv, e_cross, o_cross, inv_cross))
        recorder = Recorder("encoder_grad", 2, {}, fsdp)
    unit4, dev4, sq_d = out_norm(
        "cross_out_norm", dec_limit, o_cross, unit3, gain[3], w.dec_cross_out, residual_gain=gain[2]
    )
    dec_out, unit5, dev5, slope_d, wa_d, ads_d, sq_e = branch(
        "dec_branch", dec_limit, unit4, gain[3], gain[4], w.dec_ffn_in, w.dec_ffn_out,
        dec_down, dec_up,
    )
    grad_cross, do_cross, *dec_grads = dec_branch_grad(
        "dec_branch_grad", (enc_limit, dec_limit), dec_cot, (unit5, dev5), gain[4], (unit4, dev4), gain[3],
        slope_d, wa_d, ads_d, w.dec_ffn_out, w.dec_ffn_in, w.dec_cross_out, dec_down, dec_up,
        (sq_a, sq_b, sq_c, sq_d, sq_e),
    )
    dcq, dck, dcv = attend_grad(
        "cross_attend_grad", (cross_q, 0), (kv, 0), (kv, 8), e_cross, o_cross, inv_cross, do_cross
    )
    if hosting:
        dec_sums = recorder.reduce("dec", True)
        recorder.load("dec", dec_grads)
        enc_sums = recorder.reduce("enc", False)
    dz, part, *enc_grads = enc_adapter_grad(
        "enc_adapter_grad", enc_limit, enc_cot, (dck, dcv), w.dec_cross_kv, (unit2, dev2), gain[1],
        (unit1, dev1), gain[0], wa_e, ads_e, enc_down, enc_up, **at(1, 20.0, "enc"),
    )
    grad_one, do_enc = enc_hidden_grad(
        "enc_hidden_grad", enc_limit, dz, part, slope_e, (unit1, dev1), gain[0],
        w.enc_ffn_out, w.enc_ffn_in, w.enc_attn_out, **at(2, 28.0),
    )
    deq, dek, dev = attend_grad(
        "enc_attend_grad", (enc_q, 0), (enc_k, 0), (enc_v, 0), e_enc, o_enc, inv_enc, do_enc, **at(1, 37.0)
    )
    if hosting:
        value = recorder.run()
        grad_one, deq, dek, dev = map(value, (grad_one, deq, dek, dev))
        *dec_grads, tally = map(value, dec_sums)
        enc_grads = [value(a) for a in enc_sums]
    else:
        everyone = ("fsdp", "dp")
        down, up = lax.psum(dec_grads, everyone)
        dec_grads, tally = [down, up[: dec_up.shape[0]]], up[dec_up.shape[0] :]
        enc_grads = lax.psum(enc_grads, everyone)
    grad_self, do_self = middle_grad(
        "dec_middle_grad", dec_limit, grad_cross, dcq, (unit3, dev3), gain[2], w.dec_cross_q,
        w.dec_self_out,
    )
    dsq, dsk, dsv = attend_grad(
        "dec_attend_grad", (sqkv, 0), (sqkv, 8), (sqkv, 16), e_self, o_self, inv_self, do_self
    )
    dec_grad, *dec_grads = input_grad(
        "dec_input_grad", dec_limit, grad_self, [dsq, dsk, dsv], w.dec_self_qkv, dec_grads
    )
    enc_grad, *enc_grads, rms = input_grad(
        "enc_input_grad", enc_limit, grad_one, [deq, dek, dev], w.enc_qkv, enc_grads, tally
    )
    return enc_out, dec_out, enc_grad, dec_grad, *enc_grads, *dec_grads, rms[:7, 0]


def shards(fsdp, dp, enc_input, dec_input, enc_cot, dec_cot, *rest):
    mats, (gains, enc_down, enc_up, dec_down, dec_up, enc_lengths, dec_lengths) = rest[:11], rest[11:]
    return layers(
        enc_lengths, dec_lengths, enc_input, dec_input, enc_cot, dec_cot, dict(zip(NAMES, mats)),
        fsdp == 8 and dp == 4, fsdp, gains, (enc_down, enc_up, dec_down, dec_up),
    )


def solution(mesh):
    by_rows = P(("fsdp", "dp"), None)
    placed = (by_rows,) * 4 + (P("fsdp", None),) * 11 + (P(),) * 5 + (P(("fsdp", "dp")),) * 2
    return jax.shard_map(
        functools.partial(shards, mesh.shape["fsdp"], mesh.shape["dp"]),
        mesh=mesh,
        in_specs=placed,
        out_specs=(by_rows,) * 4 + (P(),) * 5,
        check_vma=False,
    )
```
